32 devices in a mesh: pipe: 4 (over y, x), tensor: 4 (over z), dp: 2 (over core).
Axes of the slice: x: 2, y: 2, z: 4, core: 2. Of those that a mesh axis runs over, the one named last changes fastest.
Arguments:
- weight_main: bfloat16 [4, 4096, 2, 1024], P('pipe', None, None, 'tensor'), may hold values from -0.09375 to 0.09375
- weight_state: bfloat16 [4, 4096, 2, 128], P('pipe', None, None, 'tensor'), may hold values from -0.09375 to 0.09375
- weight_step: bfloat16 [4, 16, 4096], P('pipe', 'tensor'), may hold values from -0.09375 to 0.09375
- weight_out: bfloat16 [4, 1024, 4096], P('pipe', 'tensor'), may hold values from -0.1875 to 0.1875
- conv_main: float32 [4, 4, 1024], P('pipe', None, 'tensor'), may hold values from -3 to 3
- conv_state: float32 [4, 4, 2, 128], P('pipe'), may hold values from -3 to 3
- step_bias: float32 [4, 16], P('pipe', 'tensor'), may hold values from -3 to 0
- decay_log: float32 [4, 16], P('pipe', 'tensor'), may hold values from -5 to 0.5
- skip_gain: float32 [4, 16], P('pipe', 'tensor'), may hold values from 1 to 6
- norm_gain: float32 [4, 1024], P('pipe', 'tensor'), may hold values from 0.5 to 1.5
- saved_main: bfloat16 [4, 256, 2, 1024], P('pipe', 'dp', None, 'tensor'), parts along dimension 1, may hold values from -6 to 6
- saved_state: bfloat16 [4, 256, 2, 128], P('pipe', 'dp'), parts along dimension 1, may hold values from -6 to 6
- saved_step: bfloat16 [4, 16, 256], P('pipe', 'tensor', 'dp'), parts along dimension 2, may hold values from -6 to 6
- output_grad: bfloat16 [256, 4096], P('dp', 'tensor'), parts along dimension 0, may hold values from -6 to 6
Outputs:
- input_grads: bfloat16 [4, 256, 4096], P('pipe', 'dp', 'tensor'), parts along dimension 1
The draws below stay inside these ranges and needn't reach their ends.
There are 2 independent parts, one for each index of `dp`. The reference program is written for one: setup_inputs(seed, part) draws one part's arguments, and reference() takes and returns one part's arrays. A program takes and returns all parts, laid end to end along the dimension named above; an argument that names none is the same for every part. Nothing has to cross between parts.
All inputs are finite; a program needn't handle non-finite values.
Results may differ from the reference program's by a relative error of at most 0.02.
Values may be sent and summed in bfloat16 or wider, within the bound.
No kernel may reach another device: no remote copies, remote signals or barrier semaphores. Data moves between devices by JAX's collectives and lax.ppermute only.
A program may use at most 64 MiB of HBM per device.

```python
import jax
import jax.numpy as jnp
from jax import lax

D = 4096
HEADS_DEV = 4
HEAD_DIM = 64
NSTATE = 128
GROUP_SPAN = 4
KCONV = 4
STRETCH = 128
SEQLEN = 128
HEADS = 16
GROUPS = 1
N_PIPE = 4


def level_of(stream_key, shape, pieces, smallest, top_value):
    def one(dim, shards_of):
        draws = jax.random.uniform(jax.random.fold_in(jax.random.fold_in(stream_key, 6), dim), (shards_of,), jnp.float32, smallest / len(pieces), top_value / len(pieces))
        return jnp.repeat(jnp.exp(draws), shape[dim] // shards_of).reshape((-1,) + (1,) * (len(shape) - dim - 1))

    factor_of = one(*pieces[0])
    for cut in pieces[1:]:
        factor_of = factor_of * one(*cut)
    return factor_of


def gaussian(own_key, shape, width, limit, shards=(), held_as=jnp.bfloat16):
    entries = jax.random.normal(own_key, shape, jnp.float32) * width
    if len(shards) > 0:
        entries = level_of(own_key, shape, shards, -0.22, 0.18) * entries
    return jnp.clip(entries, min=-limit, max=limit).astype(held_as)


def setup_inputs(seed: int = 0, part: int = 0) -> dict:
    keys = jax.random.split(jax.random.key(seed), 15)
    part_keys = jax.random.split(jax.random.fold_in(keys[14], part), 15)
    weight_main = gaussian(keys[0], (N_PIPE, D, 2, HEADS * HEAD_DIM), D ** -0.5, 0.09375, ((0, 4), (3, 4)))
    weight_state = gaussian(keys[1], (N_PIPE, D, 2, GROUPS * NSTATE), D ** -0.5, 0.09375, ((0, 4), (3, 4)))
    weight_step = gaussian(keys[2], (N_PIPE, HEADS, D), D ** -0.5, 0.09375, ((0, 4), (1, 4)))
    weight_out = gaussian(keys[3], (N_PIPE, HEADS * HEAD_DIM, D), (HEADS * HEAD_DIM) ** -0.5, 0.1875, ((0, 4), (1, 4)))
    conv_main = gaussian(keys[4], (N_PIPE, KCONV, HEADS * HEAD_DIM), KCONV ** -0.5, 3.0, ((0, 4), (2, 4)), jnp.float32)
    conv_state = gaussian(keys[5], (N_PIPE, KCONV, 2, GROUPS * NSTATE), KCONV ** -0.5, 3.0, ((0, 4),), jnp.float32)
    step_bias = jnp.clip(-3.0 + 3.0 * jax.random.uniform(keys[6], (N_PIPE, HEADS), jnp.float32) ** level_of(keys[6], (N_PIPE, HEADS), ((0, 4), (1, 4)), -0.2, 0.2), -3.0, 0.0)
    decay_log = jnp.clip(-5.0 + 5.5 * jax.random.uniform(keys[7], (N_PIPE, HEADS), jnp.float32) ** level_of(keys[7], (N_PIPE, HEADS), ((0, 4), (1, 4)), -0.2, 0.2), -5.0, 0.5)
    skip_gain = jnp.clip(1.0 + 5.0 * jax.random.uniform(keys[8], (N_PIPE, HEADS), jnp.float32) ** level_of(keys[8], (N_PIPE, HEADS), ((0, 4), (1, 4)), -0.2, 0.2), 1.0, 6.0)
    norm_gain = jnp.clip(0.5 + 1.0 * jax.random.uniform(keys[9], (N_PIPE, HEADS * HEAD_DIM), jnp.float32) ** level_of(keys[9], (N_PIPE, HEADS * HEAD_DIM), ((0, 4), (1, 4)), -0.2, 0.2), 0.5, 1.5)
    saved_main = gaussian(part_keys[10], (N_PIPE, SEQLEN, 2, HEADS * HEAD_DIM), 1.0, 6.0, ((0, 4), (3, 4)))
    saved_state = gaussian(part_keys[11], (N_PIPE, SEQLEN, 2, GROUPS * NSTATE), 1.0, 6.0, ((0, 4),))
    saved_step = gaussian(part_keys[12], (N_PIPE, HEADS, SEQLEN), 1.0, 6.0, ((0, 4), (1, 4)))
    output_grad = gaussian(part_keys[13], (SEQLEN, D), 1.0, 6.0, ((1, 4),))
    return {"weight_main": weight_main, "weight_state": weight_state, "weight_step": weight_step, "weight_out": weight_out, "conv_main": conv_main, "conv_state": conv_state, "step_bias": step_bias, "decay_log": decay_log, "skip_gain": skip_gain, "norm_gain": norm_gain, "saved_main": saved_main, "saved_state": saved_state, "saved_step": saved_step, "output_grad": output_grad}


EPSILON = 1e-05
HIGHEST = lax.Precision.HIGHEST

def causal_conv(signal, kernel):
    taps = kernel.shape[0]
    length = signal.shape[0]
    padded = jnp.pad(signal, ((taps - 1, 0), (0, 0)))
    summed = kernel[0] * padded[0:length]
    for offset in range(1, taps):
        summed = summed + kernel[offset] * padded[offset:offset + length]
    return summed

def state_space(values, step_sizes, decay_rates, inputs, readout):
    length, head_count, head_size = values.shape
    blocks = length // STRETCH
    state_width = inputs.shape[1]
    decays = (step_sizes * decay_rates[:, None]).reshape(head_count, blocks, STRETCH)
    running = jnp.cumsum(decays, axis=2)
    scaled = (values * step_sizes.T[:, :, None]).reshape(blocks, STRETCH, head_count, head_size)
    inputs_blocked = inputs.reshape(blocks, STRETCH, state_width)
    readout_blocked = readout.reshape(blocks, STRETCH, state_width)
    scores = jnp.einsum('cin,cjn->cij', readout_blocked, inputs_blocked, precision=HIGHEST)
    position = jnp.arange(STRETCH)
    causal = position[:, None] >= position[None, :]
    differ = running[:, :, :, None] - running[:, :, None, :]
    weights = jnp.where(causal, jnp.exp(jnp.where(causal, differ, 0.0)), 0.0) * scores[None]
    within = jnp.einsum('hcij,cjhp->cihp', weights, scaled, precision=HIGHEST)
    tail_decay = jnp.exp(running[:, :, -1:] - running)
    weighted = scaled * jnp.transpose(tail_decay, (1, 2, 0))[:, :, :, None]
    block_sums = jnp.einsum('cjhp,cjn->chpn', weighted, inputs_blocked, precision=HIGHEST)
    shrinks = jnp.exp(running[:, :, -1]).T

    def advance(carried, item):
        newest, shrink = item
        return (carried * shrink[:, None, None] + newest, carried)
    anchor = jnp.zeros((head_count, head_size, state_width), jnp.float32)
    _, entering = lax.scan(advance, anchor, (block_sums, shrinks))
    across = jnp.einsum('cin,chpn->cihp', readout_blocked, entering, precision=HIGHEST)
    across = across * jnp.transpose(jnp.exp(running), (1, 2, 0))[:, :, :, None]
    return (within + across).reshape(length, head_count, head_size)

def mamba_mixer(main_proj, state_proj, step_proj, conv_main, conv_state, step_bias, decay_log, skip_gain, norm_gain):
    length = main_proj.shape[0]
    head_count = step_proj.shape[0]
    gating = main_proj[:, 0]
    mixed_in = jax.nn.silu(causal_conv(main_proj[:, 1], conv_main))
    flat_state = state_proj.reshape(length, -1)
    state_conv = jax.nn.silu(causal_conv(flat_state, conv_state.reshape(conv_state.shape[0], -1))).reshape(length, 2, -1)
    step_sizes = jax.nn.softplus(step_proj + step_bias[:, None])
    decay_rates = -jnp.exp(decay_log)
    values = mixed_in.reshape(length, head_count, -1)
    scanned = state_space(values, step_sizes, decay_rates, state_conv[:, 0], state_conv[:, 1])
    scanned = scanned + skip_gain[None, :, None] * values
    gated = scanned.reshape(length, -1) * jax.nn.silu(gating)
    inverse = lax.rsqrt(lax.optimization_barrier(jnp.mean(gated * gated, axis=1, keepdims=True)) + EPSILON)
    return gated * inverse * norm_gain

def reference(weight_main, weight_state, weight_step, weight_out, conv_main, conv_state, step_bias, decay_log, skip_gain, norm_gain, saved_main, saved_state, saved_step, output_grad):
    group_width = HEADS_DEV * HEAD_DIM
    quarter = NSTATE // GROUP_SPAN
    carry = output_grad
    results = []
    for section in range(N_PIPE - 1, -1, -1):

        def group_term(summed, group):
            state_start = (group * NSTATE).astype(jnp.int32)
            state_part = lax.dynamic_slice_in_dim(saved_state[section], state_start, NSTATE, 2).astype(jnp.float32)
            conv_state_part = lax.dynamic_slice_in_dim(conv_state[section], state_start, NSTATE, 2)

            def member_term(state_total, member):
                device = group * GROUP_SPAN + member
                channel_start = (device * group_width).astype(jnp.int32)
                head_start = (device * HEADS_DEV).astype(jnp.int32)
                main_part = lax.dynamic_slice_in_dim(saved_main[section], channel_start, group_width, 2).astype(jnp.float32)
                step_part = lax.dynamic_slice_in_dim(saved_step[section], head_start, HEADS_DEV, 0).astype(jnp.float32)
                conv_main_part = lax.dynamic_slice_in_dim(conv_main[section], channel_start, group_width, 1)
                bias_part = lax.dynamic_slice_in_dim(step_bias[section], head_start, HEADS_DEV, 0)
                decay_part = lax.dynamic_slice_in_dim(decay_log[section], head_start, HEADS_DEV, 0)
                skip_part = lax.dynamic_slice_in_dim(skip_gain[section], head_start, HEADS_DEV, 0)
                gain_part = lax.dynamic_slice_in_dim(norm_gain[section], channel_start, group_width, 0)
                out_rows = lax.dynamic_slice_in_dim(weight_out[section], channel_start, group_width, 0)
                main_cols = lax.dynamic_slice_in_dim(weight_main[section], channel_start, group_width, 2).reshape(D, -1)
                step_rows = lax.dynamic_slice_in_dim(weight_step[section], head_start, HEADS_DEV, 0)

                def local_mixer(first_in, second_in, third_in):
                    return mamba_mixer(first_in, second_in, third_in, conv_main_part, conv_state_part, bias_part, decay_part, skip_part, gain_part)
                dnormed = lax.dot_general(carry, out_rows, (((1,), (1,)), ((), ())), preferred_element_type=jnp.float32)
                _, pullback = jax.vjp(local_mixer, main_part, state_part, step_part)
                grad_main, grad_state, grad_step = pullback(dnormed)
                grad_main = grad_main.astype(jnp.bfloat16).reshape(SEQLEN, -1)
                grad_step = grad_step.astype(jnp.bfloat16)
                partial_sum = lax.dot_general(grad_main, main_cols, (((1,), (1,)), ((), ())), preferred_element_type=jnp.float32)
                partial_sum = partial_sum + lax.dot_general(grad_step, step_rows, (((0,), (0,)), ((), ())), preferred_element_type=jnp.float32)
                return (state_total + grad_state, partial_sum)
            anchor = jnp.zeros((SEQLEN, 2, NSTATE), jnp.float32)
            state_total, partials = lax.scan(member_term, anchor, jnp.arange(GROUP_SPAN, dtype=jnp.int32))
            grad_state = state_total.astype(jnp.bfloat16)
            for member in range(GROUP_SPAN):
                piece = grad_state[:, :, member * quarter:(member + 1) * quarter].reshape(SEQLEN, -1)
                cols = lax.dynamic_slice_in_dim(weight_state[section], state_start + member * quarter, quarter, 2).reshape(D, -1)
                term = partials[member] + lax.dot_general(piece, cols, (((1,), (1,)), ((), ())), preferred_element_type=jnp.float32)
                summed = summed + term
            return (summed, None)
        summed, _ = lax.scan(group_term, jnp.zeros((SEQLEN, D), jnp.float32), jnp.arange(GROUPS, dtype=jnp.int32))
        carry = summed.astype(jnp.bfloat16)
        results.append(carry)
    return jnp.stack(results[::-1])
```

```python
import jax
import jax.numpy as jnp
from jax import lax
from jax.experimental import pallas as pl
from jax.experimental.pallas import tpu as pltpu
from jax.sharding import PartitionSpec as P

NSTATE = 128
GROUP_SPAN = 4
STRETCH = 128


EPSILON = 1e-05
HIGHEST = lax.Precision.HIGHEST


def from_partner(value, axis, bit):
    mask = 2**bit
    pairs = [(source, source ^ mask) for source in range(lax.axis_size(axis))]
    return lax.ppermute(value, axis, pairs)


def passed_along(value, axis, steps):
    count = lax.axis_size(axis)
    leading, last = (max(0, -steps), min(count, count - steps))
    return lax.ppermute(value, axis, [(source, source + steps) for source in range(leading, last)])


def causal_conv(signal, kernel):
    taps = kernel.shape[0]
    length = signal.shape[0]
    padded = jnp.pad(signal, ((taps - 1, 0), (0, 0)))
    summed = kernel[0] * padded[0:length]
    for offset in range(1, taps):
        summed = summed + kernel[offset] * padded[offset : offset + length]
    return summed


def state_space(values, step_sizes, decay_rates, inputs, readout):
    length, head_count, head_size = values.shape
    blocks = length // STRETCH
    state_width = inputs.shape[1]
    decays = (step_sizes * decay_rates[:, None]).reshape(head_count, blocks, STRETCH)
    running = jnp.cumsum(decays, axis=2)
    scaled = (values * step_sizes.T[:, :, None]).reshape(blocks, STRETCH, head_count, head_size)
    inputs_blocked = inputs.reshape(blocks, STRETCH, state_width)
    readout_blocked = readout.reshape(blocks, STRETCH, state_width)
    scores = jnp.einsum("cin,cjn->cij", readout_blocked, inputs_blocked, precision=HIGHEST)
    position = jnp.arange(STRETCH)
    causal = position[:, None] >= position[None, :]
    differ = running[:, :, :, None] - running[:, :, None, :]
    weights = jnp.where(causal, jnp.exp(jnp.where(causal, differ, 0.0)), 0.0) * scores[None]
    within = jnp.einsum("hcij,cjhp->cihp", weights, scaled, precision=HIGHEST)
    tail_decay = jnp.exp(running[:, :, -1:] - running)
    weighted = scaled * jnp.transpose(tail_decay, (1, 2, 0))[:, :, :, None]
    block_sums = jnp.einsum("cjhp,cjn->chpn", weighted, inputs_blocked, precision=HIGHEST)
    shrinks = jnp.exp(running[:, :, -1]).T

    def advance(carried, item):
        newest, shrink = item
        return (carried * shrink[:, None, None] + newest, carried)

    anchor = jnp.zeros((head_count, head_size, state_width), jnp.float32)
    _, entering = lax.scan(advance, anchor, (block_sums, shrinks))
    across = jnp.einsum("cin,chpn->cihp", readout_blocked, entering, precision=HIGHEST)
    across = across * jnp.transpose(jnp.exp(running), (1, 2, 0))[:, :, :, None]
    return (within + across).reshape(length, head_count, head_size)


def mamba_mixer(
    main_proj,
    state_proj,
    step_proj,
    conv_main,
    conv_state,
    step_bias,
    decay_log,
    skip_gain,
    norm_gain,
):
    length = main_proj.shape[0]
    head_count = step_proj.shape[0]
    gating = main_proj[:, 0]
    mixed_in = jax.nn.silu(causal_conv(main_proj[:, 1], conv_main))
    flat_state = state_proj.reshape(length, -1)
    state_conv = jax.nn.silu(
        causal_conv(flat_state, conv_state.reshape(conv_state.shape[0], -1))
    ).reshape(length, 2, -1)
    step_sizes = jax.nn.softplus(step_proj + step_bias[:, None])
    decay_rates = -jnp.exp(decay_log)
    values = mixed_in.reshape(length, head_count, -1)
    scanned = state_space(values, step_sizes, decay_rates, state_conv[:, 0], state_conv[:, 1])
    scanned = scanned + skip_gain[None, :, None] * values
    gated = scanned.reshape(length, -1) * jax.nn.silu(gating)
    inverse = lax.rsqrt(jnp.mean(gated * gated, axis=1, keepdims=True) + EPSILON)
    return gated * inverse * norm_gain


def wide_body(
    weight_main,
    weight_state,
    weight_step,
    weight_out,
    conv_main,
    conv_state,
    step_bias,
    decay_log,
    skip_gain,
    norm_gain,
    saved_main,
    saved_state,
    saved_step,
    output_grad,
):
    sections = lax.axis_size("pipe")
    section = lax.axis_index("pipe")
    tensor_index = lax.axis_index("tensor")
    member = tensor_index % GROUP_SPAN
    group = tensor_index // GROUP_SPAN
    span_bits = GROUP_SPAN.bit_length() - 1
    length = saved_main.shape[1]
    col_count = output_grad.shape[1]
    model_width = weight_out.shape[2]
    main_cols = weight_main[0].reshape(model_width, -1)
    state_cols = weight_state[0].reshape(model_width, -1)
    step_rows = weight_step[0]
    out_rows = weight_out[0]
    state_group = lax.dynamic_slice_in_dim(saved_state[0], group * NSTATE, NSTATE, 2)
    conv_group = lax.dynamic_slice_in_dim(conv_state[0], group * NSTATE, NSTATE, 2)

    def local_mixer(first_in, second_in, third_in):
        return mamba_mixer(
            first_in,
            second_in,
            third_in,
            conv_main[0],
            conv_group,
            step_bias[0],
            decay_log[0],
            skip_gain[0],
            norm_gain[0],
        )

    _, pullback = jax.vjp(
        local_mixer,
        saved_main[0].astype(jnp.float32),
        state_group.astype(jnp.float32),
        saved_step[0].astype(jnp.float32),
    )
    result = jnp.zeros((length, col_count), jnp.bfloat16)
    incoming = output_grad
    for moment in range(sections):
        back_grad_main, back_grad_state, back_grad_step = pullback(
            lax.dot_general(
                lax.all_gather(incoming, "tensor", axis=1, tiled=True),
                out_rows,
                (((1,), (1,)), ((), ())),
                preferred_element_type=jnp.float32,
            )
        )
        kept = back_grad_state
        for bit in range(span_bits - 1, -1, -1):
            half = kept.shape[2] // 2
            lower = kept[:, :, :half]
            upper = kept[:, :, half:]
            high = member // 2**bit % 2 == 1
            own = jnp.where(high, upper, lower)
            other = jnp.where(high, lower, upper)
            kept = own + from_partner(other, "tensor", bit)
        grad_main = back_grad_main.astype(jnp.bfloat16).reshape(length, -1)
        grad_state = kept.astype(jnp.bfloat16).reshape(length, -1)
        grad_step = back_grad_step.astype(jnp.bfloat16)
        summed = lax.dot_general(
            main_cols, grad_main, (((1,), (1,)), ((), ())), preferred_element_type=jnp.float32
        )
        summed = summed + lax.dot_general(
            state_cols, grad_state, (((1,), (1,)), ((), ())), preferred_element_type=jnp.float32
        )
        owned = lax.psum_scatter(
            summed
            + lax.dot_general(
                step_rows, grad_step, (((0,), (0,)), ((), ())), preferred_element_type=jnp.float32
            ),
            "tensor",
            scatter_dimension=0,
            tiled=True,
        ).T.astype(jnp.bfloat16)
        result = jnp.where(section == sections - 1 - moment, owned, result)
        if moment + 1 < sections:
            incoming = passed_along(owned, "pipe", -1)
    return result[None]


BF16 = jnp.bfloat16
F32 = jnp.float32
SPACE = pltpu.VMEM
VMEM_BYTES = 48 * 2**20


def dot_nt(left, right, **options):
    return lax.dot_general(
        left, right, (((1,), (1,)), ((), ())), preferred_element_type=F32, **options
    )


def dot_tn(left, right):
    return lax.dot_general(left, right, (((0,), (0,)), ((), ())), preferred_element_type=F32)


def dot_nn(left, right, **options):
    return jnp.dot(left, right, preferred_element_type=F32, **options)


def iota(shape, dim):
    return lax.broadcasted_iota(jnp.int32, shape, dim)


def head_lanes(shape, head, size):
    lane = iota(shape, 1)
    return (lane >= head * size) & (lane < (head + 1) * size)


def conv_taps(signal, taps):
    count = taps.shape[0]
    row = iota(signal.shape, 0)
    total = taps[count - 1 : count] * signal
    for back in range(1, count):
        moved = jnp.where(row >= back, pltpu.roll(signal, back, 0), 0.0)
        total = total + taps[count - 1 - back : count - back] * moved
    return total


def conv_taps_back(grad, taps):
    count = taps.shape[0]
    length = grad.shape[0]
    row = iota(grad.shape, 0)
    total = taps[count - 1 : count] * grad
    for ahead in range(1, count):
        moved = jnp.where(row < length - ahead, pltpu.roll(grad, length - ahead, 0), 0.0)
        total = total + taps[count - 1 - ahead : count - ahead] * moved
    return total


def silu_and_slope(value):
    gate = jax.nn.sigmoid(value)
    return value * gate, gate * (1.0 + value * (1.0 - gate))


def forward_kernel(
    heads,
    gate_ref,
    mixer_ref,
    state_ref,
    step_ref,
    taps_main_ref,
    taps_state_ref,
    heads_ref,
    gain_ref,
    maps_ref,
    decay_ref,
    decayed_ref,
    values_ref,
    state_out_ref,
    slope_ref,
):
    length, channels = gate_ref.shape
    size = channels // heads
    states = state_ref.shape[1] // 2
    gate, gate_slope = silu_and_slope(gate_ref[...].astype(F32))
    value, value_slope = silu_and_slope(
        conv_taps(mixer_ref[...].astype(F32), taps_main_ref[...])
    )
    state, state_slope = silu_and_slope(
        conv_taps(state_ref[...].astype(F32), taps_state_ref[...])
    )
    inputs = state[:, :states]
    readout = state[:, states:]
    raw_step = step_ref[...] + heads_ref[0:1]
    step = jnp.maximum(raw_step, 0.0) + jnp.log1p(jnp.exp(-jnp.abs(raw_step)))
    slope_ref[...] = jax.nn.sigmoid(raw_step)
    rate = -jnp.exp(heads_ref[1:2])
    square = (length, length)
    later = iota(square, 0) >= iota(square, 1)
    earlier = iota(square, 0) <= iota(square, 1)
    running = dot_nn(later.astype(F32), step * rate, precision=HIGHEST)
    running_row = running.T
    scores = dot_nt(readout, inputs, precision=HIGHEST)
    scores_back = dot_nt(inputs, readout, precision=HIGHEST)
    wide = (length, channels)
    step_wide = jnp.zeros(wide, F32)
    skip_wide = jnp.zeros(wide, F32)
    for head in range(heads):
        lanes = head_lanes(wide, head, size)
        step_wide = jnp.where(lanes, step[:, head : head + 1], step_wide)
        skip_wide = jnp.where(lanes, heads_ref[2:3, head : head + 1], skip_wide)
    scaled = value * step_wide
    output = skip_wide * value
    for head in range(heads):
        lanes = head_lanes(wide, head, size)
        columns = pl.ds(head * length, length)
        column = running[:, head : head + 1]
        row = running_row[head : head + 1, :]
        decay = jnp.where(later, jnp.exp(jnp.where(later, column - row, 0.0)), 0.0)
        back = jnp.where(earlier, jnp.exp(jnp.where(earlier, row - column, 0.0)), 0.0)
        weights = decay * scores
        own = jnp.where(lanes, scaled, 0.0)
        output = output + dot_nn(weights, own, precision=HIGHEST)
        decay_ref[0, :, columns] = decay
        decay_ref[1, :, columns] = weights
        decayed_ref[:, columns] = (back * scores_back).astype(BF16)
        values_ref[columns, :] = own.astype(BF16)
    gated = output * gate
    inverse = lax.rsqrt(jnp.mean(gated * gated, axis=1, keepdims=True) + EPSILON)
    gain = gain_ref[...]
    normal = gated * inverse
    maps_ref[0] = gain * inverse
    maps_ref[1] = normal * inverse
    maps_ref[2] = gain * normal * (1.0 / channels)
    maps_ref[3] = gate
    maps_ref[4] = output * gate_slope
    maps_ref[5] = skip_wide * value_slope
    maps_ref[6] = step_wide * value_slope
    maps_ref[7] = value
    maps_ref[8] = state_slope
    state_out_ref[0] = inputs.astype(BF16)
    state_out_ref[1] = readout.astype(BF16)


def mixer_back(heads, dnormed, residuals):
    (
        maps_ref,
        decay_ref,
        decayed_ref,
        values_ref,
        state_ref,
        slope_ref,
        taps_main_ref,
        taps_state_ref,
        heads_ref,
    ) = residuals
    length, channels = dnormed.shape
    size = channels // heads
    shared = jnp.sum(dnormed * maps_ref[2], axis=1, keepdims=True)
    d_gated = dnormed * maps_ref[0] - maps_ref[1] * shared
    d_output = d_gated * maps_ref[3]
    d_gate = d_gated * maps_ref[4]
    by_head = jnp.concatenate(
        [
            jnp.where(head_lanes(d_output.shape, head, size), d_output, 0.0).astype(BF16)
            for head in range(heads)
        ],
        axis=0,
    )
    d_scaled = dot_nn(decayed_ref[...], by_head)
    d_weights = dot_nt(d_output.astype(BF16), values_ref[...])
    d_decayed = d_weights * decay_ref[0]
    d_scores = d_decayed[:, :length]
    for head in range(1, heads):
        d_scores = d_scores + d_decayed[:, head * length : (head + 1) * length]
    d_exponent = d_weights * decay_ref[1]
    square = (length, length)
    onward = (iota(square, 0) <= iota(square, 1)).astype(BF16)
    spanning = dot_nn(onward, d_exponent.astype(BF16))
    row = iota(spanning.shape, 0)
    source = iota(spanning.shape, 1) % length
    spanning = jnp.where(source < row, spanning, 0.0)
    lane = iota((channels, 128), 1)
    of_channel = (iota((channels, 128), 0) // size == lane).astype(BF16)
    of_source = (
        iota((heads * length, 128), 0) // length == iota((heads * length, 128), 1)
    ).astype(BF16)
    rate = -jnp.exp(heads_ref[1:2])
    d_step = dot_nn((d_scaled * maps_ref[7]).astype(BF16), of_channel)
    d_step = d_step + rate * dot_nn(spanning.astype(BF16), of_source)
    d_step = d_step * slope_ref[...]
    rounded = d_scores.astype(BF16)
    d_readout = dot_nn(rounded, state_ref[0])
    d_inputs = dot_tn(rounded, state_ref[1])
    d_state = jnp.concatenate([d_inputs, d_readout], axis=1) * maps_ref[8]
    d_mixer = d_output * maps_ref[5] + d_scaled * maps_ref[6]
    main = jnp.concatenate(
        [
            d_gate.astype(BF16),
            conv_taps_back(d_mixer, taps_main_ref[...]).astype(BF16),
            d_step.astype(BF16),
        ],
        axis=1,
    )
    return main, conv_taps_back(d_state, taps_state_ref[...]).astype(BF16)


def section_kernel(heads, chunks, first, *refs):
    count = chunks
    incoming = refs[:count]
    refs = refs[count:]
    out_rows_ref = None
    if first:
        out_rows_ref, refs = refs[0], refs[1:]
    residuals, refs = refs[:9], refs[9:]
    cols_ref, refs = refs[0], refs[1:]
    outs, refs = refs[:chunks], refs[chunks:]
    cols, cols_sems = refs[0], refs[1]
    me = lax.axis_index("tensor")
    width = cols.shape[1]
    copies = []
    if first:
        rows, rows_sem = refs[2], refs[3]
        rows_copy = pltpu.make_async_copy(out_rows_ref, rows, rows_sem)
        rows_copy.start()
    for hop in range(chunks):
        chunk = lax.rem(me + hop, chunks)
        copy = pltpu.make_async_copy(
            cols_ref.at[pl.ds(pl.multiple_of(chunk * width, width), width), :],
            cols.at[hop],
            cols_sems.at[hop],
        )
        copy.start()
        copies.append(copy)
    if first:
        rows_copy.wait()
        dnormed = None
        for hop in range(chunks):
            chunk = lax.rem(me + chunks - hop, chunks)
            term = dot_nt(
                incoming[hop][...], rows[:, pl.ds(pl.multiple_of(chunk * width, width), width)]
            )
            dnormed = term if dnormed is None else dnormed + term
    else:
        dnormed = incoming[0][...].astype(F32)
        for hop in range(1, chunks):
            dnormed = dnormed + incoming[hop][...].astype(F32)
    main, state = mixer_back(heads, dnormed, residuals)
    for hop in range(chunks):
        copies[hop].wait()
        outs[hop][:, :width] = dot_nt(main, cols[hop]).astype(BF16)
        outs[hop][:, width:] = state


def carry_kernel(chunks, last, *refs):
    parts = refs[:chunks]
    state_ref, refs = refs[chunks], refs[chunks + 1 :]
    if not last:
        own_ref, other_ref, refs = refs[0], refs[1], refs[2:]
        carry_ref, outs, refs = refs[0], refs[1 : 1 + chunks], refs[1 + chunks :]
        own, other, sems = refs
        copies = [
            pltpu.make_async_copy(own_ref, own, sems.at[0]),
            pltpu.make_async_copy(other_ref, other, sems.at[1]),
        ]
        for copy in copies:
            copy.start()
    else:
        carry_ref = refs[0]
    width = carry_ref.shape[1]
    total = parts[0][...].astype(F32)
    for part in parts[1:]:
        total = total + part[...].astype(F32)
    carry = total[:, :width] + dot_nn(total[:, width:].astype(BF16), state_ref[...])
    carry = carry.astype(BF16)
    carry_ref[...] = carry
    if not last:
        half = own.shape[0] // chunks
        core = lax.axis_index("dp")
        for copy, held, place in ((copies[0], own, core), (copies[1], other, 1 - core)):
            copy.wait()
            product = dot_nt(carry, held[...]).astype(BF16)
            lanes = pl.ds(pl.multiple_of(place * half, half), half)
            for hop in range(chunks):
                outs[hop][:, lanes] = product[:, hop * half : (hop + 1) * half]


def kernel_params():
    return pltpu.CompilerParams(vmem_limit_bytes=VMEM_BYTES)


def whole(count):
    return [pl.BlockSpec(memory_space=SPACE)] * count


def section_pairs(sections, chunks, source, target, hop):
    return [
        (source * chunks + index, target * chunks + (index + hop) % chunks)
        for index in range(chunks)
    ]


def relay_body(
    weight_main,
    weight_state,
    weight_step,
    weight_out,
    conv_main,
    conv_state,
    step_bias,
    decay_log,
    skip_gain,
    norm_gain,
    saved_main,
    saved_state,
    saved_step,
    output_grad,
):
    sections = lax.axis_size("pipe")
    chunks = lax.axis_size("tensor")
    section = lax.axis_index("pipe")
    me = lax.axis_index("tensor")
    core = lax.axis_index("dp")
    length, width = output_grad.shape
    model_width = weight_out.shape[2]
    heads = step_bias.shape[1]
    channels = weight_out.shape[1]
    half_rows = channels // 2
    half_width = width // 2
    place = ("pipe", "tensor")

    last_own = jnp.where(section == sections - 1, output_grad, jnp.zeros_like(output_grad))
    incoming = [last_own]
    for hop in range(1, chunks):
        pairs = section_pairs(sections, chunks, sections - 1, sections - 1, hop)
        incoming.append(lax.ppermute(output_grad, place, pairs))

    own_half = []
    for hop in range(chunks):
        chunk = (me + hop) % chunks
        piece = lax.dynamic_slice(
            weight_out[0], (core * half_rows, chunk * width), (half_rows, width)
        )
        pairs = []
        for source in range(sections - 1):
            pairs += section_pairs(sections, chunks, source, source + 1, hop)
        own_half.append(lax.ppermute(piece, place, pairs))
    own_half = jnp.concatenate(own_half, axis=0)
    other_half = lax.ppermute(own_half, "dp", [(0, 1), (1, 0)])

    state_cols = weight_state[0].reshape(model_width, -1).T
    pieces = []
    for hop in range(chunks):
        chunk = (me + hop) % chunks
        piece = lax.dynamic_slice(
            state_cols,
            (0, chunk * width + core * half_width),
            (state_cols.shape[0], half_width),
        )
        if hop:
            pairs = [(index, (index + hop) % chunks) for index in range(chunks)]
            piece = lax.ppermute(piece, "tensor", pairs)
        pieces.append(piece)
    state_own = jnp.stack(pieces)
    state_other = lax.ppermute(state_own, "dp", [(0, 1), (1, 0)])
    lower = jnp.where(core == 0, state_own, state_other)
    upper = jnp.where(core == 0, state_other, state_own)
    state_rows = jnp.concatenate([lower, upper], axis=2)
    order = (me - jnp.arange(chunks)) % chunks
    state_rows = jnp.take(state_rows, order, axis=0)
    state_rows = state_rows.reshape(chunks, 2, -1, width).transpose(1, 0, 2, 3)
    state_rows = state_rows.reshape(-1, width)

    step_cols = jnp.pad(weight_step[0].T, ((0, 0), (0, 128 - heads)))
    cols = jnp.concatenate([weight_main[0].reshape(model_width, -1), step_cols], axis=1)

    lanes = ((0, 0), (0, 128 - heads))
    by_head = jnp.pad(
        jnp.stack([step_bias[0], decay_log[0], skip_gain[0]]), ((0, 5), (0, 128 - heads))
    )
    steps = jnp.pad(saved_step[0].astype(F32).T, lanes)
    taps_main = conv_main[0]
    taps_state = conv_state[0].reshape(conv_state.shape[1], -1)
    state_width = taps_state.shape[1]
    residual_shapes = (
        jax.ShapeDtypeStruct((9, length, channels), F32),
        jax.ShapeDtypeStruct((2, length, heads * length), F32),
        jax.ShapeDtypeStruct((length, heads * length), BF16),
        jax.ShapeDtypeStruct((heads * length, channels), BF16),
        jax.ShapeDtypeStruct((2, length, state_width // 2), BF16),
        jax.ShapeDtypeStruct((length, 128), F32),
    )
    residuals = pl.pallas_call(
        lambda *refs: forward_kernel(heads, *refs),
        out_shape=residual_shapes,
        in_specs=whole(8),
        out_specs=whole(6),
        compiler_params=kernel_params(),
        name="forward_residuals",
    )(
        saved_main[0, :, 0],
        saved_main[0, :, 1],
        saved_state[0].reshape(length, -1),
        steps,
        taps_main,
        taps_state,
        by_head,
        norm_gain,
    )
    residuals = tuple(residuals) + (taps_main, taps_state, by_head)
    message = jax.ShapeDtypeStruct((length, width + state_width), BF16)
    slice_out = jax.ShapeDtypeStruct((length, channels), BF16)
    hbm = pl.BlockSpec(memory_space=pl.ANY)

    result = jnp.zeros((length, width), BF16)
    for moment in range(sections):
        active = sections - 1 - moment
        first = moment == 0
        last = moment + 1 == sections
        scratch = [
            pltpu.VMEM((chunks, width, cols.shape[1]), BF16),
            pltpu.SemaphoreType.DMA((chunks,)),
        ]
        if first:
            scratch += [pltpu.VMEM((channels, model_width), BF16), pltpu.SemaphoreType.DMA]
        parts = pl.pallas_call(
            lambda *refs, first=first: section_kernel(heads, chunks, first, *refs),
            out_shape=(message,) * chunks,
            in_specs=whole(chunks) + [hbm] * first + whole(9) + [hbm],
            out_specs=whole(chunks),
            scratch_shapes=scratch,
            compiler_params=kernel_params(),
            name="section_first" if first else "section_next",
        )(*incoming, *((weight_out[0],) if first else ()), *residuals, cols)
        gathered = [parts[0]]
        for hop in range(1, chunks):
            pairs = section_pairs(sections, chunks, active, active, hop)
            gathered.append(lax.ppermute(parts[hop], place, pairs))
        carry_shape = jax.ShapeDtypeStruct((length, width), BF16)
        scratch = []
        if not last:
            scratch = [
                pltpu.VMEM(own_half.shape, BF16),
                pltpu.VMEM(own_half.shape, BF16),
                pltpu.SemaphoreType.DMA((2,)),
            ]
        outs = pl.pallas_call(
            lambda *refs, last=last: carry_kernel(chunks, last, *refs),
            out_shape=(carry_shape,) + (() if last else (slice_out,) * chunks),
            in_specs=whole(chunks + 1) + ([] if last else [hbm] * 2),
            out_specs=whole(1 if last else 1 + chunks),
            scratch_shapes=scratch,
            compiler_params=kernel_params(),
            name="carry_last" if last else "carry_next",
        )(*gathered, state_rows, *(() if last else (own_half, other_half)))
        result = jnp.where(section == active, outs[0], result)
        if not last:
            incoming = []
            for hop in range(chunks):
                pairs = section_pairs(sections, chunks, active, active - 1, chunks - hop)
                incoming.append(lax.ppermute(outs[1 + hop], place, pairs))
    return result[None]


def solution(mesh):
    narrow = mesh.shape["tensor"] == GROUP_SPAN
    return jax.shard_map(
        relay_body if narrow else wide_body,
        mesh=mesh,
        in_specs=(
            P("pipe", None, None, "tensor"),
            P("pipe", None, None, "tensor"),
            P("pipe", "tensor", None),
            P("pipe", "tensor", None),
            P("pipe", None, "tensor"),
            P("pipe", None, None, None),
            P("pipe", "tensor"),
            P("pipe", "tensor"),
            P("pipe", "tensor"),
            P("pipe", "tensor"),
            P("pipe", "dp", None, "tensor"),
            P("pipe", "dp", None, None),
            P("pipe", "tensor", "dp"),
            P("dp", "tensor"),
        ),
        out_specs=P("pipe", "dp", "tensor"),
        check_vma=False,
    )
```

```python
import jax
import jax.numpy as jnp
from jax import lax
from jax.experimental import pallas as pl
from jax.experimental.pallas import tpu as pltpu
from jax.sharding import PartitionSpec as P

NSTATE = 128
GROUP_SPAN = 4
STRETCH = 128


EPSILON = 1e-05
HIGHEST = lax.Precision.HIGHEST


def from_partner(value, axis, bit):
    mask = 2**bit
    pairs = [(source, source ^ mask) for source in range(lax.axis_size(axis))]
    return lax.ppermute(value, axis, pairs)


def passed_along(value, axis, steps):
    count = lax.axis_size(axis)
    leading, last = (max(0, -steps), min(count, count - steps))
    return lax.ppermute(value, axis, [(source, source + steps) for source in range(leading, last)])


def causal_conv(signal, kernel):
    taps = kernel.shape[0]
    length = signal.shape[0]
    padded = jnp.pad(signal, ((taps - 1, 0), (0, 0)))
    summed = kernel[0] * padded[0:length]
    for offset in range(1, taps):
        summed = summed + kernel[offset] * padded[offset : offset + length]
    return summed


def state_space(values, step_sizes, decay_rates, inputs, readout):
    length, head_count, head_size = values.shape
    blocks = length // STRETCH
    state_width = inputs.shape[1]
    decays = (step_sizes * decay_rates[:, None]).reshape(head_count, blocks, STRETCH)
    running = jnp.cumsum(decays, axis=2)
    scaled = (values * step_sizes.T[:, :, None]).reshape(blocks, STRETCH, head_count, head_size)
    inputs_blocked = inputs.reshape(blocks, STRETCH, state_width)
    readout_blocked = readout.reshape(blocks, STRETCH, state_width)
    scores = jnp.einsum("cin,cjn->cij", readout_blocked, inputs_blocked, precision=HIGHEST)
    position = jnp.arange(STRETCH)
    causal = position[:, None] >= position[None, :]
    differ = running[:, :, :, None] - running[:, :, None, :]
    weights = jnp.where(causal, jnp.exp(jnp.where(causal, differ, 0.0)), 0.0) * scores[None]
    within = jnp.einsum("hcij,cjhp->cihp", weights, scaled, precision=HIGHEST)
    tail_decay = jnp.exp(running[:, :, -1:] - running)
    weighted = scaled * jnp.transpose(tail_decay, (1, 2, 0))[:, :, :, None]
    block_sums = jnp.einsum("cjhp,cjn->chpn", weighted, inputs_blocked, precision=HIGHEST)
    shrinks = jnp.exp(running[:, :, -1]).T

    def advance(carried, item):
        newest, shrink = item
        return (carried * shrink[:, None, None] + newest, carried)

    anchor = jnp.zeros((head_count, head_size, state_width), jnp.float32)
    _, entering = lax.scan(advance, anchor, (block_sums, shrinks))
    across = jnp.einsum("cin,chpn->cihp", readout_blocked, entering, precision=HIGHEST)
    across = across * jnp.transpose(jnp.exp(running), (1, 2, 0))[:, :, :, None]
    return (within + across).reshape(length, head_count, head_size)


def mamba_mixer(
    main_proj,
    state_proj,
    step_proj,
    conv_main,
    conv_state,
    step_bias,
    decay_log,
    skip_gain,
    norm_gain,
):
    length = main_proj.shape[0]
    head_count = step_proj.shape[0]
    gating = main_proj[:, 0]
    mixed_in = jax.nn.silu(causal_conv(main_proj[:, 1], conv_main))
    flat_state = state_proj.reshape(length, -1)
    state_conv = jax.nn.silu(
        causal_conv(flat_state, conv_state.reshape(conv_state.shape[0], -1))
    ).reshape(length, 2, -1)
    step_sizes = jax.nn.softplus(step_proj + step_bias[:, None])
    decay_rates = -jnp.exp(decay_log)
    values = mixed_in.reshape(length, head_count, -1)
    scanned = state_space(values, step_sizes, decay_rates, state_conv[:, 0], state_conv[:, 1])
    scanned = scanned + skip_gain[None, :, None] * values
    gated = scanned.reshape(length, -1) * jax.nn.silu(gating)
    inverse = lax.rsqrt(jnp.mean(gated * gated, axis=1, keepdims=True) + EPSILON)
    return gated * inverse * norm_gain


def wide_body(
    weight_main,
    weight_state,
    weight_step,
    weight_out,
    conv_main,
    conv_state,
    step_bias,
    decay_log,
    skip_gain,
    norm_gain,
    saved_main,
    saved_state,
    saved_step,
    output_grad,
):
    sections = lax.axis_size("pipe")
    section = lax.axis_index("pipe")
    tensor_index = lax.axis_index("tensor")
    member = tensor_index % GROUP_SPAN
    group = tensor_index // GROUP_SPAN
    span_bits = GROUP_SPAN.bit_length() - 1
    length = saved_main.shape[1]
    col_count = output_grad.shape[1]
    model_width = weight_out.shape[2]
    main_cols = weight_main[0].reshape(model_width, -1)
    state_cols = weight_state[0].reshape(model_width, -1)
    step_rows = weight_step[0]
    out_rows = weight_out[0]
    state_group = lax.dynamic_slice_in_dim(saved_state[0], group * NSTATE, NSTATE, 2)
    conv_group = lax.dynamic_slice_in_dim(conv_state[0], group * NSTATE, NSTATE, 2)

    def local_mixer(first_in, second_in, third_in):
        return mamba_mixer(
            first_in,
            second_in,
            third_in,
            conv_main[0],
            conv_group,
            step_bias[0],
            decay_log[0],
            skip_gain[0],
            norm_gain[0],
        )

    _, pullback = jax.vjp(
        local_mixer,
        saved_main[0].astype(jnp.float32),
        state_group.astype(jnp.float32),
        saved_step[0].astype(jnp.float32),
    )
    result = jnp.zeros((length, col_count), jnp.bfloat16)
    incoming = output_grad
    for moment in range(sections):
        back_grad_main, back_grad_state, back_grad_step = pullback(
            lax.dot_general(
                lax.all_gather(incoming, "tensor", axis=1, tiled=True),
                out_rows,
                (((1,), (1,)), ((), ())),
                preferred_element_type=jnp.float32,
            )
        )
        kept = back_grad_state
        for bit in range(span_bits - 1, -1, -1):
            half = kept.shape[2] // 2
            lower = kept[:, :, :half]
            upper = kept[:, :, half:]
            high = member // 2**bit % 2 == 1
            own = jnp.where(high, upper, lower)
            other = jnp.where(high, lower, upper)
            kept = own + from_partner(other, "tensor", bit)
        grad_main = back_grad_main.astype(jnp.bfloat16).reshape(length, -1)
        grad_state = kept.astype(jnp.bfloat16).reshape(length, -1)
        grad_step = back_grad_step.astype(jnp.bfloat16)
        summed = lax.dot_general(
            main_cols, grad_main, (((1,), (1,)), ((), ())), preferred_element_type=jnp.float32
        )
        summed = summed + lax.dot_general(
            state_cols, grad_state, (((1,), (1,)), ((), ())), preferred_element_type=jnp.float32
        )
        owned = lax.psum_scatter(
            summed
            + lax.dot_general(
                step_rows, grad_step, (((0,), (0,)), ((), ())), preferred_element_type=jnp.float32
            ),
            "tensor",
            scatter_dimension=0,
            tiled=True,
        ).T.astype(jnp.bfloat16)
        result = jnp.where(section == sections - 1 - moment, owned, result)
        if moment + 1 < sections:
            incoming = passed_along(owned, "pipe", -1)
    return result[None]


BF16 = jnp.bfloat16
F32 = jnp.float32
SPACE = pltpu.VMEM
VMEM_BYTES = 48 * 2**20


def dot_nt(left, right, **options):
    return lax.dot_general(
        left, right, (((1,), (1,)), ((), ())), preferred_element_type=F32, **options
    )


def dot_tn(left, right):
    return lax.dot_general(left, right, (((0,), (0,)), ((), ())), preferred_element_type=F32)


def dot_nn(left, right, **options):
    return jnp.dot(left, right, preferred_element_type=F32, **options)


def iota(shape, dim):
    return lax.broadcasted_iota(jnp.int32, shape, dim)


def head_lanes(shape, head, size):
    lane = iota(shape, 1)
    return (lane >= head * size) & (lane < (head + 1) * size)


def conv_taps(signal, taps):
    count = taps.shape[0]
    row = iota(signal.shape, 0)
    total = taps[count - 1 : count] * signal
    for back in range(1, count):
        moved = jnp.where(row >= back, pltpu.roll(signal, back, 0), 0.0)
        total = total + taps[count - 1 - back : count - back] * moved
    return total


def conv_taps_back(grad, taps):
    count = taps.shape[0]
    length = grad.shape[0]
    row = iota(grad.shape, 0)
    total = taps[count - 1 : count] * grad
    for ahead in range(1, count):
        moved = jnp.where(row < length - ahead, pltpu.roll(grad, length - ahead, 0), 0.0)
        total = total + taps[count - 1 - ahead : count - ahead] * moved
    return total


def silu_and_slope(value):
    gate = jax.nn.sigmoid(value)
    return value * gate, gate * (1.0 + value * (1.0 - gate))


def forward_kernel(
    heads,
    gate_ref,
    mixer_ref,
    state_ref,
    step_ref,
    taps_main_ref,
    taps_state_ref,
    heads_ref,
    gain_ref,
    maps_ref,
    decay_ref,
    decayed_ref,
    values_ref,
    state_out_ref,
    slope_ref,
):
    length, channels = gate_ref.shape
    size = channels // heads
    states = state_ref.shape[1] // 2
    gate, gate_slope = silu_and_slope(gate_ref[...].astype(F32))
    value, value_slope = silu_and_slope(
        conv_taps(mixer_ref[...].astype(F32), taps_main_ref[...])
    )
    state, state_slope = silu_and_slope(
        conv_taps(state_ref[...].astype(F32), taps_state_ref[...])
    )
    inputs = state[:, :states]
    readout = state[:, states:]
    raw_step = step_ref[...] + heads_ref[0:1]
    step = jnp.maximum(raw_step, 0.0) + jnp.log1p(jnp.exp(-jnp.abs(raw_step)))
    slope_ref[...] = jax.nn.sigmoid(raw_step)
    rate = -jnp.exp(heads_ref[1:2])
    square = (length, length)
    later = iota(square, 0) >= iota(square, 1)
    earlier = iota(square, 0) <= iota(square, 1)
    running = dot_nn(later.astype(F32), step * rate, precision=HIGHEST)
    running_row = running.T
    scores = dot_nt(readout, inputs, precision=HIGHEST)
    scores_back = dot_nt(inputs, readout, precision=HIGHEST)
    wide = (length, channels)
    step_wide = jnp.zeros(wide, F32)
    skip_wide = jnp.zeros(wide, F32)
    for head in range(heads):
        lanes = head_lanes(wide, head, size)
        step_wide = jnp.where(lanes, step[:, head : head + 1], step_wide)
        skip_wide = jnp.where(lanes, heads_ref[2:3, head : head + 1], skip_wide)
    scaled = value * step_wide
    output = skip_wide * value
    for head in range(heads):
        lanes = head_lanes(wide, head, size)
        columns = pl.ds(head * length, length)
        column = running[:, head : head + 1]
        row = running_row[head : head + 1, :]
        decay = jnp.where(later, jnp.exp(jnp.where(later, column - row, 0.0)), 0.0)
        back = jnp.where(earlier, jnp.exp(jnp.where(earlier, row - column, 0.0)), 0.0)
        weights = decay * scores
        own = jnp.where(lanes, scaled, 0.0)
        output = output + dot_nn(weights, own, precision=HIGHEST)
        decay_ref[0, :, columns] = decay
        decay_ref[1, :, columns] = weights
        decayed_ref[:, columns] = (back * scores_back).astype(BF16)
        values_ref[columns, :] = own.astype(BF16)
    gated = output * gate
    inverse = lax.rsqrt(jnp.mean(gated * gated, axis=1, keepdims=True) + EPSILON)
    gain = gain_ref[...]
    normal = gated * inverse
    maps_ref[0] = gain * inverse
    maps_ref[1] = normal * inverse
    maps_ref[2] = gain * normal * (1.0 / channels)
    maps_ref[3] = gate
    maps_ref[4] = output * gate_slope
    maps_ref[5] = skip_wide * value_slope
    maps_ref[6] = step_wide * value_slope
    maps_ref[7] = value
    maps_ref[8] = state_slope
    state_out_ref[0] = inputs.astype(BF16)
    state_out_ref[1] = readout.astype(BF16)


def mixer_back(heads, dnormed, residuals):
    (
        maps_ref,
        decay_ref,
        decayed_ref,
        values_ref,
        state_ref,
        slope_ref,
        taps_main_ref,
        taps_state_ref,
        heads_ref,
    ) = residuals
    length, channels = dnormed.shape
    size = channels // heads
    shared = jnp.sum(dnormed * maps_ref[2], axis=1, keepdims=True)
    d_gated = dnormed * maps_ref[0] - maps_ref[1] * shared
    d_output = d_gated * maps_ref[3]
    d_gate = d_gated * maps_ref[4]
    by_head = jnp.concatenate(
        [
            jnp.where(head_lanes(d_output.shape, head, size), d_output, 0.0).astype(BF16)
            for head in range(heads)
        ],
        axis=0,
    )
    d_scaled = dot_nn(decayed_ref[...], by_head)
    d_weights = dot_nt(d_output.astype(BF16), values_ref[...])
    d_decayed = d_weights * decay_ref[0]
    d_scores = d_decayed[:, :length]
    for head in range(1, heads):
        d_scores = d_scores + d_decayed[:, head * length : (head + 1) * length]
    d_exponent = d_weights * decay_ref[1]
    square = (length, length)
    onward = (iota(square, 0) <= iota(square, 1)).astype(BF16)
    spanning = dot_nn(onward, d_exponent.astype(BF16))
    row = iota(spanning.shape, 0)
    source = iota(spanning.shape, 1) % length
    spanning = jnp.where(source < row, spanning, 0.0)
    lane = iota((channels, 128), 1)
    of_channel = (iota((channels, 128), 0) // size == lane).astype(BF16)
    of_source = (
        iota((heads * length, 128), 0) // length == iota((heads * length, 128), 1)
    ).astype(BF16)
    rate = -jnp.exp(heads_ref[1:2])
    d_step = dot_nn((d_scaled * maps_ref[7]).astype(BF16), of_channel)
    d_step = d_step + rate * dot_nn(spanning.astype(BF16), of_source)
    d_step = d_step * slope_ref[...]
    rounded = d_scores.astype(BF16)
    d_readout = dot_nn(rounded, state_ref[0])
    d_inputs = dot_tn(rounded, state_ref[1])
    d_state = jnp.concatenate([d_inputs, d_readout], axis=1) * maps_ref[8]
    d_mixer = d_output * maps_ref[5] + d_scaled * maps_ref[6]
    main = jnp.concatenate(
        [
            d_gate.astype(BF16),
            conv_taps_back(d_mixer, taps_main_ref[...]).astype(BF16),
            d_step.astype(BF16),
        ],
        axis=1,
    )
    return main, conv_taps_back(d_state, taps_state_ref[...]).astype(BF16)


def first_kernel(heads, chunks, *refs):
    incoming, refs = refs[:chunks], refs[chunks:]
    out_rows_ref, refs = refs[0], refs[1:]
    residuals, refs = refs[:9], refs[9:]
    cols_ref, refs = refs[0], refs[1:]
    outs, refs = refs[:chunks], refs[chunks:]
    cols, cols_sems, rows, rows_sem = refs
    me = lax.axis_index("tensor")
    width = cols.shape[1]
    rows_copy = pltpu.make_async_copy(out_rows_ref, rows, rows_sem)
    rows_copy.start()
    copies = start_cols(chunks, cols_ref, cols, cols_sems)
    rows_copy.wait()
    dnormed = None
    for hop in range(chunks):
        chunk = lax.rem(me + chunks - hop, chunks)
        term = dot_nt(
            incoming[hop][...], rows[:, pl.ds(pl.multiple_of(chunk * width, width), width)]
        )
        dnormed = term if dnormed is None else dnormed + term
    main, state = mixer_back(heads, dnormed, residuals)
    project(chunks, main, state, copies, cols, outs)


def start_cols(chunks, cols_ref, cols, cols_sems):
    me = lax.axis_index("tensor")
    width = cols.shape[1]
    copies = []
    for hop in range(chunks):
        chunk = lax.rem(me + hop, chunks)
        copy = pltpu.make_async_copy(
            cols_ref.at[pl.ds(pl.multiple_of(chunk * width, width), width), :],
            cols.at[hop],
            cols_sems.at[hop],
        )
        copy.start()
        copies.append(copy)
    return copies


def project(chunks, main, state, copies, cols, outs):
    width = cols.shape[1]
    for hop in range(chunks):
        copies[hop].wait()
        outs[hop][:, :width] = dot_nt(main, cols[hop]).astype(BF16)
        outs[hop][:, width:] = state


def project_kernel(chunks, main_ref, state_ref, cols_ref, *refs):
    outs, refs = refs[:chunks], refs[chunks:]
    cols, cols_sems = refs
    copies = start_cols(chunks, cols_ref, cols, cols_sems)
    project(chunks, main_ref[...], state_ref[...], copies, cols, outs)


def next_kernel(heads, chunks, *refs):
    incoming, refs = refs[:chunks], refs[chunks:]
    residuals, refs = refs[:9], refs[9:]
    main_ref, state_ref = refs
    dnormed = incoming[0][...].astype(F32)
    for hop in range(1, chunks):
        dnormed = dnormed + incoming[hop][...].astype(F32)
    main, state = mixer_back(heads, dnormed, residuals)
    main_ref[...] = main
    state_ref[...] = state


def compose_kernel(chunks, *refs):
    rows, refs = refs[:chunks], refs[chunks:]
    cols_ref, state_cols_ref, main_ref, state_ref, main_sum, state_sum = refs
    step = pl.program_id(0)

    @pl.when(step == 0)
    def _():
        main_sum[...] = jnp.zeros_like(main_sum)
        state_sum[...] = jnp.zeros_like(state_sum)

    size = rows[0].shape[0]
    for hop in range(chunks):
        place = pl.ds(hop * size, size)
        main_sum[place, :] += dot_nn(rows[hop][...], cols_ref[...])
        state_sum[:, place] += dot_nt(state_cols_ref[...], rows[hop][...])

    @pl.when(step == pl.num_programs(0) - 1)
    def _():
        main_ref[...] = main_sum[...].astype(BF16)
        state_ref[...] = state_sum[...].astype(BF16)


def send_kernel(
    chunks, main_ref, state_ref, main_own_ref, main_other_ref, state_own_ref, state_other_ref, *outs
):
    core = lax.axis_index("dp")
    size = main_own_ref.shape[0] // chunks
    main = main_ref[...]
    state = state_ref[...]
    for main_map, state_map, place in (
        (main_own_ref, state_own_ref, core),
        (main_other_ref, state_other_ref, 1 - core),
    ):
        product = dot_nt(main, main_map[...]) + dot_nn(state, state_map[...])
        product = product.astype(BF16)
        lanes = pl.ds(pl.multiple_of(place * size, size), size)
        for hop in range(chunks):
            outs[hop][:, lanes] = product[:, hop * size : (hop + 1) * size]


def carry_kernel(chunks, last, *refs):
    parts = refs[:chunks]
    state_ref, refs = refs[chunks], refs[chunks + 1 :]
    if not last:
        own_ref, other_ref, refs = refs[0], refs[1], refs[2:]
        carry_ref, outs, refs = refs[0], refs[1 : 1 + chunks], refs[1 + chunks :]
        own, other, sems = refs
        copies = [
            pltpu.make_async_copy(own_ref, own, sems.at[0]),
            pltpu.make_async_copy(other_ref, other, sems.at[1]),
        ]
        for copy in copies:
            copy.start()
    else:
        carry_ref = refs[0]
    width = carry_ref.shape[1]
    total = parts[0][...].astype(F32)
    for part in parts[1:]:
        total = total + part[...].astype(F32)
    carry = total[:, :width] + dot_nn(total[:, width:].astype(BF16), state_ref[...])
    carry = carry.astype(BF16)
    carry_ref[...] = carry
    if not last:
        half = own.shape[0] // chunks
        core = lax.axis_index("dp")
        for copy, held, place in ((copies[0], own, core), (copies[1], other, 1 - core)):
            copy.wait()
            product = dot_nt(carry, held[...]).astype(BF16)
            lanes = pl.ds(pl.multiple_of(place * half, half), half)
            for hop in range(chunks):
                outs[hop][:, lanes] = product[:, hop * half : (hop + 1) * half]


SWAP = [(0, 1), (1, 0)]


def after(value, dependency):
    return lax.optimization_barrier((value, dependency))[0]


def by_member(pieces, order):
    count, _, width = pieces.shape
    pieces = jnp.take(pieces, order, axis=0).reshape(count, 2, -1, width)
    return pieces.transpose(1, 0, 2, 3).reshape(-1, width)


def kernel_params():
    return pltpu.CompilerParams(vmem_limit_bytes=VMEM_BYTES)


def whole(count):
    return [pl.BlockSpec(memory_space=SPACE)] * count


def section_pairs(sections, chunks, source, target, hop):
    return [
        (source * chunks + index, target * chunks + (index + hop) % chunks)
        for index in range(chunks)
    ]


def relay_body(
    weight_main,
    weight_state,
    weight_step,
    weight_out,
    conv_main,
    conv_state,
    step_bias,
    decay_log,
    skip_gain,
    norm_gain,
    saved_main,
    saved_state,
    saved_step,
    output_grad,
):
    sections = lax.axis_size("pipe")
    chunks = lax.axis_size("tensor")
    section = lax.axis_index("pipe")
    me = lax.axis_index("tensor")
    core = lax.axis_index("dp")
    length, width = output_grad.shape
    model_width = weight_out.shape[2]
    heads = step_bias.shape[1]
    channels = weight_out.shape[1]
    half_rows = channels // 2
    half_width = width // 2
    place = ("pipe", "tensor")

    incoming = [jnp.where(section == sections - 1, output_grad, jnp.zeros_like(output_grad))]
    for hop in range(1, chunks):
        pairs = section_pairs(sections, chunks, sections - 1, sections - 1, hop)
        incoming.append(lax.ppermute(output_grad, place, pairs))

    out_half = lax.dynamic_slice_in_dim(weight_out[0], core * half_rows, half_rows, 0)
    gathered_rows = []
    for hop in range(chunks):
        pairs = []
        for source in range(sections - 2):
            pairs += section_pairs(sections, chunks, source, source + 1, hop)
        gathered_rows.append(lax.ppermute(out_half, place, pairs))

    step_cols = jnp.pad(weight_step[0].T, ((0, 0), (0, 128 - heads)))
    cols = jnp.concatenate([weight_main[0].reshape(model_width, -1), step_cols], axis=1)

    lanes = ((0, 0), (0, 128 - heads))
    by_head = jnp.pad(
        jnp.stack([step_bias[0], decay_log[0], skip_gain[0]]), ((0, 5), (0, 128 - heads))
    )
    steps = jnp.pad(saved_step[0].astype(F32).T, lanes)
    taps_main = conv_main[0]
    taps_state = conv_state[0].reshape(conv_state.shape[1], -1)
    state_width = taps_state.shape[1]
    residual_shapes = (
        jax.ShapeDtypeStruct((9, length, channels), F32),
        jax.ShapeDtypeStruct((2, length, heads * length), F32),
        jax.ShapeDtypeStruct((length, heads * length), BF16),
        jax.ShapeDtypeStruct((heads * length, channels), BF16),
        jax.ShapeDtypeStruct((2, length, state_width // 2), BF16),
        jax.ShapeDtypeStruct((length, 128), F32),
    )
    residuals = pl.pallas_call(
        lambda *refs: forward_kernel(heads, *refs),
        out_shape=residual_shapes,
        in_specs=whole(8),
        out_specs=whole(6),
        compiler_params=kernel_params(),
        name="forward_residuals",
    )(
        saved_main[0, :, 0],
        saved_main[0, :, 1],
        saved_state[0].reshape(length, -1),
        steps,
        taps_main,
        taps_state,
        by_head,
        norm_gain,
    )
    residuals = tuple(residuals) + (taps_main, taps_state, by_head)
    message = jax.ShapeDtypeStruct((length, width + state_width), BF16)
    slice_out = jax.ShapeDtypeStruct((length, channels), BF16)
    carry_shape = jax.ShapeDtypeStruct((length, width), BF16)
    main_shape = jax.ShapeDtypeStruct((length, cols.shape[1]), BF16)
    state_shape = jax.ShapeDtypeStruct((length, state_width), BF16)
    hbm = pl.BlockSpec(memory_space=pl.ANY)

    incoming[1:] = lax.optimization_barrier(tuple(incoming[1:]))
    weight_late = after(weight_out[0], incoming[1])
    own_half = []
    for hop in range(chunks):
        chunk = (me + hop) % chunks
        piece = lax.dynamic_slice(
            weight_late, (core * half_rows, chunk * width), (half_rows, width)
        )
        pairs = section_pairs(sections, chunks, sections - 2, sections - 1, hop)
        own_half.append(lax.ppermute(piece, place, pairs))

    cols_scratch = [
        pltpu.VMEM((chunks, width, cols.shape[1]), BF16),
        pltpu.SemaphoreType.DMA((chunks,)),
    ]
    parts = pl.pallas_call(
        lambda *refs: first_kernel(heads, chunks, *refs),
        out_shape=(message,) * chunks,
        in_specs=whole(chunks) + [hbm] + whole(9) + [hbm],
        out_specs=whole(chunks),
        scratch_shapes=cols_scratch
        + [pltpu.VMEM((channels, model_width), BF16), pltpu.SemaphoreType.DMA],
        compiler_params=kernel_params(),
        name="section_first",
    )(*incoming, weight_out[0], *residuals, cols)
    exchanged = [parts[0]]
    for hop in range(1, chunks):
        pairs = section_pairs(sections, chunks, sections - 1, sections - 1, hop)
        exchanged.append(lax.ppermute(parts[hop], place, pairs))

    state_cols = weight_state[0].reshape(model_width, -1).T
    state_late = after(state_cols, parts[0])
    pieces = []
    for hop in range(chunks):
        chunk = (me + hop) % chunks
        piece = lax.dynamic_slice(
            state_late,
            (0, chunk * width + core * half_width),
            (state_cols.shape[0], half_width),
        )
        if hop:
            pairs = [(index, (index + hop) % chunks) for index in range(chunks)]
            piece = lax.ppermute(piece, "tensor", pairs)
        pieces.append(piece)
    own_half = jnp.concatenate(own_half, axis=0)
    other_half = lax.ppermute(own_half, "dp", SWAP)
    state_own = jnp.stack(pieces)
    state_other = lax.ppermute(state_own, "dp", SWAP)
    lower = jnp.where(core == 0, state_own, state_other)
    upper = jnp.where(core == 0, state_other, state_own)
    order = (me - jnp.arange(chunks)) % chunks
    state_rows = by_member(jnp.concatenate([lower, upper], axis=2), order)

    def carry_call(last, *operands):
        scratch = []
        if not last:
            scratch = [
                pltpu.VMEM(own_half.shape, BF16),
                pltpu.VMEM(own_half.shape, BF16),
                pltpu.SemaphoreType.DMA((2,)),
            ]
        return pl.pallas_call(
            lambda *refs: carry_kernel(chunks, last, *refs),
            out_shape=(carry_shape,) + (() if last else (slice_out,) * chunks),
            in_specs=whole(chunks + 1) + ([] if last else [hbm] * 2),
            out_specs=whole(1 if last else 1 + chunks),
            scratch_shapes=scratch,
            compiler_params=kernel_params(),
            name="carry_last" if last else "carry_next",
        )(*operands)

    def pass_back(messages, active):
        moved = []
        for hop in range(chunks):
            pairs = section_pairs(sections, chunks, active, active - 1, chunks - hop)
            moved.append(lax.ppermute(messages[hop], place, pairs))
        return moved

    carry, *messages = carry_call(False, *exchanged, state_rows, own_half, other_half)
    result = carry
    incoming = pass_back(messages, sections - 1)

    kept = None
    composed = None
    for active in range(sections - 2, -1, -1):
        main, state = pl.pallas_call(
            lambda *refs: next_kernel(heads, chunks, *refs),
            out_shape=(main_shape, state_shape),
            in_specs=whole(chunks + 9),
            out_specs=whole(2),
            compiler_params=kernel_params(),
            name="section_next",
        )(*incoming, *residuals)
        if kept is None:
            kept = (main, state)
        else:
            kept = tuple(
                jnp.where(section == active, new, old) for new, old in zip((main, state), kept)
            )
        if active == 0:
            break
        if composed is None:
            depth = model_width // 8
            total = chunks * half_rows
            late_rows = after(tuple(gathered_rows), main)
            main_map, state_map = pl.pallas_call(
                lambda *refs: compose_kernel(chunks, *refs),
                grid=(8,),
                out_shape=(
                    jax.ShapeDtypeStruct((total, cols.shape[1]), BF16),
                    jax.ShapeDtypeStruct((state_cols.shape[0], total), BF16),
                ),
                in_specs=[pl.BlockSpec((half_rows, depth), lambda step: (0, step))] * chunks
                + [
                    pl.BlockSpec((depth, cols.shape[1]), lambda step: (step, 0)),
                    pl.BlockSpec((state_cols.shape[0], depth), lambda step: (0, step)),
                ],
                out_specs=[
                    pl.BlockSpec((total, cols.shape[1]), lambda step: (0, 0)),
                    pl.BlockSpec((state_cols.shape[0], total), lambda step: (0, 0)),
                ],
                scratch_shapes=[
                    pltpu.VMEM((total, cols.shape[1]), F32),
                    pltpu.VMEM((state_cols.shape[0], total), F32),
                ],
                compiler_params=kernel_params(),
                name="compose_weights",
            )(*late_rows, cols, state_cols)
            shared = [state_map]
            for hop in range(1, chunks):
                pairs = []
                for target in range(1, sections - 1):
                    pairs += section_pairs(sections, chunks, target, target, hop)
                moved = lax.ppermute(state_map, place, pairs)
                shared.append(jnp.roll(moved, hop * half_rows, axis=1))
            state_map = by_member(jnp.stack(shared), order)
            composed = (
                main_map,
                lax.ppermute(main_map, "dp", SWAP),
                state_map,
                lax.ppermute(state_map, "dp", SWAP),
            )
        messages = pl.pallas_call(
            lambda *refs: send_kernel(chunks, *refs),
            out_shape=(slice_out,) * chunks,
            in_specs=whole(6),
            out_specs=whole(chunks),
            compiler_params=kernel_params(),
            name="send_back",
        )(main, state, *composed)
        incoming = pass_back(messages, active)

    parts = pl.pallas_call(
        lambda *refs: project_kernel(chunks, *refs),
        out_shape=(message,) * chunks,
        in_specs=whole(2) + [hbm],
        out_specs=whole(chunks),
        scratch_shapes=cols_scratch,
        compiler_params=kernel_params(),
        name="project",
    )(*kept, cols)
    exchanged = [parts[0]]
    for hop in range(1, chunks):
        pairs = []
        for source in range(sections - 1):
            pairs += section_pairs(sections, chunks, source, source, hop)
        exchanged.append(lax.ppermute(parts[hop], place, pairs))
    carry = carry_call(True, *exchanged, state_rows)[0]
    return jnp.where(section == sections - 1, result, carry)[None]


def solution(mesh):
    narrow = mesh.shape["tensor"] == GROUP_SPAN
    return jax.shard_map(
        relay_body if narrow else wide_body,
        mesh=mesh,
        in_specs=(
            P("pipe", None, None, "tensor"),
            P("pipe", None, None, "tensor"),
            P("pipe", "tensor", None),
            P("pipe", "tensor", None),
            P("pipe", None, "tensor"),
            P("pipe", None, None, None),
            P("pipe", "tensor"),
            P("pipe", "tensor"),
            P("pipe", "tensor"),
            P("pipe", "tensor"),
            P("pipe", "dp", None, "tensor"),
            P("pipe", "dp", None, None),
            P("pipe", "tensor", "dp"),
            P("dp", "tensor"),
        ),
        out_specs=P("pipe", "dp", "tensor"),
        check_vma=False,
    )
```

```python
import jax
import jax.numpy as jnp
from jax import lax
from jax.experimental import pallas as pl
from jax.experimental.pallas import tpu as pltpu
from jax.sharding import PartitionSpec as P

NSTATE = 128
GROUP_SPAN = 4
STRETCH = 128


EPSILON = 1e-05
HIGHEST = lax.Precision.HIGHEST


def from_partner(value, axis, bit):
    mask = 2**bit
    pairs = [(source, source ^ mask) for source in range(lax.axis_size(axis))]
    return lax.ppermute(value, axis, pairs)


def passed_along(value, axis, steps):
    count = lax.axis_size(axis)
    leading, last = (max(0, -steps), min(count, count - steps))
    return lax.ppermute(value, axis, [(source, source + steps) for source in range(leading, last)])


def causal_conv(signal, kernel):
    taps = kernel.shape[0]
    length = signal.shape[0]
    padded = jnp.pad(signal, ((taps - 1, 0), (0, 0)))
    summed = kernel[0] * padded[0:length]
    for offset in range(1, taps):
        summed = summed + kernel[offset] * padded[offset : offset + length]
    return summed


def state_space(values, step_sizes, decay_rates, inputs, readout):
    length, head_count, head_size = values.shape
    blocks = length // STRETCH
    state_width = inputs.shape[1]
    decays = (step_sizes * decay_rates[:, None]).reshape(head_count, blocks, STRETCH)
    running = jnp.cumsum(decays, axis=2)
    scaled = (values * step_sizes.T[:, :, None]).reshape(blocks, STRETCH, head_count, head_size)
    inputs_blocked = inputs.reshape(blocks, STRETCH, state_width)
    readout_blocked = readout.reshape(blocks, STRETCH, state_width)
    scores = jnp.einsum("cin,cjn->cij", readout_blocked, inputs_blocked, precision=HIGHEST)
    position = jnp.arange(STRETCH)
    causal = position[:, None] >= position[None, :]
    differ = running[:, :, :, None] - running[:, :, None, :]
    weights = jnp.where(causal, jnp.exp(jnp.where(causal, differ, 0.0)), 0.0) * scores[None]
    within = jnp.einsum("hcij,cjhp->cihp", weights, scaled, precision=HIGHEST)
    tail_decay = jnp.exp(running[:, :, -1:] - running)
    weighted = scaled * jnp.transpose(tail_decay, (1, 2, 0))[:, :, :, None]
    block_sums = jnp.einsum("cjhp,cjn->chpn", weighted, inputs_blocked, precision=HIGHEST)
    shrinks = jnp.exp(running[:, :, -1]).T

    def advance(carried, item):
        newest, shrink = item
        return (carried * shrink[:, None, None] + newest, carried)

    anchor = jnp.zeros((head_count, head_size, state_width), jnp.float32)
    _, entering = lax.scan(advance, anchor, (block_sums, shrinks))
    across = jnp.einsum("cin,chpn->cihp", readout_blocked, entering, precision=HIGHEST)
    across = across * jnp.transpose(jnp.exp(running), (1, 2, 0))[:, :, :, None]
    return (within + across).reshape(length, head_count, head_size)


def mamba_mixer(
    main_proj,
    state_proj,
    step_proj,
    conv_main,
    conv_state,
    step_bias,
    decay_log,
    skip_gain,
    norm_gain,
):
    length = main_proj.shape[0]
    head_count = step_proj.shape[0]
    gating = main_proj[:, 0]
    mixed_in = jax.nn.silu(causal_conv(main_proj[:, 1], conv_main))
    flat_state = state_proj.reshape(length, -1)
    state_conv = jax.nn.silu(
        causal_conv(flat_state, conv_state.reshape(conv_state.shape[0], -1))
    ).reshape(length, 2, -1)
    step_sizes = jax.nn.softplus(step_proj + step_bias[:, None])
    decay_rates = -jnp.exp(decay_log)
    values = mixed_in.reshape(length, head_count, -1)
    scanned = state_space(values, step_sizes, decay_rates, state_conv[:, 0], state_conv[:, 1])
    scanned = scanned + skip_gain[None, :, None] * values
    gated = scanned.reshape(length, -1) * jax.nn.silu(gating)
    inverse = lax.rsqrt(jnp.mean(gated * gated, axis=1, keepdims=True) + EPSILON)
    return gated * inverse * norm_gain


def wide_body(
    weight_main,
    weight_state,
    weight_step,
    weight_out,
    conv_main,
    conv_state,
    step_bias,
    decay_log,
    skip_gain,
    norm_gain,
    saved_main,
    saved_state,
    saved_step,
    output_grad,
):
    sections = lax.axis_size("pipe")
    section = lax.axis_index("pipe")
    tensor_index = lax.axis_index("tensor")
    member = tensor_index % GROUP_SPAN
    group = tensor_index // GROUP_SPAN
    span_bits = GROUP_SPAN.bit_length() - 1
    length = saved_main.shape[1]
    col_count = output_grad.shape[1]
    model_width = weight_out.shape[2]
    main_cols = weight_main[0].reshape(model_width, -1)
    state_cols = weight_state[0].reshape(model_width, -1)
    step_rows = weight_step[0]
    out_rows = weight_out[0]
    state_group = lax.dynamic_slice_in_dim(saved_state[0], group * NSTATE, NSTATE, 2)
    conv_group = lax.dynamic_slice_in_dim(conv_state[0], group * NSTATE, NSTATE, 2)

    def local_mixer(first_in, second_in, third_in):
        return mamba_mixer(
            first_in,
            second_in,
            third_in,
            conv_main[0],
            conv_group,
            step_bias[0],
            decay_log[0],
            skip_gain[0],
            norm_gain[0],
        )

    _, pullback = jax.vjp(
        local_mixer,
        saved_main[0].astype(jnp.float32),
        state_group.astype(jnp.float32),
        saved_step[0].astype(jnp.float32),
    )
    result = jnp.zeros((length, col_count), jnp.bfloat16)
    incoming = output_grad
    for moment in range(sections):
        back_grad_main, back_grad_state, back_grad_step = pullback(
            lax.dot_general(
                lax.all_gather(incoming, "tensor", axis=1, tiled=True),
                out_rows,
                (((1,), (1,)), ((), ())),
                preferred_element_type=jnp.float32,
            )
        )
        kept = back_grad_state
        for bit in range(span_bits - 1, -1, -1):
            half = kept.shape[2] // 2
            lower = kept[:, :, :half]
            upper = kept[:, :, half:]
            high = member // 2**bit % 2 == 1
            own = jnp.where(high, upper, lower)
            other = jnp.where(high, lower, upper)
            kept = own + from_partner(other, "tensor", bit)
        grad_main = back_grad_main.astype(jnp.bfloat16).reshape(length, -1)
        grad_state = kept.astype(jnp.bfloat16).reshape(length, -1)
        grad_step = back_grad_step.astype(jnp.bfloat16)
        summed = lax.dot_general(
            main_cols, grad_main, (((1,), (1,)), ((), ())), preferred_element_type=jnp.float32
        )
        summed = summed + lax.dot_general(
            state_cols, grad_state, (((1,), (1,)), ((), ())), preferred_element_type=jnp.float32
        )
        owned = lax.psum_scatter(
            summed
            + lax.dot_general(
                step_rows, grad_step, (((0,), (0,)), ((), ())), preferred_element_type=jnp.float32
            ),
            "tensor",
            scatter_dimension=0,
            tiled=True,
        ).T.astype(jnp.bfloat16)
        result = jnp.where(section == sections - 1 - moment, owned, result)
        if moment + 1 < sections:
            incoming = passed_along(owned, "pipe", -1)
    return result[None]


BF16 = jnp.bfloat16
F32 = jnp.float32
SPACE = pltpu.VMEM
VMEM_BYTES = 48 * 2**20


def dot_nt(left, right, **options):
    return lax.dot_general(
        left, right, (((1,), (1,)), ((), ())), preferred_element_type=F32, **options
    )


def dot_tn(left, right):
    return lax.dot_general(left, right, (((0,), (0,)), ((), ())), preferred_element_type=F32)


def dot_nn(left, right, **options):
    return jnp.dot(left, right, preferred_element_type=F32, **options)


def iota(shape, dim):
    return lax.broadcasted_iota(jnp.int32, shape, dim)


def head_lanes(shape, head, size):
    lane = iota(shape, 1)
    return (lane >= head * size) & (lane < (head + 1) * size)


def conv_taps(signal, taps):
    count = taps.shape[0]
    row = iota(signal.shape, 0)
    total = taps[count - 1 : count] * signal
    for back in range(1, count):
        moved = jnp.where(row >= back, pltpu.roll(signal, back, 0), 0.0)
        total = total + taps[count - 1 - back : count - back] * moved
    return total


def conv_taps_back(grad, taps):
    count = taps.shape[0]
    length = grad.shape[0]
    row = iota(grad.shape, 0)
    total = taps[count - 1 : count] * grad
    for ahead in range(1, count):
        moved = jnp.where(row < length - ahead, pltpu.roll(grad, length - ahead, 0), 0.0)
        total = total + taps[count - 1 - ahead : count - ahead] * moved
    return total


def silu_and_slope(value):
    gate = jax.nn.sigmoid(value)
    return value * gate, gate * (1.0 + value * (1.0 - gate))


def forward_kernel(
    heads,
    gate_ref,
    mixer_ref,
    state_ref,
    step_ref,
    taps_main_ref,
    taps_state_ref,
    heads_ref,
    gain_ref,
    maps_ref,
    decay_ref,
    decayed_ref,
    values_ref,
    state_out_ref,
    slope_ref,
):
    length, channels = gate_ref.shape
    size = channels // heads
    states = state_ref.shape[1] // 2
    gate, gate_slope = silu_and_slope(gate_ref[...].astype(F32))
    value, value_slope = silu_and_slope(
        conv_taps(mixer_ref[...].astype(F32), taps_main_ref[...])
    )
    state, state_slope = silu_and_slope(
        conv_taps(state_ref[...].astype(F32), taps_state_ref[...])
    )
    inputs = state[:, :states]
    readout = state[:, states:]
    raw_step = step_ref[...] + heads_ref[0:1]
    step = jnp.maximum(raw_step, 0.0) + jnp.log1p(jnp.exp(-jnp.abs(raw_step)))
    slope_ref[...] = jax.nn.sigmoid(raw_step)
    rate = -jnp.exp(heads_ref[1:2])
    square = (length, length)
    later = iota(square, 0) >= iota(square, 1)
    earlier = iota(square, 0) <= iota(square, 1)
    running = dot_nn(later.astype(F32), step * rate, precision=HIGHEST)
    running_row = running.T
    scores = dot_nt(readout, inputs, precision=HIGHEST)
    scores_back = dot_nt(inputs, readout, precision=HIGHEST)
    wide = (length, channels)
    step_wide = jnp.zeros(wide, F32)
    skip_wide = jnp.zeros(wide, F32)
    for head in range(heads):
        lanes = head_lanes(wide, head, size)
        step_wide = jnp.where(lanes, step[:, head : head + 1], step_wide)
        skip_wide = jnp.where(lanes, heads_ref[2:3, head : head + 1], skip_wide)
    scaled = value * step_wide
    output = skip_wide * value
    for head in range(heads):
        lanes = head_lanes(wide, head, size)
        columns = pl.ds(head * length, length)
        column = running[:, head : head + 1]
        row = running_row[head : head + 1, :]
        decay = jnp.where(later, jnp.exp(jnp.where(later, column - row, 0.0)), 0.0)
        back = jnp.where(earlier, jnp.exp(jnp.where(earlier, row - column, 0.0)), 0.0)
        weights = decay * scores
        own = jnp.where(lanes, scaled, 0.0)
        output = output + dot_nn(weights, own, precision=HIGHEST)
        decay_ref[0, :, columns] = decay
        decay_ref[1, :, columns] = weights
        decayed_ref[:, columns] = (back * scores_back).astype(BF16)
        values_ref[columns, :] = own.astype(BF16)
    gated = output * gate
    inverse = lax.rsqrt(jnp.mean(gated * gated, axis=1, keepdims=True) + EPSILON)
    gain = gain_ref[...]
    normal = gated * inverse
    maps_ref[0] = gain * inverse
    maps_ref[1] = normal * inverse
    maps_ref[2] = gain * normal * (1.0 / channels)
    maps_ref[3] = gate
    maps_ref[4] = output * gate_slope
    maps_ref[5] = skip_wide * value_slope
    maps_ref[6] = step_wide * value_slope
    maps_ref[7] = value
    maps_ref[8] = state_slope
    state_out_ref[0] = inputs.astype(BF16)
    state_out_ref[1] = readout.astype(BF16)


def mixer_back(heads, dnormed, residuals):
    (
        maps_ref,
        decay_ref,
        decayed_ref,
        values_ref,
        state_ref,
        slope_ref,
        taps_main_ref,
        taps_state_ref,
        heads_ref,
    ) = residuals
    length, channels = dnormed.shape
    size = channels // heads
    shared = jnp.sum(dnormed * maps_ref[2], axis=1, keepdims=True)
    d_gated = dnormed * maps_ref[0] - maps_ref[1] * shared
    d_output = d_gated * maps_ref[3]
    d_gate = d_gated * maps_ref[4]
    by_head = jnp.concatenate(
        [
            jnp.where(head_lanes(d_output.shape, head, size), d_output, 0.0).astype(BF16)
            for head in range(heads)
        ],
        axis=0,
    )
    d_scaled = dot_nn(decayed_ref[...], by_head)
    d_weights = dot_nt(d_output.astype(BF16), values_ref[...])
    d_decayed = d_weights * decay_ref[0]
    d_scores = d_decayed[:, :length]
    for head in range(1, heads):
        d_scores = d_scores + d_decayed[:, head * length : (head + 1) * length]
    d_exponent = d_weights * decay_ref[1]
    square = (length, length)
    onward = (iota(square, 0) <= iota(square, 1)).astype(BF16)
    spanning = dot_nn(onward, d_exponent.astype(BF16))
    row = iota(spanning.shape, 0)
    source = iota(spanning.shape, 1) % length
    spanning = jnp.where(source < row, spanning, 0.0)
    lane = iota((channels, 128), 1)
    of_channel = (iota((channels, 128), 0) // size == lane).astype(BF16)
    of_source = (
        iota((heads * length, 128), 0) // length == iota((heads * length, 128), 1)
    ).astype(BF16)
    rate = -jnp.exp(heads_ref[1:2])
    d_step = dot_nn((d_scaled * maps_ref[7]).astype(BF16), of_channel)
    d_step = d_step + rate * dot_nn(spanning.astype(BF16), of_source)
    d_step = d_step * slope_ref[...]
    rounded = d_scores.astype(BF16)
    d_readout = dot_nn(rounded, state_ref[0])
    d_inputs = dot_tn(rounded, state_ref[1])
    d_state = jnp.concatenate([d_inputs, d_readout], axis=1) * maps_ref[8]
    d_mixer = d_output * maps_ref[5] + d_scaled * maps_ref[6]
    main = jnp.concatenate(
        [
            d_gate.astype(BF16),
            conv_taps_back(d_mixer, taps_main_ref[...]).astype(BF16),
            d_step.astype(BF16),
        ],
        axis=1,
    )
    return main, conv_taps_back(d_state, taps_state_ref[...]).astype(BF16)


def picked_members(chunks, state):
    me = lax.axis_index("tensor")
    states = state.shape[1] // 2
    share = states // chunks
    shape = (state.shape[1], 128)
    row = iota(shape, 0)
    lane = iota(shape, 1)
    source = jnp.where(lane < share, lane, lane + states - share)
    pieces = []
    for hop in range(chunks):
        member = lax.rem(me + hop, chunks)
        picked = (row == source + member * share) & (lane < 2 * share)
        pieces.append(dot_nn(state, picked.astype(BF16)).astype(BF16))
    return pieces


def first_kernel(heads, chunks, *refs):
    incoming, refs = refs[:chunks], refs[chunks:]
    rows_ref, refs = refs[0], refs[1:]
    residuals, refs = refs[:9], refs[9:]
    main_ref, outs = refs[0], refs[1:]
    me = lax.axis_index("tensor")
    width = incoming[0].shape[1]
    dnormed = None
    for hop in range(chunks):
        chunk = lax.rem(me + chunks - hop, chunks)
        term = dot_nt(
            incoming[hop][...], rows_ref[:, pl.ds(pl.multiple_of(chunk * width, width), width)]
        )
        dnormed = term if dnormed is None else dnormed + term
    main, state = mixer_back(heads, dnormed, residuals)
    main_ref[...] = main
    for out, piece in zip(outs, picked_members(chunks, state)):
        out[...] = piece


def next_kernel(heads, chunks, active, *refs):
    incoming, refs = refs[:chunks], refs[chunks:]
    residuals, refs = refs[:9], refs[9:]
    channels = residuals[0].shape[2]
    dnormed = incoming[0][:, :channels].astype(F32)
    for hop in range(1, chunks):
        dnormed = dnormed + incoming[hop][:, :channels].astype(F32)
    states = residuals[4].shape[2] * 2
    joined = incoming[0].shape[1] > channels
    if joined:
        place = slice(channels, channels + states)
        state = incoming[0][:, place].astype(F32)
        for hop in range(1, chunks):
            state = state + incoming[hop][:, place].astype(F32)
        share = states // chunks
        pieces = picked_members(chunks, state.astype(BF16))
        place = slice(channels + states, channels + states + channels // 2)
        for hop in range(chunks):
            piece = pieces[hop][:, :share]
            halves = [incoming[hop][start : start + share, place] for start in (0, share)]
            dnormed = dnormed + jnp.concatenate([dot_nn(piece, half) for half in halves], axis=1)
    main, state = mixer_back(heads, dnormed, residuals)
    if joined:
        done = lax.axis_index("pipe") > active
        main = jnp.where(done, refs[0][...], main)
        state = jnp.where(done, refs[1][...], state)
        refs = refs[2:]
    refs[0][...] = main
    refs[1][...] = state
    if active == 0:
        for ref, piece in zip(refs[2:], picked_members(chunks, state)):
            ref[...] = piece


def sum_pieces(pieces, width):
    total = pieces[0][...].astype(F32)
    for piece in pieces[1:]:
        total = total + piece[...].astype(F32)
    return total.astype(BF16)[:, :width]


def project_kernel(chunks, *refs):
    main_ref, refs = refs[0], refs[1:]
    pieces, refs = refs[:chunks], refs[chunks:]
    state_cols_ref, cols_ref, refs = refs[0], refs[1], refs[2:]
    outs, refs = refs[:chunks], refs[chunks:]
    cols, sems = refs
    me = lax.axis_index("tensor")
    width = cols.shape[1]
    places = []
    copies = []
    for hop in range(chunks):
        place = pl.ds(pl.multiple_of(lax.rem(me + hop, chunks) * width, width), width)
        copy = pltpu.make_async_copy(cols_ref.at[place, :], cols.at[hop], sems.at[hop])
        copy.start()
        places.append(place)
        copies.append(copy)
    main = main_ref[...]
    state = sum_pieces(pieces, pieces[0].shape[1])
    state = state[:, : state_cols_ref.shape[0]]
    for hop in range(chunks):
        product = dot_nn(state, state_cols_ref[:, places[hop]])
        copies[hop].wait()
        outs[hop][...] = (product + dot_nt(main, cols[hop])).astype(BF16)


def compose_kernel(rows_ref, cols_ref, main_ref, main_sum):
    step = pl.program_id(0)
    main = dot_nn(rows_ref[...], cols_ref[...])

    @pl.when(step == 0)
    def _():
        main_sum[...] = main

    @pl.when(step > 0)
    def _():
        main_sum[...] += main

    @pl.when(step == pl.num_programs(0) - 1)
    def _():
        main_ref[...] = main_sum[...].astype(BF16)


def compose_last_kernel(half, *refs):
    rows, refs = refs[:half], refs[half:]
    done, refs = refs[: half - 1], refs[half - 1 :]
    cols_ref, state_ref, joint_ref, main_sum, maps_sum = refs
    step = pl.program_id(0)
    size = rows[0].shape[0]
    map_width = main_sum.shape[1]

    @pl.when(step == 0)
    def _():
        main_sum[...] = jnp.zeros_like(main_sum)
        maps_sum[...] = jnp.zeros_like(maps_sum)

    main_sum[...] += dot_nn(rows[-1][...], cols_ref[...])
    for hop in range(half):
        maps_sum[:, hop * size : (hop + 1) * size] += dot_nt(state_ref[...], rows[hop][...])

    @pl.when(step == pl.num_programs(0) - 1)
    def _():
        joint_ref[...] = jnp.zeros_like(joint_ref)
        for hop in range(half - 1):
            joint_ref[:size, hop * map_width : (hop + 1) * map_width] = done[hop][...]
        joint_ref[:size, (half - 1) * map_width :] = main_sum[...].astype(BF16)
        joint_ref[size:, : half * size] = maps_sum[...].astype(BF16)


def by_hop(chunks, own, other):
    core = lax.axis_index("dp")
    half = chunks // 2
    return [
        jnp.where((core == 0) == (hop < half), own[hop % half], other[hop % half])
        for hop in range(chunks)
    ]


def send_kernel(chunks, main_ref, state_ref, *refs):
    sources, refs = refs[:2], refs[2:]
    outs, held, sems = refs[:chunks], refs[chunks:-1], refs[-1]
    half = chunks // 2
    map_width = main_ref.shape[1]
    states = state_ref.shape[1]
    share = states // chunks
    size = held[0].shape[0] - share
    copies = [
        pltpu.make_async_copy(source, place, sems.at[index])
        for index, (source, place) in enumerate(zip(sources, held))
    ]
    for copy in copies:
        copy.start()
    main = main_ref[...]
    for copy in copies:
        copy.wait()

    def terms(joint):
        return [
            dot_nt(main, joint[:size, hop * map_width : (hop + 1) * map_width])
            for hop in range(half)
        ]

    def maps(joint):
        return [joint[size:, hop * size : (hop + 1) * size] for hop in range(half)]

    total = by_hop(chunks, terms(held[0]), terms(held[1]))
    kept = by_hop(chunks, maps(held[0]), maps(held[1]))
    for hop in range(chunks):
        outs[hop][:, :size] = total[hop].astype(BF16)
        outs[hop][:, size : size + states] = state_ref[...]
        for part in range(2):
            outs[hop][part * share : (part + 1) * share, size + states :] = kept[hop][
                :, part * (size // 2) : (part + 1) * (size // 2)
            ]


def carry_kernel(chunks, last, *refs):
    parts, refs = refs[:chunks], refs[chunks:]
    if last:
        done_ref, out_ref = refs
    else:
        refs = refs[1:]
    carry = sum_pieces(parts, parts[0].shape[1])
    if last:
        is_last = lax.axis_index("pipe") == lax.axis_size("pipe") - 1
        out_ref[0] = jnp.where(is_last, done_ref[...], carry)
        return
    half = chunks // 2
    own, other = refs[:half], refs[half : 2 * half]
    refs[2 * half][...] = carry

    terms = by_hop(
        chunks,
        [dot_nt(carry, row[...]) for row in own],
        [dot_nt(carry, row[...]) for row in other],
    )
    for hop in range(chunks):
        refs[2 * half + 1 + hop][...] = terms[hop].astype(BF16)


def after(value, dependency):
    return lax.optimization_barrier((value, dependency))[0]


def kernel_params():
    return pltpu.CompilerParams(vmem_limit_bytes=VMEM_BYTES)


def whole(count):
    return [pl.BlockSpec(memory_space=SPACE)] * count


def section_pairs(sections, chunks, source, target, hop):
    return [
        (source * chunks + index, target * chunks + (index + hop) % chunks)
        for index in range(chunks)
    ]


def relay_body(
    weight_main,
    weight_state,
    weight_step,
    weight_out,
    conv_main,
    conv_state,
    step_bias,
    decay_log,
    skip_gain,
    norm_gain,
    saved_main,
    saved_state,
    saved_step,
    output_grad,
):
    sections = lax.axis_size("pipe")
    chunks = lax.axis_size("tensor")
    section = lax.axis_index("pipe")
    me = lax.axis_index("tensor")
    core = lax.axis_index("dp")
    length, width = output_grad.shape
    model_width = weight_out.shape[2]
    heads = step_bias.shape[1]
    channels = weight_out.shape[1]
    place = ("pipe", "tensor")

    def within(active, hop):
        return section_pairs(sections, chunks, active, active, hop)

    half = chunks // 2

    def by_core(sources, hop):
        pairs = []
        for source in sources:
            for index in range(chunks):
                for lane in range(2):
                    target = (index + hop + lane * half) % chunks
                    start = (source * chunks + index) * 2 + lane
                    pairs.append((start, ((source + 1) * chunks + target) * 2 + lane))
        return pairs

    everywhere = ("pipe", "tensor", "dp")

    def swap(value, sections_in):
        pairs = []
        for source in sections_in:
            for start in range(source * chunks * 2, (source + 1) * chunks * 2):
                pairs.append((start, start ^ 1))
        return lax.ppermute(value, everywhere, pairs)

    incoming = [output_grad]
    for hop in range(1, chunks):
        incoming.append(lax.ppermute(output_grad, place, within(sections - 1, hop)))

    rows = [lax.ppermute(weight_out[0], everywhere, by_core(range(sections - 2), 0))]
    lanes = ((0, 0), (0, 128 - heads))
    by_head = jnp.pad(
        jnp.stack([step_bias[0], decay_log[0], skip_gain[0]]), ((0, 5), (0, 128 - heads))
    )
    steps = jnp.pad(saved_step[0].astype(F32).T, lanes)
    chunk_rows = []
    for hop in range(half):
        chunk = (me + hop + core * half) % chunks
        chunk_rows.append(lax.dynamic_slice_in_dim(weight_out[0], chunk * width, width, 1))
    steps, chunk_rows = lax.optimization_barrier((steps, chunk_rows))
    taps_main = conv_main[0]
    taps_state = conv_state[0].reshape(conv_state.shape[1], -1)
    state_width = taps_state.shape[1]
    residual_shapes = (
        jax.ShapeDtypeStruct((9, length, channels), F32),
        jax.ShapeDtypeStruct((2, length, heads * length), F32),
        jax.ShapeDtypeStruct((length, heads * length), BF16),
        jax.ShapeDtypeStruct((heads * length, channels), BF16),
        jax.ShapeDtypeStruct((2, length, state_width // 2), BF16),
        jax.ShapeDtypeStruct((length, 128), F32),
    )
    residuals = pl.pallas_call(
        lambda *refs: forward_kernel(heads, *refs),
        out_shape=residual_shapes,
        in_specs=whole(8),
        out_specs=whole(6),
        compiler_params=kernel_params(),
        name="forward_residuals",
    )(
        saved_main[0, :, 0],
        saved_main[0, :, 1],
        saved_state[0].reshape(length, -1),
        steps,
        taps_main,
        taps_state,
        by_head,
        norm_gain,
    )
    residuals = tuple(residuals) + (taps_main, taps_state, by_head)
    slice_out = jax.ShapeDtypeStruct((length, channels), BF16)
    message = jax.ShapeDtypeStruct((length, width), BF16)
    map_width = 2 * channels + 128
    main_shape = jax.ShapeDtypeStruct((length, map_width), BF16)
    piece_shape = jax.ShapeDtypeStruct((length, 128), BF16)
    hbm = pl.BlockSpec(memory_space=pl.ANY)
    step_cols, main_cols = after((weight_step[0], weight_main[0]), incoming[1])
    step_cols = jnp.pad(step_cols.T, ((0, 0), (0, 128 - heads)))
    main_cols = main_cols.reshape(model_width, -1)
    cols = jnp.concatenate([main_cols, step_cols], axis=1)
    residuals = residuals[:-1] + (after(by_head, main_cols),)

    for hop, piece in enumerate(chunk_rows):
        piece = after(piece, (residuals[0], main_cols, step_cols, *incoming[1:]))
        chunk_rows[hop] = lax.ppermute(piece, everywhere, by_core([sections - 2], hop))
    main, *pieces = pl.pallas_call(
        lambda *refs: first_kernel(heads, chunks, *refs),
        out_shape=(main_shape,) + (piece_shape,) * chunks,
        in_specs=whole(chunks + 10),
        out_specs=whole(1 + chunks),
        compiler_params=kernel_params(),
        name="section_first",
    )(*incoming, weight_out[0], *residuals)

    def share_state(pieces, sections_in):
        shared = [pieces[0]]
        for hop in range(1, chunks):
            pairs = []
            for source in sections_in:
                pairs += within(source, hop)
            shared.append(lax.ppermute(pieces[hop], place, pairs))
        return shared

    def project_call(main, pieces):
        return pl.pallas_call(
            lambda *refs: project_kernel(chunks, *refs),
            out_shape=(message,) * chunks,
            in_specs=whole(2 + chunks) + [hbm],
            out_specs=whole(chunks),
            scratch_shapes=[
                pltpu.VMEM((chunks, width, map_width), BF16),
                pltpu.SemaphoreType.DMA((chunks,)),
            ],
            compiler_params=kernel_params(),
            name="project",
        )(main, *pieces, state_cols, cols)

    pieces = share_state(after(pieces, rows[0]), [sections - 1])
    for hop in range(1, half):
        following = after(weight_out[0], (rows[-1], *chunk_rows, *pieces[1:]))
        rows.append(lax.ppermute(following, everywhere, by_core(range(sections - 2), hop)))
    state_cols = after(weight_state[0], main).reshape(model_width, -1).T
    state_share = state_cols.shape[0]
    chunk_others = [swap(after(held, tuple(pieces[1:])), [sections - 1]) for held in chunk_rows]
    pieces[0] = after(pieces[0], chunk_others)
    parts = project_call(main, pieces)
    exchanged = [parts[0]]
    for hop in range(1, chunks):
        exchanged.append(lax.ppermute(parts[hop], place, within(sections - 1, hop)))

    grid_steps = 4
    depth = model_width // grid_steps
    rows_spec = pl.BlockSpec((channels, depth), lambda step: (0, step))
    cols_spec = pl.BlockSpec((depth, map_width), lambda step: (step, 0))
    map_spec = pl.BlockSpec((channels, map_width), lambda step: (0, 0))
    map_shape = jax.ShapeDtypeStruct((channels, map_width), BF16)
    main_own = [
        pl.pallas_call(
            compose_kernel,
            grid=(grid_steps,),
            out_shape=map_shape,
            in_specs=[rows_spec, cols_spec],
            out_specs=map_spec,
            scratch_shapes=[pltpu.VMEM((channels, map_width), F32)],
            compiler_params=kernel_params(),
            name="compose_weights",
        )(after(held, parts[0]), cols)
        for held in rows[:-1]
    ]


    def pass_back(messages, active):
        moved = []
        for hop in range(chunks):
            pairs = section_pairs(sections, chunks, active, active - 1, chunks - hop)
            moved.append(lax.ppermute(messages[hop], place, pairs))
        return moved

    carry, *messages = pl.pallas_call(
        lambda *refs: carry_kernel(chunks, False, *refs),
        out_shape=(message,) + (slice_out,) * chunks,
        in_specs=whole(2 * chunks + 1),
        out_specs=whole(1 + chunks),
        compiler_params=kernel_params(),
        name="carry_next",
    )(*exchanged, after(by_head, main_own), *chunk_rows, *chunk_others)
    result = carry
    incoming = pass_back(messages, sections - 1)
    joint_shape = jax.ShapeDtypeStruct((channels + state_share, half * map_width), BF16)
    joint = pl.pallas_call(
        lambda *refs: compose_last_kernel(half, *refs),
        grid=(grid_steps,),
        out_shape=joint_shape,
        in_specs=[rows_spec] * half
        + [map_spec] * (half - 1)
        + [cols_spec, pl.BlockSpec((state_share, depth), lambda step: (0, step))],
        out_specs=pl.BlockSpec(joint_shape.shape, lambda step: (0, 0)),
        scratch_shapes=[
            pltpu.VMEM((channels, map_width), F32),
            pltpu.VMEM((state_share, half * channels), F32),
        ],
        compiler_params=kernel_params(),
        name="compose_last",
    )(*rows[:-1], after(rows[-1], messages[0]), *main_own, cols, state_cols)
    residuals = residuals[:-1] + (after(by_head, joint),)

    state_shape = jax.ShapeDtypeStruct((length, state_width), BF16)
    joined = jax.ShapeDtypeStruct((length, channels + state_width + channels // 2), BF16)
    assert 2 * state_share == length

    def next_call(incoming, kept, active):
        count = chunks if active == 0 else 0
        main, state, *pieces = pl.pallas_call(
            lambda *refs: next_kernel(heads, chunks, active, *refs),
            out_shape=(main_shape, state_shape) + (piece_shape,) * count,
            in_specs=whole(chunks + 9 + len(kept)),
            out_specs=whole(2 + count),
            compiler_params=kernel_params(),
            name="section_next",
        )(*incoming, *residuals, *kept)
        return (main, state), pieces

    joint_other = None
    kept = ()
    for active in range(sections - 2, -1, -1):
        kept, pieces = next_call(incoming, kept, active)
        if active == 0:
            break
        if joint_other is None:
            joint_other = swap(after(joint, kept[0]), range(1, sections - 1))
        messages = pl.pallas_call(
            lambda *refs: send_kernel(chunks, *refs),
            out_shape=(joined,) * chunks,
            in_specs=whole(2) + [hbm] * 2,
            out_specs=whole(chunks),
            scratch_shapes=[pltpu.VMEM(joint_shape.shape, BF16)] * 2
            + [pltpu.SemaphoreType.DMA((2,))],
            compiler_params=kernel_params(),
            name="send_back",
        )(*kept, joint, joint_other)
        incoming = pass_back(messages, active)
    pieces = share_state(pieces, range(sections - 1))

    parts = project_call(kept[0], pieces)
    exchanged = [parts[0]]
    for hop in range(1, chunks):
        pairs = []
        for source in range(sections - 1):
            pairs += within(source, hop)
        exchanged.append(lax.ppermute(parts[hop], place, pairs))
    return pl.pallas_call(
        lambda *refs: carry_kernel(chunks, True, *refs),
        out_shape=jax.ShapeDtypeStruct((1, length, width), BF16),
        in_specs=whole(chunks + 1),
        out_specs=pl.BlockSpec(memory_space=SPACE),
        compiler_params=kernel_params(),
        name="carry_last",
    )(*exchanged, result)


def solution(mesh):
    narrow = mesh.shape["tensor"] == GROUP_SPAN
    return jax.shard_map(
        relay_body if narrow else wide_body,
        mesh=mesh,
        in_specs=(
            P("pipe", None, None, "tensor"),
            P("pipe", None, None, "tensor"),
            P("pipe", "tensor", None),
            P("pipe", "tensor", None),
            P("pipe", None, "tensor"),
            P("pipe", None, None, None),
            P("pipe", "tensor"),
            P("pipe", "tensor"),
            P("pipe", "tensor"),
            P("pipe", "tensor"),
            P("pipe", "dp", None, "tensor"),
            P("pipe", "dp", None, None),
            P("pipe", "tensor", "dp"),
            P("dp", "tensor"),
        ),
        out_specs=P("pipe", "dp", "tensor"),
        check_vma=False,
    )
```

```python
import jax
import jax.numpy as jnp
from jax import lax
from jax.experimental import pallas as pl
from jax.experimental.pallas import tpu as pltpu
from jax.sharding import PartitionSpec as P

NSTATE = 128
GROUP_SPAN = 4
STRETCH = 128


EPSILON = 1e-05
HIGHEST = lax.Precision.HIGHEST


def from_partner(value, axis, bit):
    mask = 2**bit
    pairs = [(source, source ^ mask) for source in range(lax.axis_size(axis))]
    return lax.ppermute(value, axis, pairs)


def passed_along(value, axis, steps):
    count = lax.axis_size(axis)
    leading, last = (max(0, -steps), min(count, count - steps))
    return lax.ppermute(value, axis, [(source, source + steps) for source in range(leading, last)])


def causal_conv(signal, kernel):
    taps = kernel.shape[0]
    length = signal.shape[0]
    padded = jnp.pad(signal, ((taps - 1, 0), (0, 0)))
    summed = kernel[0] * padded[0:length]
    for offset in range(1, taps):
        summed = summed + kernel[offset] * padded[offset : offset + length]
    return summed


def state_space(values, step_sizes, decay_rates, inputs, readout):
    length, head_count, head_size = values.shape
    blocks = length // STRETCH
    state_width = inputs.shape[1]
    decays = (step_sizes * decay_rates[:, None]).reshape(head_count, blocks, STRETCH)
    running = jnp.cumsum(decays, axis=2)
    scaled = (values * step_sizes.T[:, :, None]).reshape(blocks, STRETCH, head_count, head_size)
    inputs_blocked = inputs.reshape(blocks, STRETCH, state_width)
    readout_blocked = readout.reshape(blocks, STRETCH, state_width)
    scores = jnp.einsum("cin,cjn->cij", readout_blocked, inputs_blocked, precision=HIGHEST)
    position = jnp.arange(STRETCH)
    causal = position[:, None] >= position[None, :]
    differ = running[:, :, :, None] - running[:, :, None, :]
    weights = jnp.where(causal, jnp.exp(jnp.where(causal, differ, 0.0)), 0.0) * scores[None]
    within = jnp.einsum("hcij,cjhp->cihp", weights, scaled, precision=HIGHEST)
    tail_decay = jnp.exp(running[:, :, -1:] - running)
    weighted = scaled * jnp.transpose(tail_decay, (1, 2, 0))[:, :, :, None]
    block_sums = jnp.einsum("cjhp,cjn->chpn", weighted, inputs_blocked, precision=HIGHEST)
    shrinks = jnp.exp(running[:, :, -1]).T

    def advance(carried, item):
        newest, shrink = item
        return (carried * shrink[:, None, None] + newest, carried)

    anchor = jnp.zeros((head_count, head_size, state_width), jnp.float32)
    _, entering = lax.scan(advance, anchor, (block_sums, shrinks))
    across = jnp.einsum("cin,chpn->cihp", readout_blocked, entering, precision=HIGHEST)
    across = across * jnp.transpose(jnp.exp(running), (1, 2, 0))[:, :, :, None]
    return (within + across).reshape(length, head_count, head_size)


def mamba_mixer(
    main_proj,
    state_proj,
    step_proj,
    conv_main,
    conv_state,
    step_bias,
    decay_log,
    skip_gain,
    norm_gain,
):
    length = main_proj.shape[0]
    head_count = step_proj.shape[0]
    gating = main_proj[:, 0]
    mixed_in = jax.nn.silu(causal_conv(main_proj[:, 1], conv_main))
    flat_state = state_proj.reshape(length, -1)
    state_conv = jax.nn.silu(
        causal_conv(flat_state, conv_state.reshape(conv_state.shape[0], -1))
    ).reshape(length, 2, -1)
    step_sizes = jax.nn.softplus(step_proj + step_bias[:, None])
    decay_rates = -jnp.exp(decay_log)
    values = mixed_in.reshape(length, head_count, -1)
    scanned = state_space(values, step_sizes, decay_rates, state_conv[:, 0], state_conv[:, 1])
    scanned = scanned + skip_gain[None, :, None] * values
    gated = scanned.reshape(length, -1) * jax.nn.silu(gating)
    inverse = lax.rsqrt(jnp.mean(gated * gated, axis=1, keepdims=True) + EPSILON)
    return gated * inverse * norm_gain


def wide_body(
    weight_main,
    weight_state,
    weight_step,
    weight_out,
    conv_main,
    conv_state,
    step_bias,
    decay_log,
    skip_gain,
    norm_gain,
    saved_main,
    saved_state,
    saved_step,
    output_grad,
):
    sections = lax.axis_size("pipe")
    section = lax.axis_index("pipe")
    tensor_index = lax.axis_index("tensor")
    member = tensor_index % GROUP_SPAN
    group = tensor_index // GROUP_SPAN
    span_bits = GROUP_SPAN.bit_length() - 1
    length = saved_main.shape[1]
    col_count = output_grad.shape[1]
    model_width = weight_out.shape[2]
    main_cols = weight_main[0].reshape(model_width, -1)
    state_cols = weight_state[0].reshape(model_width, -1)
    step_rows = weight_step[0]
    out_rows = weight_out[0]
    state_group = lax.dynamic_slice_in_dim(saved_state[0], group * NSTATE, NSTATE, 2)
    conv_group = lax.dynamic_slice_in_dim(conv_state[0], group * NSTATE, NSTATE, 2)

    def local_mixer(first_in, second_in, third_in):
        return mamba_mixer(
            first_in,
            second_in,
            third_in,
            conv_main[0],
            conv_group,
            step_bias[0],
            decay_log[0],
            skip_gain[0],
            norm_gain[0],
        )

    _, pullback = jax.vjp(
        local_mixer,
        saved_main[0].astype(jnp.float32),
        state_group.astype(jnp.float32),
        saved_step[0].astype(jnp.float32),
    )
    result = jnp.zeros((length, col_count), jnp.bfloat16)
    incoming = output_grad
    for moment in range(sections):
        back_grad_main, back_grad_state, back_grad_step = pullback(
            lax.dot_general(
                lax.all_gather(incoming, "tensor", axis=1, tiled=True),
                out_rows,
                (((1,), (1,)), ((), ())),
                preferred_element_type=jnp.float32,
            )
        )
        kept = back_grad_state
        for bit in range(span_bits - 1, -1, -1):
            half = kept.shape[2] // 2
            lower = kept[:, :, :half]
            upper = kept[:, :, half:]
            high = member // 2**bit % 2 == 1
            own = jnp.where(high, upper, lower)
            other = jnp.where(high, lower, upper)
            kept = own + from_partner(other, "tensor", bit)
        grad_main = back_grad_main.astype(jnp.bfloat16).reshape(length, -1)
        grad_state = kept.astype(jnp.bfloat16).reshape(length, -1)
        grad_step = back_grad_step.astype(jnp.bfloat16)
        summed = lax.dot_general(
            main_cols, grad_main, (((1,), (1,)), ((), ())), preferred_element_type=jnp.float32
        )
        summed = summed + lax.dot_general(
            state_cols, grad_state, (((1,), (1,)), ((), ())), preferred_element_type=jnp.float32
        )
        owned = lax.psum_scatter(
            summed
            + lax.dot_general(
                step_rows, grad_step, (((0,), (0,)), ((), ())), preferred_element_type=jnp.float32
            ),
            "tensor",
            scatter_dimension=0,
            tiled=True,
        ).T.astype(jnp.bfloat16)
        result = jnp.where(section == sections - 1 - moment, owned, result)
        if moment + 1 < sections:
            incoming = passed_along(owned, "pipe", -1)
    return result[None]


BF16 = jnp.bfloat16
F32 = jnp.float32
SPACE = pltpu.VMEM
VMEM_BYTES = 48 * 2**20


def dot_nt(left, right, **options):
    return lax.dot_general(
        left, right, (((1,), (1,)), ((), ())), preferred_element_type=F32, **options
    )


def dot_tn(left, right):
    return lax.dot_general(left, right, (((0,), (0,)), ((), ())), preferred_element_type=F32)


def dot_nn(left, right, **options):
    return jnp.dot(left, right, preferred_element_type=F32, **options)


def iota(shape, dim):
    return lax.broadcasted_iota(jnp.int32, shape, dim)


def head_lanes(shape, head, size):
    lane = iota(shape, 1)
    return (lane >= head * size) & (lane < (head + 1) * size)


def conv_taps(signal, taps):
    count = taps.shape[0]
    row = iota(signal.shape, 0)
    total = taps[count - 1 : count] * signal
    for back in range(1, count):
        moved = jnp.where(row >= back, pltpu.roll(signal, back, 0), 0.0)
        total = total + taps[count - 1 - back : count - back] * moved
    return total


def conv_taps_back(grad, taps):
    count = taps.shape[0]
    length = grad.shape[0]
    row = iota(grad.shape, 0)
    total = taps[count - 1 : count] * grad
    for ahead in range(1, count):
        moved = jnp.where(row < length - ahead, pltpu.roll(grad, length - ahead, 0), 0.0)
        total = total + taps[count - 1 - ahead : count - ahead] * moved
    return total


def silu_and_slope(value):
    gate = jax.nn.sigmoid(value)
    return value * gate, gate * (1.0 + value * (1.0 - gate))


def forward_kernel(
    heads,
    gate_ref,
    mixer_ref,
    state_ref,
    step_ref,
    taps_main_ref,
    taps_state_ref,
    heads_ref,
    gain_ref,
    maps_ref,
    decay_ref,
    decayed_ref,
    values_ref,
    state_out_ref,
    slope_ref,
):
    length, channels = gate_ref.shape
    size = channels // heads
    states = state_ref.shape[1] // 2
    gate, gate_slope = silu_and_slope(gate_ref[...].astype(F32))
    value, value_slope = silu_and_slope(
        conv_taps(mixer_ref[...].astype(F32), taps_main_ref[...])
    )
    state, state_slope = silu_and_slope(
        conv_taps(state_ref[...].astype(F32), taps_state_ref[...])
    )
    inputs = state[:, :states]
    readout = state[:, states:]
    raw_step = step_ref[...] + heads_ref[0:1]
    step = jnp.maximum(raw_step, 0.0) + jnp.log1p(jnp.exp(-jnp.abs(raw_step)))
    slope_ref[...] = jax.nn.sigmoid(raw_step)
    rate = -jnp.exp(heads_ref[1:2])
    square = (length, length)
    later = iota(square, 0) >= iota(square, 1)
    earlier = iota(square, 0) <= iota(square, 1)
    running = dot_nn(later.astype(F32), step * rate, precision=HIGHEST)
    running_row = running.T
    scores = dot_nt(readout, inputs, precision=HIGHEST)
    scores_back = dot_nt(inputs, readout, precision=HIGHEST)
    wide = (length, channels)
    step_wide = jnp.zeros(wide, F32)
    skip_wide = jnp.zeros(wide, F32)
    for head in range(heads):
        lanes = head_lanes(wide, head, size)
        step_wide = jnp.where(lanes, step[:, head : head + 1], step_wide)
        skip_wide = jnp.where(lanes, heads_ref[2:3, head : head + 1], skip_wide)
    scaled = value * step_wide
    output = skip_wide * value
    for head in range(heads):
        lanes = head_lanes(wide, head, size)
        columns = pl.ds(head * length, length)
        column = running[:, head : head + 1]
        row = running_row[head : head + 1, :]
        decay = jnp.where(later, jnp.exp(jnp.where(later, column - row, 0.0)), 0.0)
        back = jnp.where(earlier, jnp.exp(jnp.where(earlier, row - column, 0.0)), 0.0)
        weights = decay * scores
        own = jnp.where(lanes, scaled, 0.0)
        output = output + dot_nn(weights, own, precision=HIGHEST)
        decay_ref[0, :, columns] = decay
        decay_ref[1, :, columns] = weights
        decayed_ref[:, columns] = (back * scores_back).astype(BF16)
        values_ref[columns, :] = own.astype(BF16)
    gated = output * gate
    inverse = lax.rsqrt(jnp.mean(gated * gated, axis=1, keepdims=True) + EPSILON)
    gain = gain_ref[...]
    normal = gated * inverse
    maps_ref[0] = gain * inverse
    maps_ref[1] = normal * inverse
    maps_ref[2] = gain * normal * (1.0 / channels)
    maps_ref[3] = gate
    maps_ref[4] = output * gate_slope
    maps_ref[5] = skip_wide * value_slope
    maps_ref[6] = step_wide * value_slope
    maps_ref[7] = value
    maps_ref[8] = state_slope
    state_out_ref[0] = inputs.astype(BF16)
    state_out_ref[1] = readout.astype(BF16)


def mixer_back(heads, dnormed, residuals):
    (
        maps_ref,
        decay_ref,
        decayed_ref,
        values_ref,
        state_ref,
        slope_ref,
        taps_main_ref,
        taps_state_ref,
        heads_ref,
    ) = residuals
    length, channels = dnormed.shape
    size = channels // heads
    shared = jnp.sum(dnormed * maps_ref[2], axis=1, keepdims=True)
    d_gated = dnormed * maps_ref[0] - maps_ref[1] * shared
    d_output = d_gated * maps_ref[3]
    d_gate = d_gated * maps_ref[4]
    by_head = jnp.concatenate(
        [
            jnp.where(head_lanes(d_output.shape, head, size), d_output, 0.0).astype(BF16)
            for head in range(heads)
        ],
        axis=0,
    )
    d_scaled = dot_nn(decayed_ref[...], by_head)
    d_weights = dot_nt(d_output.astype(BF16), values_ref[...])
    d_decayed = d_weights * decay_ref[0]
    d_scores = d_decayed[:, :length]
    for head in range(1, heads):
        d_scores = d_scores + d_decayed[:, head * length : (head + 1) * length]
    d_exponent = d_weights * decay_ref[1]
    square = (length, length)
    onward = (iota(square, 0) <= iota(square, 1)).astype(BF16)
    spanning = dot_nn(onward, d_exponent.astype(BF16))
    row = iota(spanning.shape, 0)
    source = iota(spanning.shape, 1) % length
    spanning = jnp.where(source < row, spanning, 0.0)
    lane = iota((channels, 128), 1)
    of_channel = (iota((channels, 128), 0) // size == lane).astype(BF16)
    of_source = (
        iota((heads * length, 128), 0) // length == iota((heads * length, 128), 1)
    ).astype(BF16)
    rate = -jnp.exp(heads_ref[1:2])
    d_step = dot_nn((d_scaled * maps_ref[7]).astype(BF16), of_channel)
    d_step = d_step + rate * dot_nn(spanning.astype(BF16), of_source)
    d_step = d_step * slope_ref[...]
    rounded = d_scores.astype(BF16)
    d_readout = dot_nn(rounded, state_ref[0])
    d_inputs = dot_tn(rounded, state_ref[1])
    d_state = jnp.concatenate([d_inputs, d_readout], axis=1) * maps_ref[8]
    d_mixer = d_output * maps_ref[5] + d_scaled * maps_ref[6]
    main = jnp.concatenate(
        [
            d_gate.astype(BF16),
            conv_taps_back(d_mixer, taps_main_ref[...]).astype(BF16),
            d_step.astype(BF16),
        ],
        axis=1,
    )
    return main, conv_taps_back(d_state, taps_state_ref[...]).astype(BF16)


def picked_members(chunks, state):
    me = lax.axis_index("tensor")
    states = state.shape[1] // 2
    share = states // chunks
    shape = (state.shape[1], 128)
    row = iota(shape, 0)
    lane = iota(shape, 1)
    source = jnp.where(lane < share, lane, lane + states - share)
    pieces = []
    for hop in range(chunks):
        member = lax.rem(me + hop, chunks)
        picked = (row == source + member * share) & (lane < 2 * share)
        pieces.append(dot_nn(state, picked.astype(BF16)).astype(BF16))
    return pieces


def first_kernel(heads, chunks, *refs):
    incoming, refs = refs[:chunks], refs[chunks:]
    rows_ref, refs = refs[0], refs[1:]
    residuals, refs = refs[:9], refs[9:]
    main_ref, outs = refs[0], refs[1:]
    dnormed = gathered_product(chunks, lax.axis_index("tensor"), incoming, rows_ref)
    main, state = mixer_back(heads, dnormed, residuals)
    main_ref[...] = main
    for out, piece in zip(outs, picked_members(chunks, state)):
        out[...] = piece


def next_kernel(heads, chunks, count, active, *refs):
    incoming, refs = refs[:count], refs[count:]
    residuals, refs = refs[:9], refs[9:]
    channels = residuals[0].shape[2]
    dnormed = incoming[0][:, :channels].astype(F32)
    for message in incoming[1:]:
        dnormed = dnormed + message[:, :channels].astype(F32)
    states = residuals[4].shape[2] * 2
    joined = count > 1
    if joined:
        place = slice(channels, channels + states)
        state = incoming[0][:, place].astype(F32)
        for hop in range(1, chunks):
            state = state + incoming[hop][:, place].astype(F32)
        share = states // chunks
        pieces = picked_members(chunks, state.astype(BF16))
        place = slice(channels + states, channels + states + channels // 2)
        for hop in range(chunks):
            piece = pieces[hop][:, :share]
            halves = [incoming[hop][start : start + share, place] for start in (0, share)]
            dnormed = dnormed + jnp.concatenate([dot_nn(piece, half) for half in halves], axis=1)
    main, state = mixer_back(heads, dnormed, residuals)
    if joined:
        done = lax.axis_index("pipe") > active
        main = jnp.where(done, refs[0][...], main)
        state = jnp.where(done, refs[1][...], state)
        refs = refs[2:]
    refs[0][...] = main
    refs[1][...] = state
    if joined:
        for ref, piece in zip(refs[2:], picked_members(chunks, state)):
            ref[...] = piece


def sum_pieces(pieces, width):
    total = pieces[0][...].astype(F32)
    for piece in pieces[1:]:
        total = total + piece[...].astype(F32)
    return total.astype(BF16)[:, :width]


def project_kernel(chunks, final, *refs):
    main_ref, refs = refs[0], refs[1:]
    pieces, refs = refs[:chunks], refs[chunks:]
    count = chunks if final else 0
    newest, refs = refs[:count], refs[count:]
    state_ref, refs = refs[0], refs[1:]
    if final:
        own_ref, other_ref, refs = refs[0], refs[1], refs[2:]
    cols_ref, refs = refs[0], refs[1:]
    outs, refs = refs[:chunks], refs[chunks:]
    cols, sems = refs
    me = lax.axis_index("tensor")
    width = cols.shape[1]
    places = []
    copies = []
    for hop in range(chunks):
        place = pl.ds(pl.multiple_of(lax.rem(me + hop, chunks) * width, width), width)
        copy = pltpu.make_async_copy(cols_ref.at[place, :], cols.at[hop], sems.at[hop])
        copy.start()
        places.append(place)
        copies.append(copy)
    main = main_ref[...]
    state = [sum_pieces(pieces, pieces[0].shape[1])]
    if final:
        nothing = jnp.zeros_like(state[0])
        first = lax.axis_index("pipe") == 0
        state = [
            jnp.where(first, piece[...], other)
            for piece, other in zip(newest, state + [nothing] * (chunks - 1))
        ]
    share = state_ref.shape[0]
    if final:
        others = jnp.concatenate([piece[:, :share] for piece in state[1:]], axis=1)
    core = lax.axis_index("dp")
    half = chunks // 2
    for hop in range(chunks):
        product = dot_nn(state[0][:, :share], state_ref[:, places[hop]])
        if final:
            chunk = lax.rem(me + hop, chunks)
            mine = chunk // half == core
            place = pl.ds(pl.multiple_of(lax.rem(chunk, half) * width, width), width)
            held = jnp.where(mine, own_ref[:, place], other_ref[:, place])
            product = product + dot_nn(others, held)
        copies[hop].wait()
        outs[hop][...] = (product + dot_nt(main, cols[hop])).astype(BF16)


def compose_kernel(half, *refs):
    rows, refs = refs[:half], refs[half:]
    cols_ref, state_ref, joint_ref, main_sum, maps_sum = refs
    step = pl.program_id(0)
    size = rows[0].shape[0]
    map_width = main_sum.shape[1]
    section = lax.axis_index("pipe")

    @pl.when((section > 0) & (section < lax.axis_size("pipe") - 1))
    def _():
        stacked = jnp.concatenate([row[...] for row in rows], axis=0)
        main = dot_nn(stacked, cols_ref[...])
        maps = dot_nt(state_ref[...], stacked)

        @pl.when(step == 0)
        def _():
            main_sum[...] = main
            maps_sum[...] = maps

        @pl.when(step > 0)
        def _():
            main_sum[...] += main
            maps_sum[...] += maps

        @pl.when(step == pl.num_programs(0) - 1)
        def _():
            for hop in range(half):
                joint_ref[:size, hop * map_width : (hop + 1) * map_width] = main_sum[
                    hop * size : (hop + 1) * size, :
                ].astype(BF16)
            joint_ref[size:, : half * size] = maps_sum[...].astype(BF16)


def by_hop(chunks, own, other):
    core = lax.axis_index("dp")
    half = chunks // 2
    return [
        jnp.where((core == 0) == (hop < half), own[hop % half], other[hop % half])
        for hop in range(chunks)
    ]


def send_kernel(chunks, count, main_ref, state_ref, *refs):
    others, refs = refs[:count], refs[count:]
    sources, refs = refs[:2], refs[2:]
    outs, others_ref, held, sems = refs[:chunks], refs[chunks], refs[chunks + 1 : -1], refs[-1]
    if count:

        @pl.when(lax.axis_index("pipe") == 0)
        def _():
            for index, other in enumerate(others):
                size = other.shape[0]
                others_ref[index * size : (index + 1) * size, :] = other[...]

    half = chunks // 2
    map_width = main_ref.shape[1]
    states = state_ref.shape[1]
    share = states // chunks
    size = held[0].shape[0] - share
    copies = [
        pltpu.make_async_copy(source, place, sems.at[index])
        for index, (source, place) in enumerate(zip(sources, held))
    ]
    for copy in copies:
        copy.start()
    main = main_ref[...]
    for copy in copies:
        copy.wait()

    def terms(joint):
        return [
            dot_nt(main, joint[:size, hop * map_width : (hop + 1) * map_width])
            for hop in range(half)
        ]

    def maps(joint):
        return [joint[size:, hop * size : (hop + 1) * size] for hop in range(half)]

    total = by_hop(chunks, terms(held[0]), terms(held[1]))
    kept = by_hop(chunks, maps(held[0]), maps(held[1]))
    for hop in range(chunks):
        outs[hop][:, :size] = total[hop].astype(BF16)
        outs[hop][:, size : size + states] = state_ref[...]
        for part in range(2):
            outs[hop][part * share : (part + 1) * share, size + states :] = kept[hop][
                :, part * (size // 2) : (part + 1) * (size // 2)
            ]


def carry_kernel(chunks, last, *refs):
    carry = sum_pieces(refs[:chunks], refs[0].shape[1])
    if last:
        done_ref, out_ref = refs[chunks:]
        is_last = lax.axis_index("pipe") == lax.axis_size("pipe") - 1
        out_ref[0] = jnp.where(is_last, done_ref[...], carry)
    else:
        refs[-1][...] = carry


def dnormed_kernel(chunks, *refs):
    incoming, refs = refs[:chunks], refs[chunks:]
    *sources, out_ref = refs
    core = lax.axis_index("dp")
    last = lax.axis_index("pipe") == lax.axis_size("pipe") - 1
    for lane, rows in enumerate(sources):

        @pl.when(last & (core == lane))
        def _():
            product = gathered_product(chunks, lax.axis_index("tensor"), incoming, rows)
            out_ref[...] = product.astype(BF16)


def gathered_product(chunks, me, incoming, rows):
    width = incoming[0].shape[1]
    total = None
    for hop in range(chunks):
        chunk = lax.rem(me + chunks - hop, chunks)
        term = dot_nt(
            incoming[hop][...], rows[:, pl.ds(pl.multiple_of(chunk * width, width), width)]
        )
        total = term if total is None else total + term
    return total


def after(value, dependency):
    return lax.optimization_barrier((value, dependency))[0]


def kernel_params():
    return pltpu.CompilerParams(vmem_limit_bytes=VMEM_BYTES)


def whole(count):
    return [pl.BlockSpec(memory_space=SPACE)] * count


def section_pairs(sections, chunks, source, target, hop):
    return [
        (source * chunks + index, target * chunks + (index + hop) % chunks)
        for index in range(chunks)
    ]


def relay_body(
    weight_main,
    weight_state,
    weight_step,
    weight_out,
    conv_main,
    conv_state,
    step_bias,
    decay_log,
    skip_gain,
    norm_gain,
    saved_main,
    saved_state,
    saved_step,
    output_grad,
):
    sections = lax.axis_size("pipe")
    chunks = lax.axis_size("tensor")
    section = lax.axis_index("pipe")
    me = lax.axis_index("tensor")
    core = lax.axis_index("dp")
    length, width = output_grad.shape
    model_width = weight_out.shape[2]
    heads = step_bias.shape[1]
    channels = weight_out.shape[1]
    place = ("pipe", "tensor")

    def within(active, hop):
        return section_pairs(sections, chunks, active, active, hop)

    half = chunks // 2

    def rows_up(hop):
        pairs = []
        for source in range(sections - 1):
            for index in range(chunks):
                for lane in range(2):
                    move = hop + lane * half
                    if source == sections - 2:
                        if lane != hop:
                            continue
                        move = 0
                    start = (source * chunks + index) * 2 + lane
                    target = (source + 1) * chunks + (index + move) % chunks
                    pairs.append((start, target * 2 + lane))
        return pairs

    everywhere = ("pipe", "tensor", "dp")

    def swap(value, sections_in):
        pairs = []
        for source in sections_in:
            for start in range(source * chunks * 2, (source + 1) * chunks * 2):
                pairs.append((start, start ^ 1))
        return lax.ppermute(value, everywhere, pairs)

    incoming = [output_grad]
    for hop in range(1, chunks):
        incoming.append(lax.ppermute(output_grad, place, within(sections - 1, hop)))

    rows = [lax.ppermute(weight_out[0], everywhere, rows_up(0))]
    lanes = ((0, 0), (0, 128 - heads))
    by_head = jnp.pad(
        jnp.stack([step_bias[0], decay_log[0], skip_gain[0]]), ((0, 5), (0, 128 - heads))
    )
    steps = jnp.pad(saved_step[0].astype(F32).T, lanes)
    taps_main = conv_main[0]
    taps_state = conv_state[0].reshape(conv_state.shape[1], -1)
    state_width = taps_state.shape[1]
    residual_shapes = (
        jax.ShapeDtypeStruct((9, length, channels), F32),
        jax.ShapeDtypeStruct((2, length, heads * length), F32),
        jax.ShapeDtypeStruct((length, heads * length), BF16),
        jax.ShapeDtypeStruct((heads * length, channels), BF16),
        jax.ShapeDtypeStruct((2, length, state_width // 2), BF16),
        jax.ShapeDtypeStruct((length, 128), F32),
    )
    residuals = pl.pallas_call(
        lambda *refs: forward_kernel(heads, *refs),
        out_shape=residual_shapes,
        in_specs=whole(8),
        out_specs=whole(6),
        compiler_params=kernel_params(),
        name="forward_residuals",
    )(
        saved_main[0, :, 0],
        saved_main[0, :, 1],
        saved_state[0].reshape(length, -1),
        steps,
        taps_main,
        taps_state,
        by_head,
        norm_gain,
    )
    residuals = tuple(residuals) + (taps_main, taps_state, by_head)
    slice_out = jax.ShapeDtypeStruct((length, channels), BF16)
    message = jax.ShapeDtypeStruct((length, width), BF16)
    map_width = 2 * channels + 128
    main_shape = jax.ShapeDtypeStruct((length, map_width), BF16)
    piece_shape = jax.ShapeDtypeStruct((length, 128), BF16)
    hbm = pl.BlockSpec(memory_space=pl.ANY)
    step_cols, main_cols = after((weight_step[0], weight_main[0]), incoming[1])
    step_cols = jnp.pad(step_cols.T, ((0, 0), (0, 128 - heads)))
    main_cols = main_cols.reshape(model_width, -1)
    cols = jnp.concatenate([main_cols, step_cols], axis=1)
    residuals = residuals[:-1] + (after(by_head, main_cols),)

    main, *pieces = pl.pallas_call(
        lambda *refs: first_kernel(heads, chunks, *refs),
        out_shape=(main_shape,) + (piece_shape,) * chunks,
        in_specs=whole(chunks + 10),
        out_specs=whole(1 + chunks),
        compiler_params=kernel_params(),
        name="section_first",
    )(*incoming, weight_out[0], *residuals)

    def share_state(pieces, sections_in):
        shared = [pieces[0]]
        for hop in range(1, chunks):
            pairs = []
            for source in sections_in:
                pairs += within(source, hop)
            shared.append(lax.ppermute(pieces[hop], place, pairs))
        return shared

    def project_call(main, pieces, newest=(), others=()):
        return pl.pallas_call(
            lambda *refs: project_kernel(chunks, bool(others), *refs),
            out_shape=(message,) * chunks,
            in_specs=whole(2 + chunks + len(newest) + len(others)) + [hbm],
            out_specs=whole(chunks),
            scratch_shapes=[
                pltpu.VMEM((chunks, width, map_width), BF16),
                pltpu.SemaphoreType.DMA((chunks,)),
            ],
            compiler_params=kernel_params(),
            name="project",
        )(main, *pieces, *newest, state_cols, *others, cols)

    pieces = share_state(pieces, [sections - 1])
    for hop in range(1, half):
        rows.append(lax.ppermute(after(weight_out[0], main), everywhere, rows_up(hop)))
    state_cols = after(weight_state[0], main).reshape(model_width, -1).T
    state_share = state_cols.shape[0]
    parts = project_call(main, pieces)
    exchanged = [parts[0]]
    for hop in range(1, chunks):
        exchanged.append(lax.ppermute(parts[hop], place, within(sections - 1, hop)))

    grid_steps = 4
    depth = model_width // grid_steps
    rows_spec = pl.BlockSpec((channels, depth), lambda step: (0, step))
    cols_spec = pl.BlockSpec((depth, map_width), lambda step: (step, 0))
    def pass_back(messages, active):
        moved = []
        for hop in range(chunks):
            pairs = section_pairs(sections, chunks, active, active - 1, chunks - hop)
            moved.append(lax.ppermute(messages[hop], place, pairs))
        return moved

    result = pl.pallas_call(
        lambda *refs: carry_kernel(chunks, False, *refs),
        out_shape=message,
        in_specs=whole(chunks),
        out_specs=pl.BlockSpec(memory_space=SPACE),
        compiler_params=kernel_params(),
        name="carry_next",
    )(*exchanged)
    exchanged = [result]
    for hop in range(1, chunks):
        exchanged.append(lax.ppermute(result, place, within(sections - 1, hop)))
    dnormed = pl.pallas_call(
        lambda *refs: dnormed_kernel(chunks, *refs),
        out_shape=slice_out,
        in_specs=whole(chunks + 2),
        out_specs=pl.BlockSpec(memory_space=SPACE),
        compiler_params=kernel_params(),
        name="dnormed_back",
    )(*exchanged, *rows)
    pairs = section_pairs(sections, chunks, sections - 1, sections - 2, 0)
    incoming = [lax.ppermute(dnormed, place, pairs)]
    joint_shape = jax.ShapeDtypeStruct((channels + state_share, half * map_width), BF16)
    joint = pl.pallas_call(
        lambda *refs: compose_kernel(half, *refs),
        grid=(grid_steps,),
        out_shape=joint_shape,
        in_specs=[rows_spec] * half
        + [cols_spec, pl.BlockSpec((state_share, depth), lambda step: (0, step))],
        out_specs=pl.BlockSpec(joint_shape.shape, lambda step: (0, 0)),
        scratch_shapes=[
            pltpu.VMEM((half * channels, map_width), F32),
            pltpu.VMEM((state_share, half * channels), F32),
        ],
        compiler_params=kernel_params(),
        name="compose_weights",
    )(*rows[:-1], after(rows[-1], dnormed), cols, state_cols)

    half_cols = lax.dynamic_slice_in_dim(
        after(state_cols, parts[0]), core * (model_width // 2), model_width // 2, 1
    )
    residuals = residuals[:-1] + (after(by_head, (joint, half_cols)),)

    state_shape = jax.ShapeDtypeStruct((length, state_width), BF16)
    joined = jax.ShapeDtypeStruct((length, channels + state_width + channels // 2), BF16)
    assert 2 * state_share == length

    def next_call(incoming, kept, active):
        count = chunks if len(incoming) > 1 else 0
        main, state, *pieces = pl.pallas_call(
            lambda *refs: next_kernel(heads, chunks, len(incoming), active, *refs),
            out_shape=(main_shape, state_shape) + (piece_shape,) * count,
            in_specs=whole(len(incoming) + 9 + len(kept)),
            out_specs=whole(2 + count),
            compiler_params=kernel_params(),
            name="section_next",
        )(*incoming, *residuals, *kept)
        return (main, state), pieces

    joint_other = None
    kept = ()
    summed = None
    for active in range(sections - 2, -1, -1):
        kept, pieces = next_call(incoming, kept, active)
        if active == 0:
            break
        if joint_other is None:
            joint_other = swap(after(joint, kept[0]), range(1, sections - 1))
        state_others = []
        if active == sections - 2:
            late = after(half_cols, kept[0])
            state_others = [
                lax.ppermute(late, place, within(0, chunks - away)) for away in range(1, chunks)
            ]
        count = len(state_others)
        others_shape = jax.ShapeDtypeStruct((count * state_share, model_width // 2), BF16)
        *messages, state_others = pl.pallas_call(
            lambda *refs: send_kernel(chunks, count, *refs),
            out_shape=(joined,) * chunks + (others_shape if count else piece_shape,),
            in_specs=whole(2 + count) + [hbm] * 2,
            out_specs=whole(chunks + 1),
            scratch_shapes=[pltpu.VMEM(joint_shape.shape, BF16)] * 2
            + [pltpu.SemaphoreType.DMA((2,))],
            compiler_params=kernel_params(),
            name="send_back",
        )(*kept, *state_others, joint, joint_other)
        incoming = pass_back(messages, active)
        if active == sections - 2:
            shared = (state_others, swap(state_others, [0]))
        if active == 1:
            summed = share_state(after(pieces, incoming[0]), range(1, sections - 1))

    parts = project_call(kept[0], summed, pieces, shared)
    exchanged = [parts[0]]
    for hop in range(1, chunks):
        pairs = []
        for source in range(sections - 1):
            pairs += within(source, hop)
        exchanged.append(lax.ppermute(parts[hop], place, pairs))
    return pl.pallas_call(
        lambda *refs: carry_kernel(chunks, True, *refs),
        out_shape=jax.ShapeDtypeStruct((1, length, width), BF16),
        in_specs=whole(chunks + 1),
        out_specs=pl.BlockSpec(memory_space=SPACE),
        compiler_params=kernel_params(),
        name="carry_last",
    )(*exchanged, result)


def solution(mesh):
    narrow = mesh.shape["tensor"] == GROUP_SPAN
    return jax.shard_map(
        relay_body if narrow else wide_body,
        mesh=mesh,
        in_specs=(
            P("pipe", None, None, "tensor"),
            P("pipe", None, None, "tensor"),
            P("pipe", "tensor", None),
            P("pipe", "tensor", None),
            P("pipe", None, "tensor"),
            P("pipe", None, None, None),
            P("pipe", "tensor"),
            P("pipe", "tensor"),
            P("pipe", "tensor"),
            P("pipe", "tensor"),
            P("pipe", "dp", None, "tensor"),
            P("pipe", "dp", None, None),
            P("pipe", "tensor", "dp"),
            P("dp", "tensor"),
        ),
        out_specs=P("pipe", "dp", "tensor"),
        check_vma=False,
    )
```

```python
import jax
import jax.numpy as jnp
from jax import lax
from jax.experimental import pallas as pl
from jax.experimental.pallas import tpu as pltpu
from jax.sharding import PartitionSpec as P

NSTATE = 128
GROUP_SPAN = 4
STRETCH = 128


EPSILON = 1e-05
HIGHEST = lax.Precision.HIGHEST


def from_partner(value, axis, bit):
    mask = 2**bit
    pairs = [(source, source ^ mask) for source in range(lax.axis_size(axis))]
    return lax.ppermute(value, axis, pairs)


def passed_along(value, axis, steps):
    count = lax.axis_size(axis)
    leading, last = (max(0, -steps), min(count, count - steps))
    return lax.ppermute(value, axis, [(source, source + steps) for source in range(leading, last)])


def causal_conv(signal, kernel):
    taps = kernel.shape[0]
    length = signal.shape[0]
    padded = jnp.pad(signal, ((taps - 1, 0), (0, 0)))
    summed = kernel[0] * padded[0:length]
    for offset in range(1, taps):
        summed = summed + kernel[offset] * padded[offset : offset + length]
    return summed


def state_space(values, step_sizes, decay_rates, inputs, readout):
    length, head_count, head_size = values.shape
    blocks = length // STRETCH
    state_width = inputs.shape[1]
    decays = (step_sizes * decay_rates[:, None]).reshape(head_count, blocks, STRETCH)
    running = jnp.cumsum(decays, axis=2)
    scaled = (values * step_sizes.T[:, :, None]).reshape(blocks, STRETCH, head_count, head_size)
    inputs_blocked = inputs.reshape(blocks, STRETCH, state_width)
    readout_blocked = readout.reshape(blocks, STRETCH, state_width)
    scores = jnp.einsum("cin,cjn->cij", readout_blocked, inputs_blocked, precision=HIGHEST)
    position = jnp.arange(STRETCH)
    causal = position[:, None] >= position[None, :]
    differ = running[:, :, :, None] - running[:, :, None, :]
    weights = jnp.where(causal, jnp.exp(jnp.where(causal, differ, 0.0)), 0.0) * scores[None]
    within = jnp.einsum("hcij,cjhp->cihp", weights, scaled, precision=HIGHEST)
    tail_decay = jnp.exp(running[:, :, -1:] - running)
    weighted = scaled * jnp.transpose(tail_decay, (1, 2, 0))[:, :, :, None]
    block_sums = jnp.einsum("cjhp,cjn->chpn", weighted, inputs_blocked, precision=HIGHEST)
    shrinks = jnp.exp(running[:, :, -1]).T

    def advance(carried, item):
        newest, shrink = item
        return (carried * shrink[:, None, None] + newest, carried)

    anchor = jnp.zeros((head_count, head_size, state_width), jnp.float32)
    _, entering = lax.scan(advance, anchor, (block_sums, shrinks))
    across = jnp.einsum("cin,chpn->cihp", readout_blocked, entering, precision=HIGHEST)
    across = across * jnp.transpose(jnp.exp(running), (1, 2, 0))[:, :, :, None]
    return (within + across).reshape(length, head_count, head_size)


def mamba_mixer(
    main_proj,
    state_proj,
    step_proj,
    conv_main,
    conv_state,
    step_bias,
    decay_log,
    skip_gain,
    norm_gain,
):
    length = main_proj.shape[0]
    head_count = step_proj.shape[0]
    gating = main_proj[:, 0]
    mixed_in = jax.nn.silu(causal_conv(main_proj[:, 1], conv_main))
    flat_state = state_proj.reshape(length, -1)
    state_conv = jax.nn.silu(
        causal_conv(flat_state, conv_state.reshape(conv_state.shape[0], -1))
    ).reshape(length, 2, -1)
    step_sizes = jax.nn.softplus(step_proj + step_bias[:, None])
    decay_rates = -jnp.exp(decay_log)
    values = mixed_in.reshape(length, head_count, -1)
    scanned = state_space(values, step_sizes, decay_rates, state_conv[:, 0], state_conv[:, 1])
    scanned = scanned + skip_gain[None, :, None] * values
    gated = scanned.reshape(length, -1) * jax.nn.silu(gating)
    inverse = lax.rsqrt(jnp.mean(gated * gated, axis=1, keepdims=True) + EPSILON)
    return gated * inverse * norm_gain


def wide_body(
    weight_main,
    weight_state,
    weight_step,
    weight_out,
    conv_main,
    conv_state,
    step_bias,
    decay_log,
    skip_gain,
    norm_gain,
    saved_main,
    saved_state,
    saved_step,
    output_grad,
):
    sections = lax.axis_size("pipe")
    section = lax.axis_index("pipe")
    tensor_index = lax.axis_index("tensor")
    member = tensor_index % GROUP_SPAN
    group = tensor_index // GROUP_SPAN
    span_bits = GROUP_SPAN.bit_length() - 1
    length = saved_main.shape[1]
    col_count = output_grad.shape[1]
    model_width = weight_out.shape[2]
    main_cols = weight_main[0].reshape(model_width, -1)
    state_cols = weight_state[0].reshape(model_width, -1)
    step_rows = weight_step[0]
    out_rows = weight_out[0]
    state_group = lax.dynamic_slice_in_dim(saved_state[0], group * NSTATE, NSTATE, 2)
    conv_group = lax.dynamic_slice_in_dim(conv_state[0], group * NSTATE, NSTATE, 2)

    def local_mixer(first_in, second_in, third_in):
        return mamba_mixer(
            first_in,
            second_in,
            third_in,
            conv_main[0],
            conv_group,
            step_bias[0],
            decay_log[0],
            skip_gain[0],
            norm_gain[0],
        )

    _, pullback = jax.vjp(
        local_mixer,
        saved_main[0].astype(jnp.float32),
        state_group.astype(jnp.float32),
        saved_step[0].astype(jnp.float32),
    )
    result = jnp.zeros((length, col_count), jnp.bfloat16)
    incoming = output_grad
    for moment in range(sections):
        back_grad_main, back_grad_state, back_grad_step = pullback(
            lax.dot_general(
                lax.all_gather(incoming, "tensor", axis=1, tiled=True),
                out_rows,
                (((1,), (1,)), ((), ())),
                preferred_element_type=jnp.float32,
            )
        )
        kept = back_grad_state
        for bit in range(span_bits - 1, -1, -1):
            half = kept.shape[2] // 2
            lower = kept[:, :, :half]
            upper = kept[:, :, half:]
            high = member // 2**bit % 2 == 1
            own = jnp.where(high, upper, lower)
            other = jnp.where(high, lower, upper)
            kept = own + from_partner(other, "tensor", bit)
        grad_main = back_grad_main.astype(jnp.bfloat16).reshape(length, -1)
        grad_state = kept.astype(jnp.bfloat16).reshape(length, -1)
        grad_step = back_grad_step.astype(jnp.bfloat16)
        summed = lax.dot_general(
            main_cols, grad_main, (((1,), (1,)), ((), ())), preferred_element_type=jnp.float32
        )
        summed = summed + lax.dot_general(
            state_cols, grad_state, (((1,), (1,)), ((), ())), preferred_element_type=jnp.float32
        )
        owned = lax.psum_scatter(
            summed
            + lax.dot_general(
                step_rows, grad_step, (((0,), (0,)), ((), ())), preferred_element_type=jnp.float32
            ),
            "tensor",
            scatter_dimension=0,
            tiled=True,
        ).T.astype(jnp.bfloat16)
        result = jnp.where(section == sections - 1 - moment, owned, result)
        if moment + 1 < sections:
            incoming = passed_along(owned, "pipe", -1)
    return result[None]


BF16 = jnp.bfloat16
F32 = jnp.float32
SPACE = pltpu.VMEM
VMEM_BYTES = 28 * 2**20


def dot_nt(left, right, **options):
    return lax.dot_general(
        left, right, (((1,), (1,)), ((), ())), preferred_element_type=F32, **options
    )


def dot_tn(left, right):
    return lax.dot_general(left, right, (((0,), (0,)), ((), ())), preferred_element_type=F32)


def dot_nn(left, right, **options):
    return jnp.dot(left, right, preferred_element_type=F32, **options)


def iota(shape, dim):
    return lax.broadcasted_iota(jnp.int32, shape, dim)


def head_lanes(shape, head, size):
    lane = iota(shape, 1)
    return (lane >= head * size) & (lane < (head + 1) * size)


def conv_taps(signal, taps):
    count = taps.shape[0]
    row = iota(signal.shape, 0)
    total = taps[count - 1 : count] * signal
    for back in range(1, count):
        moved = jnp.where(row >= back, pltpu.roll(signal, back, 0), 0.0)
        total = total + taps[count - 1 - back : count - back] * moved
    return total


def conv_taps_back(grad, taps):
    count = taps.shape[0]
    length = grad.shape[0]
    row = iota(grad.shape, 0)
    total = taps[count - 1 : count] * grad
    for ahead in range(1, count):
        moved = jnp.where(row < length - ahead, pltpu.roll(grad, length - ahead, 0), 0.0)
        total = total + taps[count - 1 - ahead : count - ahead] * moved
    return total


def silu_and_slope(value):
    gate = jax.nn.sigmoid(value)
    return value * gate, gate * (1.0 + value * (1.0 - gate))


def forward_kernel(
    heads,
    gate_ref,
    mixer_ref,
    state_ref,
    step_ref,
    taps_main_ref,
    taps_state_ref,
    heads_ref,
    gain_ref,
    maps_ref,
    decay_ref,
    decayed_ref,
    values_ref,
    state_out_ref,
    slope_ref,
):
    length, channels = gate_ref.shape
    size = channels // heads
    states = state_ref.shape[1] // 2
    gate, gate_slope = silu_and_slope(gate_ref[...].astype(F32))
    value, value_slope = silu_and_slope(
        conv_taps(mixer_ref[...].astype(F32), taps_main_ref[...])
    )
    state, state_slope = silu_and_slope(
        conv_taps(state_ref[...].astype(F32), taps_state_ref[...])
    )
    inputs = state[:, :states]
    readout = state[:, states:]
    raw_step = step_ref[...] + heads_ref[0:1]
    step = jnp.maximum(raw_step, 0.0) + jnp.log1p(jnp.exp(-jnp.abs(raw_step)))
    slope_ref[...] = jax.nn.sigmoid(raw_step)
    rate = -jnp.exp(heads_ref[1:2])
    square = (length, length)
    later = iota(square, 0) >= iota(square, 1)
    earlier = iota(square, 0) <= iota(square, 1)
    running = dot_nn(later.astype(F32), step * rate, precision=HIGHEST)
    running_row = running.T
    scores = dot_nt(readout, inputs, precision=HIGHEST)
    scores_back = dot_nt(inputs, readout, precision=HIGHEST)
    wide = (length, channels)
    step_wide = jnp.zeros(wide, F32)
    skip_wide = jnp.zeros(wide, F32)
    for head in range(heads):
        lanes = head_lanes(wide, head, size)
        step_wide = jnp.where(lanes, step[:, head : head + 1], step_wide)
        skip_wide = jnp.where(lanes, heads_ref[2:3, head : head + 1], skip_wide)
    scaled = value * step_wide
    output = skip_wide * value
    for head in range(heads):
        lanes = head_lanes(wide, head, size)
        columns = pl.ds(head * length, length)
        column = running[:, head : head + 1]
        row = running_row[head : head + 1, :]
        decay = jnp.where(later, jnp.exp(jnp.where(later, column - row, 0.0)), 0.0)
        back = jnp.where(earlier, jnp.exp(jnp.where(earlier, row - column, 0.0)), 0.0)
        weights = decay * scores
        own = jnp.where(lanes, scaled, 0.0)
        output = output + dot_nn(weights, own, precision=HIGHEST)
        decay_ref[0, :, columns] = decay
        decay_ref[1, :, columns] = weights
        decayed_ref[:, columns] = (back * scores_back).astype(BF16)
        values_ref[columns, :] = own.astype(BF16)
    gated = output * gate
    inverse = lax.rsqrt(jnp.mean(gated * gated, axis=1, keepdims=True) + EPSILON)
    gain = gain_ref[...]
    normal = gated * inverse
    maps_ref[0] = gain * inverse
    maps_ref[1] = normal * inverse
    maps_ref[2] = gain * normal * (1.0 / channels)
    maps_ref[3] = gate
    maps_ref[4] = output * gate_slope
    maps_ref[5] = skip_wide * value_slope
    maps_ref[6] = step_wide * value_slope
    maps_ref[7] = value
    maps_ref[8] = state_slope
    state_out_ref[0] = inputs.astype(BF16)
    state_out_ref[1] = readout.astype(BF16)


def mixer_back(heads, dnormed, residuals):
    (
        maps_ref,
        decay_ref,
        decayed_ref,
        values_ref,
        state_ref,
        slope_ref,
        taps_main_ref,
        taps_state_ref,
        heads_ref,
    ) = residuals
    length, channels = dnormed.shape
    size = channels // heads
    shared = jnp.sum(dnormed * maps_ref[2], axis=1, keepdims=True)
    d_gated = dnormed * maps_ref[0] - maps_ref[1] * shared
    d_output = d_gated * maps_ref[3]
    d_gate = d_gated * maps_ref[4]
    by_head = jnp.concatenate(
        [
            jnp.where(head_lanes(d_output.shape, head, size), d_output, 0.0).astype(BF16)
            for head in range(heads)
        ],
        axis=0,
    )
    d_scaled = dot_nn(decayed_ref[...], by_head)
    d_weights = dot_nt(d_output.astype(BF16), values_ref[...])
    d_decayed = d_weights * decay_ref[0]
    d_scores = d_decayed[:, :length]
    for head in range(1, heads):
        d_scores = d_scores + d_decayed[:, head * length : (head + 1) * length]
    d_exponent = d_weights * decay_ref[1]
    square = (length, length)
    onward = (iota(square, 0) <= iota(square, 1)).astype(BF16)
    spanning = dot_nn(onward, d_exponent.astype(BF16))
    row = iota(spanning.shape, 0)
    source = iota(spanning.shape, 1) % length
    spanning = jnp.where(source < row, spanning, 0.0)
    lane = iota((channels, 128), 1)
    of_channel = (iota((channels, 128), 0) // size == lane).astype(BF16)
    of_source = (
        iota((heads * length, 128), 0) // length == iota((heads * length, 128), 1)
    ).astype(BF16)
    rate = -jnp.exp(heads_ref[1:2])
    d_step = dot_nn((d_scaled * maps_ref[7]).astype(BF16), of_channel)
    d_step = d_step + rate * dot_nn(spanning.astype(BF16), of_source)
    d_step = d_step * slope_ref[...]
    rounded = d_scores.astype(BF16)
    d_readout = dot_nn(rounded, state_ref[0])
    d_inputs = dot_tn(rounded, state_ref[1])
    d_state = jnp.concatenate([d_inputs, d_readout], axis=1) * maps_ref[8]
    d_mixer = d_output * maps_ref[5] + d_scaled * maps_ref[6]
    main = jnp.concatenate(
        [
            d_gate.astype(BF16),
            conv_taps_back(d_mixer, taps_main_ref[...]).astype(BF16),
            d_step.astype(BF16),
        ],
        axis=1,
    )
    return main, conv_taps_back(d_state, taps_state_ref[...]).astype(BF16)


def picked_members(chunks, state):
    me = lax.axis_index("tensor")
    states = state.shape[1] // 2
    share = states // chunks
    shape = (state.shape[1], 128)
    row = iota(shape, 0)
    lane = iota(shape, 1)
    source = jnp.where(lane < share, lane, lane + states - share)
    pieces = []
    for hop in range(chunks):
        member = lax.rem(me + hop, chunks)
        picked = (row == source + member * share) & (lane < 2 * share)
        pieces.append(dot_nn(state, picked.astype(BF16)).astype(BF16))
    return pieces


def first_kernel(heads, chunks, *refs):
    incoming, refs = refs[:chunks], refs[chunks:]
    rows_ref, refs = refs[0], refs[1:]
    residuals, refs = refs[:9], refs[9:]
    main_ref, outs = refs[0], refs[1:]
    dnormed = gathered_product(chunks, lax.axis_index("tensor"), incoming, rows_ref)
    main, state = mixer_back(heads, dnormed, residuals)
    main_ref[...] = main
    for out, piece in zip(outs, picked_members(chunks, state)):
        out[...] = piece


def next_kernel(heads, chunks, count, active, *refs):
    incoming, refs = refs[:count], refs[count:]
    residuals, refs = refs[:9], refs[9:]
    channels = residuals[0].shape[2]
    dnormed = incoming[0][:, :channels].astype(F32)
    for message in incoming[1:]:
        dnormed = dnormed + message[:, :channels].astype(F32)
    states = residuals[4].shape[2] * 2
    joined = count > 1
    if joined:
        place = slice(channels, channels + states)
        state = incoming[0][:, place].astype(F32)
        for hop in range(1, chunks):
            state = state + incoming[hop][:, place].astype(F32)
        share = states // chunks
        pieces = picked_members(chunks, state.astype(BF16))
        place = slice(channels + states, channels + states + channels // 2)
        for hop in range(chunks):
            piece = pieces[hop][:, :share]
            halves = [incoming[hop][start : start + share, place] for start in (0, share)]
            dnormed = dnormed + jnp.concatenate([dot_nn(piece, half) for half in halves], axis=1)
    main, state = mixer_back(heads, dnormed, residuals)
    if joined:
        done = lax.axis_index("pipe") > active
        main = jnp.where(done, refs[0][...], main)
        state = jnp.where(done, refs[1][...], state)
        refs = refs[2:]
    refs[0][...] = main
    refs[1][...] = state
    if joined:
        for ref, piece in zip(refs[2:], picked_members(chunks, state)):
            ref[...] = piece


def sum_pieces(pieces, width):
    total = pieces[0][...].astype(F32)
    for piece in pieces[1:]:
        total = total + piece[...].astype(F32)
    return total.astype(BF16)[:, :width]


def project_kernel(chunks, final, *refs):
    main_ref, refs = refs[0], refs[1:]
    pieces, refs = refs[:chunks], refs[chunks:]
    count = chunks if final else 0
    newest, refs = refs[:count], refs[count:]
    state_ref, refs = refs[0], refs[1:]
    if final:
        own_ref, other_ref, refs = refs[0], refs[1], refs[2:]
    step_rows_ref, cols_ref, refs = refs[0], refs[1], refs[2:]
    outs, refs = refs[:chunks], refs[chunks:]
    cols, sems = refs
    wide = cols.shape[2]
    heads = step_rows_ref.shape[0]
    me = lax.axis_index("tensor")
    width = cols.shape[1]
    places = []
    copies = []
    for hop in range(chunks):
        place = pl.ds(pl.multiple_of(lax.rem(me + hop, chunks) * width, width), width)
        copy = pltpu.make_async_copy(cols_ref.at[place, :], cols.at[hop], sems.at[hop])
        copy.start()
        places.append(place)
        copies.append(copy)
    main = main_ref[...]
    state = [sum_pieces(pieces, pieces[0].shape[1])]
    if final:
        nothing = jnp.zeros_like(state[0])
        first = lax.axis_index("pipe") == 0
        state = [
            jnp.where(first, piece[...], other)
            for piece, other in zip(newest, state + [nothing] * (chunks - 1))
        ]
    share = state_ref.shape[0]
    if final:
        others = jnp.concatenate([piece[:, :share] for piece in state[1:]], axis=1)
    core = lax.axis_index("dp")
    half = chunks // 2
    for hop in range(chunks):
        product = dot_nn(state[0][:, :share], state_ref[:, places[hop]])
        if final:
            chunk = lax.rem(me + hop, chunks)
            mine = chunk // half == core
            place = pl.ds(pl.multiple_of(lax.rem(chunk, half) * width, width), width)
            held = jnp.where(mine, own_ref[:, place], other_ref[:, place])
            product = product + dot_nn(others, held)
        product = product + dot_nn(main[:, wide : wide + heads], step_rows_ref[:, places[hop]])
        copies[hop].wait()
        outs[hop][...] = (product + dot_nt(main[:, :wide], cols[hop])).astype(BF16)


def compose_kernel(half, *refs):
    rows, refs = refs[:half], refs[half:]
    cols_ref, step_rows_ref, state_ref, joint_ref, main_sum, maps_sum = refs
    wide = cols_ref.shape[1]
    heads = step_rows_ref.shape[0]
    step = pl.program_id(0)
    size = rows[0].shape[0]
    map_width = main_sum.shape[1]
    section = lax.axis_index("pipe")

    @pl.when((section > 0) & (section < lax.axis_size("pipe") - 1))
    def _():
        stacked = jnp.concatenate([row[...] for row in rows], axis=0)
        main = dot_nn(stacked, cols_ref[...])
        steps = dot_nt(stacked, step_rows_ref[...])
        maps = dot_nt(state_ref[...], stacked)

        @pl.when(step == 0)
        def _():
            main_sum[:, :wide] = main
            main_sum[:, wide:] = jnp.zeros_like(main_sum[:, wide:])
            main_sum[:, wide : wide + heads] = steps
            maps_sum[...] = maps

        @pl.when(step > 0)
        def _():
            main_sum[:, :wide] += main
            main_sum[:, wide : wide + heads] += steps
            maps_sum[...] += maps

        @pl.when(step == pl.num_programs(0) - 1)
        def _():
            for hop in range(half):
                joint_ref[:size, hop * map_width : (hop + 1) * map_width] = main_sum[
                    hop * size : (hop + 1) * size, :
                ].astype(BF16)
            joint_ref[size:, : half * size] = maps_sum[...].astype(BF16)


def by_hop(chunks, own, other):
    core = lax.axis_index("dp")
    half = chunks // 2
    return [
        jnp.where((core == 0) == (hop < half), own[hop % half], other[hop % half])
        for hop in range(chunks)
    ]


def send_kernel(chunks, count, main_ref, state_ref, *refs):
    others, refs = refs[:count], refs[count:]
    sources, refs = refs[:2], refs[2:]
    outs, others_ref, held, sems = refs[:chunks], refs[chunks], refs[chunks + 1 : -1], refs[-1]
    if count:

        @pl.when(lax.axis_index("pipe") == 0)
        def _():
            for index, other in enumerate(others):
                size = other.shape[0]
                others_ref[index * size : (index + 1) * size, :] = other[...]

    half = chunks // 2
    map_width = main_ref.shape[1]
    states = state_ref.shape[1]
    share = states // chunks
    size = held[0].shape[0] - share
    copies = [
        pltpu.make_async_copy(source, place, sems.at[index])
        for index, (source, place) in enumerate(zip(sources, held))
    ]
    for copy in copies:
        copy.start()
    main = main_ref[...]
    for copy in copies:
        copy.wait()

    def terms(joint):
        return [
            dot_nt(main, joint[:size, hop * map_width : (hop + 1) * map_width])
            for hop in range(half)
        ]

    def maps(joint):
        return [joint[size:, hop * size : (hop + 1) * size] for hop in range(half)]

    total = by_hop(chunks, terms(held[0]), terms(held[1]))
    kept = by_hop(chunks, maps(held[0]), maps(held[1]))
    for hop in range(chunks):
        outs[hop][:, :size] = total[hop].astype(BF16)
        outs[hop][:, size : size + states] = state_ref[...]
        for part in range(2):
            outs[hop][part * share : (part + 1) * share, size + states :] = kept[hop][
                :, part * (size // 2) : (part + 1) * (size // 2)
            ]


def carry_kernel(chunks, last, *refs):
    carry = sum_pieces(refs[:chunks], refs[0].shape[1])
    if last:
        done_ref, out_ref = refs[chunks:]
        is_last = lax.axis_index("pipe") == lax.axis_size("pipe") - 1
        out_ref[0] = jnp.where(is_last, done_ref[...], carry)
    else:
        refs[-1][...] = carry


def dnormed_kernel(chunks, *refs):
    incoming, refs = refs[:chunks], refs[chunks:]
    *sources, out_ref, rows, sem = refs
    core = lax.axis_index("dp")
    last = lax.axis_index("pipe") == lax.axis_size("pipe") - 1
    for lane, source in enumerate(sources):

        @pl.when(last & (core == lane))
        def _():
            copy = pltpu.make_async_copy(source, rows, sem)
            copy.start()
            copy.wait()

    @pl.when(last)
    def _():
        product = gathered_product(chunks, lax.axis_index("tensor"), incoming, rows)
        out_ref[...] = product.astype(BF16)


def gathered_product(chunks, me, incoming, rows):
    width = incoming[0].shape[1]
    total = None
    for hop in range(chunks):
        chunk = lax.rem(me + chunks - hop, chunks)
        term = dot_nt(
            incoming[hop][...], rows[:, pl.ds(pl.multiple_of(chunk * width, width), width)]
        )
        total = term if total is None else total + term
    return total


def after(value, dependency):
    return lax.optimization_barrier((value, dependency))[0]


def kernel_params():
    return pltpu.CompilerParams(vmem_limit_bytes=VMEM_BYTES)


def whole(count):
    return [pl.BlockSpec(memory_space=SPACE)] * count


def section_pairs(sections, chunks, source, target, hop):
    return [
        (source * chunks + index, target * chunks + (index + hop) % chunks)
        for index in range(chunks)
    ]


def relay_body(
    weight_main,
    weight_state,
    weight_step,
    weight_out,
    conv_main,
    conv_state,
    step_bias,
    decay_log,
    skip_gain,
    norm_gain,
    saved_main,
    saved_state,
    saved_step,
    output_grad,
):
    sections = lax.axis_size("pipe")
    chunks = lax.axis_size("tensor")
    section = lax.axis_index("pipe")
    me = lax.axis_index("tensor")
    core = lax.axis_index("dp")
    length, width = output_grad.shape
    model_width = weight_out.shape[2]
    heads = step_bias.shape[1]
    channels = weight_out.shape[1]
    place = ("pipe", "tensor")

    def within(active, hop):
        return section_pairs(sections, chunks, active, active, hop)

    half = chunks // 2

    def rows_up(hop):
        pairs = []
        for source in range(sections - 1):
            for index in range(chunks):
                for lane in range(2):
                    move = hop + lane * half
                    if source == sections - 2:
                        if lane != hop:
                            continue
                        move = 0
                    start = (source * chunks + index) * 2 + lane
                    target = (source + 1) * chunks + (index + move) % chunks
                    pairs.append((start, target * 2 + lane))
        return pairs

    everywhere = ("pipe", "tensor", "dp")

    def swap(value, sections_in):
        pairs = []
        for source in sections_in:
            for start in range(source * chunks * 2, (source + 1) * chunks * 2):
                pairs.append((start, start ^ 1))
        return lax.ppermute(value, everywhere, pairs)

    incoming = [output_grad]
    for hop in range(1, chunks):
        incoming.append(lax.ppermute(output_grad, place, within(sections - 1, hop)))

    rows = [lax.ppermute(weight_out[0], everywhere, rows_up(hop)) for hop in range(half)]
    lanes = ((0, 0), (0, 128 - heads))
    by_head = jnp.pad(
        jnp.stack([step_bias[0], decay_log[0], skip_gain[0]]), ((0, 5), (0, 128 - heads))
    )
    steps = jnp.pad(saved_step[0].astype(F32).T, lanes)
    taps_main = conv_main[0]
    taps_state = conv_state[0].reshape(conv_state.shape[1], -1)
    state_width = taps_state.shape[1]
    residual_shapes = (
        jax.ShapeDtypeStruct((9, length, channels), F32),
        jax.ShapeDtypeStruct((2, length, heads * length), F32),
        jax.ShapeDtypeStruct((length, heads * length), BF16),
        jax.ShapeDtypeStruct((heads * length, channels), BF16),
        jax.ShapeDtypeStruct((2, length, state_width // 2), BF16),
        jax.ShapeDtypeStruct((length, 128), F32),
    )
    residuals = pl.pallas_call(
        lambda *refs: forward_kernel(heads, *refs),
        out_shape=residual_shapes,
        in_specs=whole(8),
        out_specs=whole(6),
        compiler_params=kernel_params(),
        name="forward_residuals",
    )(
        saved_main[0, :, 0],
        saved_main[0, :, 1],
        saved_state[0].reshape(length, -1),
        steps,
        taps_main,
        taps_state,
        by_head,
        norm_gain,
    )
    residuals = tuple(residuals) + (taps_main, taps_state, by_head)
    slice_out = jax.ShapeDtypeStruct((length, channels), BF16)
    message = jax.ShapeDtypeStruct((length, width), BF16)
    map_width = 2 * channels + 128
    main_shape = jax.ShapeDtypeStruct((length, map_width), BF16)
    piece_shape = jax.ShapeDtypeStruct((length, 128), BF16)
    hbm = pl.BlockSpec(memory_space=pl.ANY)
    main_cols = weight_main[0].reshape(model_width, -1)
    step_rows = weight_step[0]
    residuals = residuals[:-1] + (after(by_head, main_cols),)

    main, *pieces = pl.pallas_call(
        lambda *refs: first_kernel(heads, chunks, *refs),
        out_shape=(main_shape,) + (piece_shape,) * chunks,
        in_specs=whole(chunks + 10),
        out_specs=whole(1 + chunks),
        compiler_params=kernel_params(),
        name="section_first",
    )(*incoming, weight_out[0], *residuals)

    def share_state(pieces, sections_in):
        shared = [pieces[0]]
        for hop in range(1, chunks):
            pairs = []
            for source in sections_in:
                pairs += within(source, hop)
            shared.append(lax.ppermute(pieces[hop], place, pairs))
        return shared

    def project_call(main, pieces, newest=(), others=()):
        return pl.pallas_call(
            lambda *refs: project_kernel(chunks, bool(others), *refs),
            out_shape=(message,) * chunks,
            in_specs=whole(3 + chunks + len(newest) + len(others)) + [hbm],
            out_specs=whole(chunks),
            scratch_shapes=[
                pltpu.VMEM((chunks, width, 2 * channels), BF16),
                pltpu.SemaphoreType.DMA((chunks,)),
            ],
            compiler_params=kernel_params(),
            name="project",
        )(main, *pieces, *newest, state_cols, *others, step_rows, main_cols)

    pieces = share_state(pieces, [sections - 1])
    state_cols = after(weight_state[0], main).reshape(model_width, -1).T
    state_share = state_cols.shape[0]
    parts = project_call(main, pieces)
    exchanged = [parts[0]]
    for hop in range(1, chunks):
        exchanged.append(lax.ppermute(parts[hop], place, within(sections - 1, hop)))

    grid_steps = 4
    depth = model_width // grid_steps
    rows_spec = pl.BlockSpec((channels, depth), lambda step: (0, step))
    def pass_back(messages, active):
        moved = []
        for hop in range(chunks):
            pairs = section_pairs(sections, chunks, active, active - 1, chunks - hop)
            moved.append(lax.ppermute(messages[hop], place, pairs))
        return moved

    result = pl.pallas_call(
        lambda *refs: carry_kernel(chunks, False, *refs),
        out_shape=message,
        in_specs=whole(chunks),
        out_specs=pl.BlockSpec(memory_space=SPACE),
        compiler_params=kernel_params(),
        name="carry_next",
    )(*exchanged)
    exchanged = [result]
    for hop in range(1, chunks):
        exchanged.append(lax.ppermute(result, place, within(sections - 1, hop)))
    dnormed = pl.pallas_call(
        lambda *refs: dnormed_kernel(chunks, *refs),
        out_shape=slice_out,
        in_specs=whole(chunks) + [hbm] * 2,
        out_specs=pl.BlockSpec(memory_space=SPACE),
        scratch_shapes=[
            pltpu.VMEM((channels, model_width), BF16),
            pltpu.SemaphoreType.DMA,
        ],
        compiler_params=kernel_params(),
        name="dnormed_back",
    )(*exchanged, *rows)
    pairs = section_pairs(sections, chunks, sections - 1, sections - 2, 0)
    incoming = [lax.ppermute(dnormed, place, pairs)]
    joint_shape = jax.ShapeDtypeStruct((channels + state_share, half * map_width), BF16)
    joint = pl.pallas_call(
        lambda *refs: compose_kernel(half, *refs),
        grid=(grid_steps,),
        out_shape=joint_shape,
        in_specs=[rows_spec] * half
        + [pl.BlockSpec((depth, 2 * channels), lambda step: (step, 0))]
        + [pl.BlockSpec((count, depth), lambda step: (0, step)) for count in (heads, state_share)],
        out_specs=pl.BlockSpec(joint_shape.shape, lambda step: (0, 0)),
        scratch_shapes=[
            pltpu.VMEM((half * channels, map_width), F32),
            pltpu.VMEM((state_share, half * channels), F32),
        ],
        compiler_params=kernel_params(),
        name="compose_weights",
    )(*rows[:-1], after(rows[-1], dnormed), main_cols, step_rows, state_cols)

    half_cols = lax.dynamic_slice_in_dim(
        after(state_cols, parts[0]), core * (model_width // 2), model_width // 2, 1
    )
    residuals = residuals[:-1] + (after(by_head, (joint, half_cols)),)

    state_shape = jax.ShapeDtypeStruct((length, state_width), BF16)
    joined = jax.ShapeDtypeStruct((length, channels + state_width + channels // 2), BF16)
    assert 2 * state_share == length

    def next_call(incoming, kept, active):
        count = chunks if len(incoming) > 1 else 0
        main, state, *pieces = pl.pallas_call(
            lambda *refs: next_kernel(heads, chunks, len(incoming), active, *refs),
            out_shape=(main_shape, state_shape) + (piece_shape,) * count,
            in_specs=whole(len(incoming) + 9 + len(kept)),
            out_specs=whole(2 + count),
            compiler_params=kernel_params(),
            name="section_next",
        )(*incoming, *residuals, *kept)
        return (main, state), pieces

    joint_other = None
    kept = ()
    summed = None
    for active in range(sections - 2, -1, -1):
        kept, pieces = next_call(incoming, kept, active)
        if active == 0:
            break
        if joint_other is None:
            joint_other = swap(after(joint, kept[0]), range(1, sections - 1))
        state_others = []
        if active == sections - 2:
            late = after(half_cols, kept[0])
            state_others = [
                lax.ppermute(late, place, within(0, chunks - away)) for away in range(1, chunks)
            ]
        count = len(state_others)
        others_shape = jax.ShapeDtypeStruct((count * state_share, model_width // 2), BF16)
        *messages, state_others = pl.pallas_call(
            lambda *refs: send_kernel(chunks, count, *refs),
            out_shape=(joined,) * chunks + (others_shape if count else piece_shape,),
            in_specs=whole(2 + count) + [hbm] * 2,
            out_specs=whole(chunks + 1),
            scratch_shapes=[pltpu.VMEM(joint_shape.shape, BF16)] * 2
            + [pltpu.SemaphoreType.DMA((2,))],
            compiler_params=kernel_params(),
            name="send_back",
        )(*kept, *state_others, joint, joint_other)
        incoming = pass_back(messages, active)
        if active == sections - 2:
            shared = (state_others, swap(state_others, [0]))
        if active == 1:
            summed = share_state(after(pieces, incoming[0]), range(1, sections - 1))

    parts = project_call(kept[0], summed, pieces, shared)
    exchanged = [parts[0]]
    for hop in range(1, chunks):
        pairs = []
        for source in range(sections - 1):
            pairs += within(source, hop)
        exchanged.append(lax.ppermute(parts[hop], place, pairs))
    return pl.pallas_call(
        lambda *refs: carry_kernel(chunks, True, *refs),
        out_shape=jax.ShapeDtypeStruct((1, length, width), BF16),
        in_specs=whole(chunks + 1),
        out_specs=pl.BlockSpec(memory_space=SPACE),
        compiler_params=kernel_params(),
        name="carry_last",
    )(*exchanged, result)


def solution(mesh):
    narrow = mesh.shape["tensor"] == GROUP_SPAN
    return jax.shard_map(
        relay_body if narrow else wide_body,
        mesh=mesh,
        in_specs=(
            P("pipe", None, None, "tensor"),
            P("pipe", None, None, "tensor"),
            P("pipe", "tensor", None),
            P("pipe", "tensor", None),
            P("pipe", None, "tensor"),
            P("pipe", None, None, None),
            P("pipe", "tensor"),
            P("pipe", "tensor"),
            P("pipe", "tensor"),
            P("pipe", "tensor"),
            P("pipe", "dp", None, "tensor"),
            P("pipe", "dp", None, None),
            P("pipe", "tensor", "dp"),
            P("dp", "tensor"),
        ),
        out_specs=P("pipe", "dp", "tensor"),
        check_vma=False,
    )
```

```python
import jax
import jax.numpy as jnp
from jax import lax
from jax.experimental import pallas as pl
from jax.experimental.pallas import tpu as pltpu
from jax.sharding import PartitionSpec as P

NSTATE = 128
GROUP_SPAN = 4
STRETCH = 128


EPSILON = 1e-05
HIGHEST = lax.Precision.HIGHEST


def from_partner(value, axis, bit):
    mask = 2**bit
    pairs = [(source, source ^ mask) for source in range(lax.axis_size(axis))]
    return lax.ppermute(value, axis, pairs)


def passed_along(value, axis, steps):
    count = lax.axis_size(axis)
    leading, last = (max(0, -steps), min(count, count - steps))
    return lax.ppermute(value, axis, [(source, source + steps) for source in range(leading, last)])


def causal_conv(signal, kernel):
    taps = kernel.shape[0]
    length = signal.shape[0]
    padded = jnp.pad(signal, ((taps - 1, 0), (0, 0)))
    summed = kernel[0] * padded[0:length]
    for offset in range(1, taps):
        summed = summed + kernel[offset] * padded[offset : offset + length]
    return summed


def state_space(values, step_sizes, decay_rates, inputs, readout):
    length, head_count, head_size = values.shape
    blocks = length // STRETCH
    state_width = inputs.shape[1]
    decays = (step_sizes * decay_rates[:, None]).reshape(head_count, blocks, STRETCH)
    running = jnp.cumsum(decays, axis=2)
    scaled = (values * step_sizes.T[:, :, None]).reshape(blocks, STRETCH, head_count, head_size)
    inputs_blocked = inputs.reshape(blocks, STRETCH, state_width)
    readout_blocked = readout.reshape(blocks, STRETCH, state_width)
    scores = jnp.einsum("cin,cjn->cij", readout_blocked, inputs_blocked, precision=HIGHEST)
    position = jnp.arange(STRETCH)
    causal = position[:, None] >= position[None, :]
    differ = running[:, :, :, None] - running[:, :, None, :]
    weights = jnp.where(causal, jnp.exp(jnp.where(causal, differ, 0.0)), 0.0) * scores[None]
    within = jnp.einsum("hcij,cjhp->cihp", weights, scaled, precision=HIGHEST)
    tail_decay = jnp.exp(running[:, :, -1:] - running)
    weighted = scaled * jnp.transpose(tail_decay, (1, 2, 0))[:, :, :, None]
    block_sums = jnp.einsum("cjhp,cjn->chpn", weighted, inputs_blocked, precision=HIGHEST)
    shrinks = jnp.exp(running[:, :, -1]).T

    def advance(carried, item):
        newest, shrink = item
        return (carried * shrink[:, None, None] + newest, carried)

    anchor = jnp.zeros((head_count, head_size, state_width), jnp.float32)
    _, entering = lax.scan(advance, anchor, (block_sums, shrinks))
    across = jnp.einsum("cin,chpn->cihp", readout_blocked, entering, precision=HIGHEST)
    across = across * jnp.transpose(jnp.exp(running), (1, 2, 0))[:, :, :, None]
    return (within + across).reshape(length, head_count, head_size)


def mamba_mixer(
    main_proj,
    state_proj,
    step_proj,
    conv_main,
    conv_state,
    step_bias,
    decay_log,
    skip_gain,
    norm_gain,
):
    length = main_proj.shape[0]
    head_count = step_proj.shape[0]
    gating = main_proj[:, 0]
    mixed_in = jax.nn.silu(causal_conv(main_proj[:, 1], conv_main))
    flat_state = state_proj.reshape(length, -1)
    state_conv = jax.nn.silu(
        causal_conv(flat_state, conv_state.reshape(conv_state.shape[0], -1))
    ).reshape(length, 2, -1)
    step_sizes = jax.nn.softplus(step_proj + step_bias[:, None])
    decay_rates = -jnp.exp(decay_log)
    values = mixed_in.reshape(length, head_count, -1)
    scanned = state_space(values, step_sizes, decay_rates, state_conv[:, 0], state_conv[:, 1])
    scanned = scanned + skip_gain[None, :, None] * values
    gated = scanned.reshape(length, -1) * jax.nn.silu(gating)
    inverse = lax.rsqrt(jnp.mean(gated * gated, axis=1, keepdims=True) + EPSILON)
    return gated * inverse * norm_gain


def wide_body(
    weight_main,
    weight_state,
    weight_step,
    weight_out,
    conv_main,
    conv_state,
    step_bias,
    decay_log,
    skip_gain,
    norm_gain,
    saved_main,
    saved_state,
    saved_step,
    output_grad,
):
    sections = lax.axis_size("pipe")
    section = lax.axis_index("pipe")
    tensor_index = lax.axis_index("tensor")
    member = tensor_index % GROUP_SPAN
    group = tensor_index // GROUP_SPAN
    span_bits = GROUP_SPAN.bit_length() - 1
    length = saved_main.shape[1]
    col_count = output_grad.shape[1]
    model_width = weight_out.shape[2]
    main_cols = weight_main[0].reshape(model_width, -1)
    state_cols = weight_state[0].reshape(model_width, -1)
    step_rows = weight_step[0]
    out_rows = weight_out[0]
    state_group = lax.dynamic_slice_in_dim(saved_state[0], group * NSTATE, NSTATE, 2)
    conv_group = lax.dynamic_slice_in_dim(conv_state[0], group * NSTATE, NSTATE, 2)

    def local_mixer(first_in, second_in, third_in):
        return mamba_mixer(
            first_in,
            second_in,
            third_in,
            conv_main[0],
            conv_group,
            step_bias[0],
            decay_log[0],
            skip_gain[0],
            norm_gain[0],
        )

    _, pullback = jax.vjp(
        local_mixer,
        saved_main[0].astype(jnp.float32),
        state_group.astype(jnp.float32),
        saved_step[0].astype(jnp.float32),
    )
    result = jnp.zeros((length, col_count), jnp.bfloat16)
    incoming = output_grad
    for moment in range(sections):
        back_grad_main, back_grad_state, back_grad_step = pullback(
            lax.dot_general(
                lax.all_gather(incoming, "tensor", axis=1, tiled=True),
                out_rows,
                (((1,), (1,)), ((), ())),
                preferred_element_type=jnp.float32,
            )
        )
        kept = back_grad_state
        for bit in range(span_bits - 1, -1, -1):
            half = kept.shape[2] // 2
            lower = kept[:, :, :half]
            upper = kept[:, :, half:]
            high = member // 2**bit % 2 == 1
            own = jnp.where(high, upper, lower)
            other = jnp.where(high, lower, upper)
            kept = own + from_partner(other, "tensor", bit)
        grad_main = back_grad_main.astype(jnp.bfloat16).reshape(length, -1)
        grad_state = kept.astype(jnp.bfloat16).reshape(length, -1)
        grad_step = back_grad_step.astype(jnp.bfloat16)
        summed = lax.dot_general(
            main_cols, grad_main, (((1,), (1,)), ((), ())), preferred_element_type=jnp.float32
        )
        summed = summed + lax.dot_general(
            state_cols, grad_state, (((1,), (1,)), ((), ())), preferred_element_type=jnp.float32
        )
        owned = lax.psum_scatter(
            summed
            + lax.dot_general(
                step_rows, grad_step, (((0,), (0,)), ((), ())), preferred_element_type=jnp.float32
            ),
            "tensor",
            scatter_dimension=0,
            tiled=True,
        ).T.astype(jnp.bfloat16)
        result = jnp.where(section == sections - 1 - moment, owned, result)
        if moment + 1 < sections:
            incoming = passed_along(owned, "pipe", -1)
    return result[None]


BF16 = jnp.bfloat16
F32 = jnp.float32
SPACE = pltpu.VMEM
VMEM_BYTES = 28 * 2**20


def dot_nt(left, right, **options):
    return lax.dot_general(
        left, right, (((1,), (1,)), ((), ())), preferred_element_type=F32, **options
    )


def dot_tn(left, right):
    return lax.dot_general(left, right, (((0,), (0,)), ((), ())), preferred_element_type=F32)


def dot_nn(left, right, **options):
    return jnp.dot(left, right, preferred_element_type=F32, **options)


def iota(shape, dim):
    return lax.broadcasted_iota(jnp.int32, shape, dim)


def head_lanes(shape, head, size):
    lane = iota(shape, 1)
    return (lane >= head * size) & (lane < (head + 1) * size)


def conv_taps(signal, taps):
    count = taps.shape[0]
    row = iota(signal.shape, 0)
    total = taps[count - 1 : count] * signal
    for back in range(1, count):
        moved = jnp.where(row >= back, pltpu.roll(signal, back, 0), 0.0)
        total = total + taps[count - 1 - back : count - back] * moved
    return total


def conv_taps_back(grad, taps):
    count = taps.shape[0]
    length = grad.shape[0]
    row = iota(grad.shape, 0)
    total = taps[count - 1 : count] * grad
    for ahead in range(1, count):
        moved = jnp.where(row < length - ahead, pltpu.roll(grad, length - ahead, 0), 0.0)
        total = total + taps[count - 1 - ahead : count - ahead] * moved
    return total


def silu_and_slope(value):
    gate = jax.nn.sigmoid(value)
    return value * gate, gate * (1.0 + value * (1.0 - gate))


def forward_kernel(
    heads,
    gate_ref,
    mixer_ref,
    state_ref,
    step_ref,
    taps_main_ref,
    taps_state_ref,
    heads_ref,
    gain_ref,
    maps_ref,
    decay_ref,
    decayed_ref,
    values_ref,
    state_out_ref,
    slope_ref,
):
    length, channels = gate_ref.shape
    size = channels // heads
    states = state_ref.shape[1] // 2
    gate, gate_slope = silu_and_slope(gate_ref[...].astype(F32))
    value, value_slope = silu_and_slope(
        conv_taps(mixer_ref[...].astype(F32), taps_main_ref[...])
    )
    state, state_slope = silu_and_slope(
        conv_taps(state_ref[...].astype(F32), taps_state_ref[...])
    )
    inputs = state[:, :states]
    readout = state[:, states:]
    raw_step = step_ref[...] + heads_ref[0:1]
    step = jnp.maximum(raw_step, 0.0) + jnp.log1p(jnp.exp(-jnp.abs(raw_step)))
    slope_ref[...] = jax.nn.sigmoid(raw_step)
    rate = -jnp.exp(heads_ref[1:2])
    square = (length, length)
    later = iota(square, 0) >= iota(square, 1)
    earlier = iota(square, 0) <= iota(square, 1)
    running = dot_nn(later.astype(F32), step * rate, precision=HIGHEST)
    running_row = running.T
    scores = dot_nt(readout, inputs, precision=HIGHEST)
    scores_back = dot_nt(inputs, readout, precision=HIGHEST)
    wide = (length, channels)
    step_wide = jnp.zeros(wide, F32)
    skip_wide = jnp.zeros(wide, F32)
    for head in range(heads):
        lanes = head_lanes(wide, head, size)
        step_wide = jnp.where(lanes, step[:, head : head + 1], step_wide)
        skip_wide = jnp.where(lanes, heads_ref[2:3, head : head + 1], skip_wide)
    scaled = value * step_wide
    output = skip_wide * value
    for head in range(heads):
        lanes = head_lanes(wide, head, size)
        columns = pl.ds(head * length, length)
        column = running[:, head : head + 1]
        row = running_row[head : head + 1, :]
        decay = jnp.where(later, jnp.exp(jnp.where(later, column - row, 0.0)), 0.0)
        back = jnp.where(earlier, jnp.exp(jnp.where(earlier, row - column, 0.0)), 0.0)
        weights = decay * scores
        own = jnp.where(lanes, scaled, 0.0)
        output = output + dot_nn(weights, own, precision=HIGHEST)
        decay_ref[0, :, columns] = decay
        decay_ref[1, :, columns] = weights
        decayed_ref[:, columns] = (back * scores_back).astype(BF16)
        values_ref[columns, :] = own.astype(BF16)
    gated = output * gate
    inverse = lax.rsqrt(jnp.mean(gated * gated, axis=1, keepdims=True) + EPSILON)
    gain = gain_ref[...]
    normal = gated * inverse
    maps_ref[0] = gain * inverse
    maps_ref[1] = normal * inverse
    maps_ref[2] = gain * normal * (1.0 / channels)
    maps_ref[3] = gate
    maps_ref[4] = output * gate_slope
    maps_ref[5] = skip_wide * value_slope
    maps_ref[6] = step_wide * value_slope
    maps_ref[7] = value
    maps_ref[8] = state_slope
    state_out_ref[0] = inputs.astype(BF16)
    state_out_ref[1] = readout.astype(BF16)


def mixer_back(heads, dnormed, residuals):
    (
        maps_ref,
        decay_ref,
        decayed_ref,
        values_ref,
        state_ref,
        slope_ref,
        taps_main_ref,
        taps_state_ref,
        heads_ref,
    ) = residuals
    length, channels = dnormed.shape
    size = channels // heads
    shared = jnp.sum(dnormed * maps_ref[2], axis=1, keepdims=True)
    d_gated = dnormed * maps_ref[0] - maps_ref[1] * shared
    d_output = d_gated * maps_ref[3]
    d_gate = d_gated * maps_ref[4]
    by_head = jnp.concatenate(
        [
            jnp.where(head_lanes(d_output.shape, head, size), d_output, 0.0).astype(BF16)
            for head in range(heads)
        ],
        axis=0,
    )
    d_scaled = dot_nn(decayed_ref[...], by_head)
    d_weights = dot_nt(d_output.astype(BF16), values_ref[...])
    d_decayed = d_weights * decay_ref[0]
    d_scores = d_decayed[:, :length]
    for head in range(1, heads):
        d_scores = d_scores + d_decayed[:, head * length : (head + 1) * length]
    d_exponent = d_weights * decay_ref[1]
    square = (length, length)
    onward = (iota(square, 0) <= iota(square, 1)).astype(BF16)
    spanning = dot_nn(onward, d_exponent.astype(BF16))
    row = iota(spanning.shape, 0)
    source = iota(spanning.shape, 1) % length
    spanning = jnp.where(source < row, spanning, 0.0)
    lane = iota((channels, 128), 1)
    of_channel = (iota((channels, 128), 0) // size == lane).astype(BF16)
    of_source = (
        iota((heads * length, 128), 0) // length == iota((heads * length, 128), 1)
    ).astype(BF16)
    rate = -jnp.exp(heads_ref[1:2])
    d_step = dot_nn((d_scaled * maps_ref[7]).astype(BF16), of_channel)
    d_step = d_step + rate * dot_nn(spanning.astype(BF16), of_source)
    d_step = d_step * slope_ref[...]
    rounded = d_scores.astype(BF16)
    d_readout = dot_nn(rounded, state_ref[0])
    d_inputs = dot_tn(rounded, state_ref[1])
    d_state = jnp.concatenate([d_inputs, d_readout], axis=1) * maps_ref[8]
    d_mixer = d_output * maps_ref[5] + d_scaled * maps_ref[6]
    main = jnp.concatenate(
        [
            d_gate.astype(BF16),
            conv_taps_back(d_mixer, taps_main_ref[...]).astype(BF16),
            d_step.astype(BF16),
        ],
        axis=1,
    )
    return main, conv_taps_back(d_state, taps_state_ref[...]).astype(BF16)


def picked_members(chunks, state):
    me = lax.axis_index("tensor")
    states = state.shape[1] // 2
    share = states // chunks
    shape = (state.shape[1], 128)
    row = iota(shape, 0)
    lane = iota(shape, 1)
    source = jnp.where(lane < share, lane, lane + states - share)
    pieces = []
    for hop in range(chunks):
        member = lax.rem(me + hop, chunks)
        picked = (row == source + member * share) & (lane < 2 * share)
        pieces.append(dot_nn(state, picked.astype(BF16)).astype(BF16))
    return pieces


def first_kernel(heads, chunks, *refs):
    incoming, refs = refs[:chunks], refs[chunks:]
    rows_ref, refs = refs[0], refs[1:]
    residuals, refs = refs[:9], refs[9:]
    main_ref, outs = refs[0], refs[1:]
    dnormed = gathered_product(chunks, lax.axis_index("tensor"), incoming, rows_ref)
    main, state = mixer_back(heads, dnormed, residuals)
    main_ref[...] = main
    for out, piece in zip(outs, picked_members(chunks, state)):
        out[...] = piece


def next_kernel(heads, chunks, count, active, *refs):
    incoming, refs = refs[:count], refs[count:]
    residuals, refs = refs[:9], refs[9:]
    channels = residuals[0].shape[2]
    dnormed = incoming[0][:, :channels].astype(F32)
    for message in incoming[1:]:
        dnormed = dnormed + message[:, :channels].astype(F32)
    states = residuals[4].shape[2] * 2
    joined = incoming[0].shape[1] > channels
    if joined:
        place = slice(channels, channels + states)
        state = incoming[0][:, place].astype(F32)
        for hop in range(1, chunks):
            state = state + incoming[hop][:, place].astype(F32)
        share = states // chunks
        pieces = picked_members(chunks, state.astype(BF16))
        place = slice(channels + states, channels + states + channels // 2)
        for hop in range(chunks):
            piece = pieces[hop][:, :share]
            halves = [incoming[hop][start : start + share, place] for start in (0, share)]
            dnormed = dnormed + jnp.concatenate([dot_nn(piece, half) for half in halves], axis=1)
    main, state = mixer_back(heads, dnormed, residuals)
    if count > 1:
        done = lax.axis_index("pipe") > active
        main = jnp.where(done, refs[0][...], main)
        state = jnp.where(done, refs[1][...], state)
        refs = refs[2:]
    refs[0][...] = main
    refs[1][...] = state
    if count > 1:
        for ref, piece in zip(refs[2:], picked_members(chunks, state)):
            ref[...] = piece


def sum_pieces(pieces, width):
    total = pieces[0][...].astype(F32)
    for piece in pieces[1:]:
        total = total + piece[...].astype(F32)
    return total.astype(BF16)[:, :width]


def project_kernel(chunks, final, *refs):
    main_ref, refs = refs[0], refs[1:]
    pieces, refs = refs[:chunks], refs[chunks:]
    count = chunks if final else 0
    newest, refs = refs[:count], refs[count:]
    state_ref, refs = refs[0], refs[1:]
    if final:
        own_ref, other_ref, refs = refs[0], refs[1], refs[2:]
    step_rows_ref, cols_ref, refs = refs[0], refs[1], refs[2:]
    outs, refs = refs[:chunks], refs[chunks:]
    cols, sems = refs
    wide = cols.shape[2]
    heads = step_rows_ref.shape[0]
    me = lax.axis_index("tensor")
    width = cols.shape[1]
    places = []
    copies = []
    for hop in range(chunks):
        place = pl.ds(pl.multiple_of(lax.rem(me + hop, chunks) * width, width), width)
        copy = pltpu.make_async_copy(cols_ref.at[place, :], cols.at[hop], sems.at[hop])
        copy.start()
        places.append(place)
        copies.append(copy)
    main = main_ref[...]
    state = [sum_pieces(pieces, pieces[0].shape[1])]
    if final:
        nothing = jnp.zeros_like(state[0])
        first = lax.axis_index("pipe") == 0
        state = [
            jnp.where(first, piece[...], other)
            for piece, other in zip(newest, state + [nothing] * (chunks - 1))
        ]
    share = state_ref.shape[0]
    if final:
        others = jnp.concatenate([piece[:, :share] for piece in state[1:]], axis=1)
    core = lax.axis_index("dp")
    half = chunks // 2
    for hop in range(chunks):
        product = dot_nn(state[0][:, :share], state_ref[:, places[hop]])
        if final:
            chunk = lax.rem(me + hop, chunks)
            mine = chunk // half == core
            place = pl.ds(pl.multiple_of(lax.rem(chunk, half) * width, width), width)
            held = jnp.where(mine, own_ref[:, place], other_ref[:, place])
            product = product + dot_nn(others, held)
        product = product + dot_nn(main[:, wide : wide + heads], step_rows_ref[:, places[hop]])
        copies[hop].wait()
        outs[hop][...] = (product + dot_nt(main[:, :wide], cols[hop])).astype(BF16)


def compose_kernel(half, *refs):
    rows, refs = refs[:half], refs[half:]
    cols_ref, step_rows_ref, state_ref, joint_ref, main_sum, maps_sum = refs
    wide = cols_ref.shape[1]
    heads = step_rows_ref.shape[0]
    step = pl.program_id(0)
    size = rows[0].shape[0]
    map_width = main_sum.shape[1]
    section = lax.axis_index("pipe")

    @pl.when((section > 0) & (section < lax.axis_size("pipe") - 1))
    def _():
        stacked = jnp.concatenate([row[...] for row in rows], axis=0)
        main = dot_nn(stacked, cols_ref[...])
        steps = dot_nt(stacked, step_rows_ref[...])
        maps = dot_nt(state_ref[...], stacked)

        @pl.when(step == 0)
        def _():
            main_sum[:, :wide] = main
            main_sum[:, wide:] = jnp.zeros_like(main_sum[:, wide:])
            main_sum[:, wide : wide + heads] = steps
            maps_sum[...] = maps

        @pl.when(step > 0)
        def _():
            main_sum[:, :wide] += main
            main_sum[:, wide : wide + heads] += steps
            maps_sum[...] += maps

        @pl.when(step == pl.num_programs(0) - 1)
        def _():
            for hop in range(half):
                joint_ref[:size, hop * map_width : (hop + 1) * map_width] = main_sum[
                    hop * size : (hop + 1) * size, :
                ].astype(BF16)
            joint_ref[size:, : half * size] = maps_sum[...].astype(BF16)


def by_hop(chunks, own, other):
    core = lax.axis_index("dp")
    half = chunks // 2
    return [
        jnp.where((core == 0) == (hop < half), own[hop % half], other[hop % half])
        for hop in range(chunks)
    ]


def send_kernel(chunks, ahead, main_ref, state_ref, *refs):
    others, refs = refs[: chunks - 1], refs[chunks - 1 :]
    sources, refs = refs[:2], refs[2:]
    outs, refs = refs[:chunks], refs[chunks:]
    held, sems = refs[-3:-1], refs[-1]
    half = chunks // 2
    map_width = main_ref.shape[1]
    states = state_ref.shape[1]
    share = states // chunks
    size = held[0].shape[0] - share
    copies = [
        pltpu.make_async_copy(source, place, sems.at[index])
        for index, (source, place) in enumerate(zip(sources, held))
    ]
    for copy in copies:
        copy.start()
    if ahead:
        stack_ref, map_ref = refs[:2]

        @pl.when(lax.axis_index("pipe") == 0)
        def _():
            for index, other in enumerate(others):
                stack_ref[index * share : (index + 1) * share, :] = other[...]

    main = main_ref[...]
    state = state_ref[...]
    if not ahead:
        pieces = picked_members(chunks, state)
    for copy in copies:
        copy.wait()

    def terms(joint):
        return [
            dot_nt(main, joint[:size, hop * map_width : (hop + 1) * map_width])
            for hop in range(half)
        ]

    def maps(joint):
        return [joint[size:, hop * size : (hop + 1) * size] for hop in range(half)]

    total = by_hop(chunks, terms(held[0]), terms(held[1]))
    kept = by_hop(chunks, maps(held[0]), maps(held[1]))
    if not ahead:
        for hop in range(chunks):
            total[hop] = total[hop] + dot_nn(pieces[0][:, :share], kept[hop])
        for away, other in enumerate(others, 1):
            term = dot_nn(pieces[away][:, :share], other[...])
            for hop in range(chunks):
                start = (hop + away) % chunks * size
                total[hop] = total[hop] + term[:, start : start + size]
    for hop in range(chunks):
        outs[hop][:, :size] = total[hop].astype(BF16)
        if ahead:
            map_ref[:, hop * size : (hop + 1) * size] = kept[hop]
            outs[hop][:, size : size + states] = state
            for part in range(2):
                outs[hop][part * share : (part + 1) * share, size + states :] = kept[hop][
                    :, part * (size // 2) : (part + 1) * (size // 2)
                ]


def carry_kernel(chunks, *refs):
    refs[-1][...] = sum_pieces(refs[:chunks], refs[0].shape[1])


def dnormed_kernel(chunks, *refs):
    incoming, refs = refs[:chunks], refs[chunks:]
    *sources, out_ref, rows, sem = refs
    core = lax.axis_index("dp")
    last = lax.axis_index("pipe") == lax.axis_size("pipe") - 1
    for lane, source in enumerate(sources):

        @pl.when(last & (core == lane))
        def _():
            copy = pltpu.make_async_copy(source, rows, sem)
            copy.start()
            copy.wait()

    @pl.when(last)
    def _():
        product = gathered_product(chunks, lax.axis_index("tensor"), incoming, rows)
        out_ref[...] = product.astype(BF16)


def gathered_product(chunks, me, incoming, rows):
    width = incoming[0].shape[1]
    total = None
    for hop in range(chunks):
        chunk = lax.rem(me + chunks - hop, chunks)
        term = dot_nt(
            incoming[hop][...], rows[:, pl.ds(pl.multiple_of(chunk * width, width), width)]
        )
        total = term if total is None else total + term
    return total


def after(value, dependency):
    return lax.optimization_barrier((value, dependency))[0]


def kernel_params():
    return pltpu.CompilerParams(vmem_limit_bytes=VMEM_BYTES)


def whole(count):
    return [pl.BlockSpec(memory_space=SPACE)] * count


def section_pairs(sections, chunks, source, target, hop):
    return [
        (source * chunks + index, target * chunks + (index + hop) % chunks)
        for index in range(chunks)
    ]


def relay_body(
    weight_main,
    weight_state,
    weight_step,
    weight_out,
    conv_main,
    conv_state,
    step_bias,
    decay_log,
    skip_gain,
    norm_gain,
    saved_main,
    saved_state,
    saved_step,
    output_grad,
):
    sections = lax.axis_size("pipe")
    chunks = lax.axis_size("tensor")
    section = lax.axis_index("pipe")
    me = lax.axis_index("tensor")
    core = lax.axis_index("dp")
    length, width = output_grad.shape
    model_width = weight_out.shape[2]
    heads = step_bias.shape[1]
    channels = weight_out.shape[1]
    place = ("pipe", "tensor")

    def within(active, hop):
        return section_pairs(sections, chunks, active, active, hop)

    half = chunks // 2

    def rows_up(hop):
        pairs = []
        for source in range(sections - 1):
            for index in range(chunks):
                for lane in range(2):
                    move = hop + lane * half
                    if source == sections - 2:
                        if lane != hop:
                            continue
                        move = 0
                    start = (source * chunks + index) * 2 + lane
                    target = (source + 1) * chunks + (index + move) % chunks
                    pairs.append((start, target * 2 + lane))
        return pairs

    everywhere = ("pipe", "tensor", "dp")

    def swap(value, sections_in):
        pairs = []
        for source in sections_in:
            for start in range(source * chunks * 2, (source + 1) * chunks * 2):
                pairs.append((start, start ^ 1))
        return lax.ppermute(value, everywhere, pairs)

    incoming = [output_grad]
    for hop in range(1, chunks):
        incoming.append(lax.ppermute(output_grad, place, within(sections - 1, hop)))

    rows = [lax.ppermute(weight_out[0], everywhere, rows_up(hop)) for hop in range(half)]
    lanes = ((0, 0), (0, 128 - heads))
    by_head = jnp.pad(
        jnp.stack([step_bias[0], decay_log[0], skip_gain[0]]), ((0, 5), (0, 128 - heads))
    )
    steps = jnp.pad(saved_step[0].astype(F32).T, lanes)
    taps_main = conv_main[0]
    taps_state = conv_state[0].reshape(conv_state.shape[1], -1)
    state_width = taps_state.shape[1]
    residual_shapes = (
        jax.ShapeDtypeStruct((9, length, channels), F32),
        jax.ShapeDtypeStruct((2, length, heads * length), F32),
        jax.ShapeDtypeStruct((length, heads * length), BF16),
        jax.ShapeDtypeStruct((heads * length, channels), BF16),
        jax.ShapeDtypeStruct((2, length, state_width // 2), BF16),
        jax.ShapeDtypeStruct((length, 128), F32),
    )
    residuals = pl.pallas_call(
        lambda *refs: forward_kernel(heads, *refs),
        out_shape=residual_shapes,
        in_specs=whole(8),
        out_specs=whole(6),
        compiler_params=kernel_params(),
        name="forward_residuals",
    )(
        saved_main[0, :, 0],
        saved_main[0, :, 1],
        saved_state[0].reshape(length, -1),
        steps,
        taps_main,
        taps_state,
        by_head,
        norm_gain,
    )
    residuals = tuple(residuals) + (taps_main, taps_state, by_head)
    slice_out = jax.ShapeDtypeStruct((length, channels), BF16)
    message = jax.ShapeDtypeStruct((length, width), BF16)
    map_width = 2 * channels + 128
    main_shape = jax.ShapeDtypeStruct((length, map_width), BF16)
    piece_shape = jax.ShapeDtypeStruct((length, 128), BF16)
    hbm = pl.BlockSpec(memory_space=pl.ANY)
    main_cols = weight_main[0].reshape(model_width, -1)
    step_rows = weight_step[0]
    residuals = residuals[:-1] + (after(by_head, main_cols),)

    main, *pieces = pl.pallas_call(
        lambda *refs: first_kernel(heads, chunks, *refs),
        out_shape=(main_shape,) + (piece_shape,) * chunks,
        in_specs=whole(chunks + 10),
        out_specs=whole(1 + chunks),
        compiler_params=kernel_params(),
        name="section_first",
    )(*incoming, weight_out[0], *residuals)

    def share_state(pieces, sections_in):
        shared = [pieces[0]]
        for hop in range(1, chunks):
            pairs = []
            for source in sections_in:
                pairs += within(source, hop)
            shared.append(lax.ppermute(pieces[hop], place, pairs))
        return shared

    def project_call(main, pieces, newest=(), others=()):
        return pl.pallas_call(
            lambda *refs: project_kernel(chunks, bool(others), *refs),
            out_shape=(message,) * chunks,
            in_specs=whole(3 + chunks + len(newest) + len(others)) + [hbm],
            out_specs=whole(chunks),
            scratch_shapes=[
                pltpu.VMEM((chunks, width, 2 * channels), BF16),
                pltpu.SemaphoreType.DMA((chunks,)),
            ],
            compiler_params=kernel_params(),
            name="project",
        )(main, *pieces, *newest, state_cols, *others, step_rows, main_cols)

    pieces = share_state(pieces, [sections - 1])
    state_cols = after(weight_state[0], main).reshape(model_width, -1).T
    state_share = state_cols.shape[0]
    parts = project_call(main, pieces)
    exchanged = [parts[0]]
    for hop in range(1, chunks):
        exchanged.append(lax.ppermute(parts[hop], place, within(sections - 1, hop)))

    grid_steps = 2
    depth = model_width // grid_steps
    rows_spec = pl.BlockSpec((channels, depth), lambda step: (0, step))
    def pass_back(messages, active):
        moved = []
        for hop in range(chunks):
            pairs = section_pairs(sections, chunks, active, active - 1, chunks - hop)
            moved.append(lax.ppermute(messages[hop], place, pairs))
        return moved

    result = pl.pallas_call(
        lambda *refs: carry_kernel(chunks, *refs),
        out_shape=message,
        in_specs=whole(chunks),
        out_specs=pl.BlockSpec(memory_space=SPACE),
        compiler_params=kernel_params(),
        name="carry_next",
    )(*exchanged)
    exchanged = [result]
    for hop in range(1, chunks):
        exchanged.append(lax.ppermute(result, place, within(sections - 1, hop)))
    dnormed = pl.pallas_call(
        lambda *refs: dnormed_kernel(chunks, *refs),
        out_shape=slice_out,
        in_specs=whole(chunks) + [hbm] * 2,
        out_specs=pl.BlockSpec(memory_space=SPACE),
        scratch_shapes=[
            pltpu.VMEM((channels, model_width), BF16),
            pltpu.SemaphoreType.DMA,
        ],
        compiler_params=kernel_params(),
        name="dnormed_back",
    )(*exchanged, *rows)
    pairs = section_pairs(sections, chunks, sections - 1, sections - 2, 0)
    incoming = [lax.ppermute(dnormed, place, pairs)]
    joint_shape = jax.ShapeDtypeStruct((channels + state_share, half * map_width), BF16)
    joint = pl.pallas_call(
        lambda *refs: compose_kernel(half, *refs),
        grid=(grid_steps,),
        out_shape=joint_shape,
        in_specs=[rows_spec] * half
        + [pl.BlockSpec((depth, 2 * channels), lambda step: (step, 0))]
        + [pl.BlockSpec((count, depth), lambda step: (0, step)) for count in (heads, state_share)],
        out_specs=pl.BlockSpec(joint_shape.shape, lambda step: (0, 0)),
        scratch_shapes=[
            pltpu.VMEM((half * channels, map_width), F32),
            pltpu.VMEM((state_share, half * channels), F32),
        ],
        compiler_params=kernel_params(),
        name="compose_weights",
    )(*rows[:-1], after(rows[-1], dnormed), main_cols, step_rows, state_cols)

    half_cols = lax.dynamic_slice_in_dim(
        after(state_cols, parts[0]), core * (model_width // 2), model_width // 2, 1
    )
    residuals = residuals[:-1] + (after(by_head, (joint, half_cols)),)

    state_shape = jax.ShapeDtypeStruct((length, state_width), BF16)
    joined = jax.ShapeDtypeStruct((length, channels + state_width + channels // 2), BF16)
    assert 2 * state_share == length

    def next_call(incoming, kept, active):
        count = chunks if len(incoming) > 1 else 0
        main, state, *pieces = pl.pallas_call(
            lambda *refs: next_kernel(heads, chunks, len(incoming), active, *refs),
            out_shape=(main_shape, state_shape) + (piece_shape,) * count,
            in_specs=whole(len(incoming) + 9 + len(kept)),
            out_specs=whole(2 + count),
            compiler_params=kernel_params(),
            name="section_next",
        )(*incoming, *residuals, *kept)
        return (main, state), pieces

    joint_other = None
    kept = ()
    summed = None
    for active in range(sections - 2, -1, -1):
        kept, pieces = next_call(incoming, kept, active)
        if active == 0:
            break
        if joint_other is None:
            joint_other = swap(after(joint, kept[0]), range(1, sections - 1))
        ahead = active == sections - 2
        if ahead:
            late = after(half_cols, kept[0])
            others = [
                lax.ppermute(late, place, within(0, chunks - away)) for away in range(1, chunks)
            ]
            stack = jax.ShapeDtypeStruct(((chunks - 1) * state_share, model_width // 2), BF16)
            state_map = jax.ShapeDtypeStruct((state_share, chunks * channels), BF16)
            outs = (joined,) * chunks + (stack, state_map)
        else:
            outs = (slice_out,) * chunks
        messages = pl.pallas_call(
            lambda *refs: send_kernel(chunks, ahead, *refs),
            out_shape=outs,
            in_specs=whole(2 + len(others)) + [hbm] * 2,
            out_specs=whole(len(outs)),
            scratch_shapes=[pltpu.VMEM(joint_shape.shape, BF16)] * 2
            + [pltpu.SemaphoreType.DMA((2,))],
            compiler_params=kernel_params(),
            name="send_ahead" if ahead else "send_back",
        )(*kept, *others, joint, joint_other)
        incoming = pass_back(messages, active)
        if ahead:
            stack, late = messages[chunks], after(messages[chunks + 1], incoming[0])
            others = [
                lax.ppermute(late, place, within(1, chunks - away)) for away in range(1, chunks)
            ]
        else:
            shared = (stack, swap(after(stack, messages[0]), [0]))
            summed = share_state(after(pieces, incoming[0]), range(1, sections - 1))

    parts = project_call(kept[0], summed, pieces, shared)
    exchanged = [parts[0]]
    for hop in range(1, chunks):
        pairs = []
        for source in range(sections - 1):
            pairs += within(source, hop)
        exchanged.append(lax.ppermute(parts[hop], place, pairs))
    total = exchanged[0].astype(F32)
    for part in exchanged[1:]:
        total = total + part.astype(F32)
    return jnp.where(section == sections - 1, result, total.astype(BF16))[None]


def solution(mesh):
    narrow = mesh.shape["tensor"] == GROUP_SPAN
    return jax.shard_map(
        relay_body if narrow else wide_body,
        mesh=mesh,
        in_specs=(
            P("pipe", None, None, "tensor"),
            P("pipe", None, None, "tensor"),
            P("pipe", "tensor", None),
            P("pipe", "tensor", None),
            P("pipe", None, "tensor"),
            P("pipe", None, None, None),
            P("pipe", "tensor"),
            P("pipe", "tensor"),
            P("pipe", "tensor"),
            P("pipe", "tensor"),
            P("pipe", "dp", None, "tensor"),
            P("pipe", "dp", None, None),
            P("pipe", "tensor", "dp"),
            P("dp", "tensor"),
        ),
        out_specs=P("pipe", "dp", "tensor"),
        check_vma=False,
    )
```

```python
import jax
import jax.numpy as jnp
from jax import lax
from jax.experimental import pallas as pl
from jax.experimental.pallas import tpu as pltpu
from jax.sharding import PartitionSpec as P

NSTATE = 128
GROUP_SPAN = 4
STRETCH = 128


EPSILON = 1e-05
HIGHEST = lax.Precision.HIGHEST


def from_partner(value, axis, bit):
    mask = 2**bit
    pairs = [(source, source ^ mask) for source in range(lax.axis_size(axis))]
    return lax.ppermute(value, axis, pairs)


def passed_along(value, axis, steps):
    count = lax.axis_size(axis)
    leading, last = (max(0, -steps), min(count, count - steps))
    return lax.ppermute(value, axis, [(source, source + steps) for source in range(leading, last)])


def causal_conv(signal, kernel):
    taps = kernel.shape[0]
    length = signal.shape[0]
    padded = jnp.pad(signal, ((taps - 1, 0), (0, 0)))
    summed = kernel[0] * padded[0:length]
    for offset in range(1, taps):
        summed = summed + kernel[offset] * padded[offset : offset + length]
    return summed


def state_space(values, step_sizes, decay_rates, inputs, readout):
    length, head_count, head_size = values.shape
    blocks = length // STRETCH
    state_width = inputs.shape[1]
    decays = (step_sizes * decay_rates[:, None]).reshape(head_count, blocks, STRETCH)
    running = jnp.cumsum(decays, axis=2)
    scaled = (values * step_sizes.T[:, :, None]).reshape(blocks, STRETCH, head_count, head_size)
    inputs_blocked = inputs.reshape(blocks, STRETCH, state_width)
    readout_blocked = readout.reshape(blocks, STRETCH, state_width)
    scores = jnp.einsum("cin,cjn->cij", readout_blocked, inputs_blocked, precision=HIGHEST)
    position = jnp.arange(STRETCH)
    causal = position[:, None] >= position[None, :]
    differ = running[:, :, :, None] - running[:, :, None, :]
    weights = jnp.where(causal, jnp.exp(jnp.where(causal, differ, 0.0)), 0.0) * scores[None]
    within = jnp.einsum("hcij,cjhp->cihp", weights, scaled, precision=HIGHEST)
    tail_decay = jnp.exp(running[:, :, -1:] - running)
    weighted = scaled * jnp.transpose(tail_decay, (1, 2, 0))[:, :, :, None]
    block_sums = jnp.einsum("cjhp,cjn->chpn", weighted, inputs_blocked, precision=HIGHEST)
    shrinks = jnp.exp(running[:, :, -1]).T

    def advance(carried, item):
        newest, shrink = item
        return (carried * shrink[:, None, None] + newest, carried)

    anchor = jnp.zeros((head_count, head_size, state_width), jnp.float32)
    _, entering = lax.scan(advance, anchor, (block_sums, shrinks))
    across = jnp.einsum("cin,chpn->cihp", readout_blocked, entering, precision=HIGHEST)
    across = across * jnp.transpose(jnp.exp(running), (1, 2, 0))[:, :, :, None]
    return (within + across).reshape(length, head_count, head_size)


def mamba_mixer(
    main_proj,
    state_proj,
    step_proj,
    conv_main,
    conv_state,
    step_bias,
    decay_log,
    skip_gain,
    norm_gain,
):
    length = main_proj.shape[0]
    head_count = step_proj.shape[0]
    gating = main_proj[:, 0]
    mixed_in = jax.nn.silu(causal_conv(main_proj[:, 1], conv_main))
    flat_state = state_proj.reshape(length, -1)
    state_conv = jax.nn.silu(
        causal_conv(flat_state, conv_state.reshape(conv_state.shape[0], -1))
    ).reshape(length, 2, -1)
    step_sizes = jax.nn.softplus(step_proj + step_bias[:, None])
    decay_rates = -jnp.exp(decay_log)
    values = mixed_in.reshape(length, head_count, -1)
    scanned = state_space(values, step_sizes, decay_rates, state_conv[:, 0], state_conv[:, 1])
    scanned = scanned + skip_gain[None, :, None] * values
    gated = scanned.reshape(length, -1) * jax.nn.silu(gating)
    inverse = lax.rsqrt(jnp.mean(gated * gated, axis=1, keepdims=True) + EPSILON)
    return gated * inverse * norm_gain


def wide_body(
    weight_main,
    weight_state,
    weight_step,
    weight_out,
    conv_main,
    conv_state,
    step_bias,
    decay_log,
    skip_gain,
    norm_gain,
    saved_main,
    saved_state,
    saved_step,
    output_grad,
):
    sections = lax.axis_size("pipe")
    section = lax.axis_index("pipe")
    tensor_index = lax.axis_index("tensor")
    member = tensor_index % GROUP_SPAN
    group = tensor_index // GROUP_SPAN
    span_bits = GROUP_SPAN.bit_length() - 1
    length = saved_main.shape[1]
    col_count = output_grad.shape[1]
    model_width = weight_out.shape[2]
    main_cols = weight_main[0].reshape(model_width, -1)
    state_cols = weight_state[0].reshape(model_width, -1)
    step_rows = weight_step[0]
    out_rows = weight_out[0]
    state_group = lax.dynamic_slice_in_dim(saved_state[0], group * NSTATE, NSTATE, 2)
    conv_group = lax.dynamic_slice_in_dim(conv_state[0], group * NSTATE, NSTATE, 2)

    def local_mixer(first_in, second_in, third_in):
        return mamba_mixer(
            first_in,
            second_in,
            third_in,
            conv_main[0],
            conv_group,
            step_bias[0],
            decay_log[0],
            skip_gain[0],
            norm_gain[0],
        )

    _, pullback = jax.vjp(
        local_mixer,
        saved_main[0].astype(jnp.float32),
        state_group.astype(jnp.float32),
        saved_step[0].astype(jnp.float32),
    )
    result = jnp.zeros((length, col_count), jnp.bfloat16)
    incoming = output_grad
    for moment in range(sections):
        back_grad_main, back_grad_state, back_grad_step = pullback(
            lax.dot_general(
                lax.all_gather(incoming, "tensor", axis=1, tiled=True),
                out_rows,
                (((1,), (1,)), ((), ())),
                preferred_element_type=jnp.float32,
            )
        )
        kept = back_grad_state
        for bit in range(span_bits - 1, -1, -1):
            half = kept.shape[2] // 2
            lower = kept[:, :, :half]
            upper = kept[:, :, half:]
            high = member // 2**bit % 2 == 1
            own = jnp.where(high, upper, lower)
            other = jnp.where(high, lower, upper)
            kept = own + from_partner(other, "tensor", bit)
        grad_main = back_grad_main.astype(jnp.bfloat16).reshape(length, -1)
        grad_state = kept.astype(jnp.bfloat16).reshape(length, -1)
        grad_step = back_grad_step.astype(jnp.bfloat16)
        summed = lax.dot_general(
            main_cols, grad_main, (((1,), (1,)), ((), ())), preferred_element_type=jnp.float32
        )
        summed = summed + lax.dot_general(
            state_cols, grad_state, (((1,), (1,)), ((), ())), preferred_element_type=jnp.float32
        )
        owned = lax.psum_scatter(
            summed
            + lax.dot_general(
                step_rows, grad_step, (((0,), (0,)), ((), ())), preferred_element_type=jnp.float32
            ),
            "tensor",
            scatter_dimension=0,
            tiled=True,
        ).T.astype(jnp.bfloat16)
        result = jnp.where(section == sections - 1 - moment, owned, result)
        if moment + 1 < sections:
            incoming = passed_along(owned, "pipe", -1)
    return result[None]


BF16 = jnp.bfloat16
F32 = jnp.float32
SPACE = pltpu.VMEM
VMEM_BYTES = 28 * 2**20


def dot_nt(left, right, **options):
    return lax.dot_general(
        left, right, (((1,), (1,)), ((), ())), preferred_element_type=F32, **options
    )


def dot_tn(left, right):
    return lax.dot_general(left, right, (((0,), (0,)), ((), ())), preferred_element_type=F32)


def dot_nn(left, right, **options):
    return jnp.dot(left, right, preferred_element_type=F32, **options)


def iota(shape, dim):
    return lax.broadcasted_iota(jnp.int32, shape, dim)


def head_lanes(shape, head, size):
    lane = iota(shape, 1)
    return (lane >= head * size) & (lane < (head + 1) * size)


def conv_taps(signal, taps):
    count = taps.shape[0]
    row = iota(signal.shape, 0)
    total = taps[count - 1 : count] * signal
    for back in range(1, count):
        moved = jnp.where(row >= back, pltpu.roll(signal, back, 0), 0.0)
        total = total + taps[count - 1 - back : count - back] * moved
    return total


def conv_taps_back(grad, taps):
    count = taps.shape[0]
    length = grad.shape[0]
    row = iota(grad.shape, 0)
    total = taps[count - 1 : count] * grad
    for ahead in range(1, count):
        moved = jnp.where(row < length - ahead, pltpu.roll(grad, length - ahead, 0), 0.0)
        total = total + taps[count - 1 - ahead : count - ahead] * moved
    return total


def silu_and_slope(value):
    gate = jax.nn.sigmoid(value)
    return value * gate, gate * (1.0 + value * (1.0 - gate))


def forward_kernel(
    heads,
    gate_ref,
    mixer_ref,
    state_ref,
    step_ref,
    taps_main_ref,
    taps_state_ref,
    heads_ref,
    gain_ref,
    maps_ref,
    decay_ref,
    decayed_ref,
    values_ref,
    state_out_ref,
    slope_ref,
):
    length, channels = gate_ref.shape
    size = channels // heads
    states = state_ref.shape[1] // 2
    gate, gate_slope = silu_and_slope(gate_ref[...].astype(F32))
    value, value_slope = silu_and_slope(
        conv_taps(mixer_ref[...].astype(F32), taps_main_ref[...])
    )
    state, state_slope = silu_and_slope(
        conv_taps(state_ref[...].astype(F32), taps_state_ref[...])
    )
    inputs = state[:, :states]
    readout = state[:, states:]
    raw_step = step_ref[...] + heads_ref[0:1]
    step = jnp.maximum(raw_step, 0.0) + jnp.log1p(jnp.exp(-jnp.abs(raw_step)))
    slope_ref[...] = jax.nn.sigmoid(raw_step)
    rate = -jnp.exp(heads_ref[1:2])
    square = (length, length)
    later = iota(square, 0) >= iota(square, 1)
    earlier = iota(square, 0) <= iota(square, 1)
    running = dot_nn(later.astype(F32), step * rate, precision=HIGHEST)
    running_row = running.T
    scores = dot_nt(readout, inputs, precision=HIGHEST)
    scores_back = dot_nt(inputs, readout, precision=HIGHEST)
    wide = (length, channels)
    step_wide = jnp.zeros(wide, F32)
    skip_wide = jnp.zeros(wide, F32)
    for head in range(heads):
        lanes = head_lanes(wide, head, size)
        step_wide = jnp.where(lanes, step[:, head : head + 1], step_wide)
        skip_wide = jnp.where(lanes, heads_ref[2:3, head : head + 1], skip_wide)
    scaled = value * step_wide
    output = skip_wide * value
    for head in range(heads):
        lanes = head_lanes(wide, head, size)
        columns = pl.ds(head * length, length)
        column = running[:, head : head + 1]
        row = running_row[head : head + 1, :]
        decay = jnp.where(later, jnp.exp(jnp.where(later, column - row, 0.0)), 0.0)
        back = jnp.where(earlier, jnp.exp(jnp.where(earlier, row - column, 0.0)), 0.0)
        weights = decay * scores
        own = jnp.where(lanes, scaled, 0.0)
        output = output + dot_nn(weights, own, precision=HIGHEST)
        decay_ref[0, :, columns] = decay
        decay_ref[1, :, columns] = weights
        decayed_ref[:, columns] = (back * scores_back).astype(BF16)
        values_ref[columns, :] = own.astype(BF16)
    gated = output * gate
    inverse = lax.rsqrt(jnp.mean(gated * gated, axis=1, keepdims=True) + EPSILON)
    gain = gain_ref[...]
    normal = gated * inverse
    maps_ref[0] = gain * inverse
    maps_ref[1] = normal * inverse
    maps_ref[2] = gain * normal * (1.0 / channels)
    maps_ref[3] = gate
    maps_ref[4] = output * gate_slope
    maps_ref[5] = skip_wide * value_slope
    maps_ref[6] = step_wide * value_slope
    maps_ref[7] = value
    maps_ref[8] = state_slope
    state_out_ref[0] = inputs.astype(BF16)
    state_out_ref[1] = readout.astype(BF16)


def mixer_back(heads, dnormed, residuals):
    (
        maps_ref,
        decay_ref,
        decayed_ref,
        values_ref,
        state_ref,
        slope_ref,
        taps_main_ref,
        taps_state_ref,
        heads_ref,
    ) = residuals
    length, channels = dnormed.shape
    size = channels // heads
    shared = jnp.sum(dnormed * maps_ref[2], axis=1, keepdims=True)
    d_gated = dnormed * maps_ref[0] - maps_ref[1] * shared
    d_output = d_gated * maps_ref[3]
    d_gate = d_gated * maps_ref[4]
    by_head = jnp.concatenate(
        [
            jnp.where(head_lanes(d_output.shape, head, size), d_output, 0.0).astype(BF16)
            for head in range(heads)
        ],
        axis=0,
    )
    d_scaled = dot_nn(decayed_ref[...], by_head)
    d_weights = dot_nt(d_output.astype(BF16), values_ref[...])
    d_decayed = d_weights * decay_ref[0]
    d_scores = d_decayed[:, :length]
    for head in range(1, heads):
        d_scores = d_scores + d_decayed[:, head * length : (head + 1) * length]
    d_exponent = d_weights * decay_ref[1]
    square = (length, length)
    onward = (iota(square, 0) <= iota(square, 1)).astype(BF16)
    spanning = dot_nn(onward, d_exponent.astype(BF16))
    row = iota(spanning.shape, 0)
    source = iota(spanning.shape, 1) % length
    spanning = jnp.where(source < row, spanning, 0.0)
    lane = iota((channels, 128), 1)
    of_channel = (iota((channels, 128), 0) // size == lane).astype(BF16)
    of_source = (
        iota((heads * length, 128), 0) // length == iota((heads * length, 128), 1)
    ).astype(BF16)
    rate = -jnp.exp(heads_ref[1:2])
    d_step = dot_nn((d_scaled * maps_ref[7]).astype(BF16), of_channel)
    d_step = d_step + rate * dot_nn(spanning.astype(BF16), of_source)
    d_step = d_step * slope_ref[...]
    rounded = d_scores.astype(BF16)
    d_readout = dot_nn(rounded, state_ref[0])
    d_inputs = dot_tn(rounded, state_ref[1])
    d_state = jnp.concatenate([d_inputs, d_readout], axis=1) * maps_ref[8]
    d_mixer = d_output * maps_ref[5] + d_scaled * maps_ref[6]
    main = jnp.concatenate(
        [
            d_gate.astype(BF16),
            conv_taps_back(d_mixer, taps_main_ref[...]).astype(BF16),
            d_step.astype(BF16),
        ],
        axis=1,
    )
    return main, conv_taps_back(d_state, taps_state_ref[...]).astype(BF16)


def picked_members(chunks, state):
    me = lax.axis_index("tensor")
    states = state.shape[1] // 2
    share = states // chunks
    shape = (state.shape[1], 128)
    row = iota(shape, 0)
    lane = iota(shape, 1)
    source = jnp.where(lane < share, lane, lane + states - share)
    pieces = []
    for hop in range(chunks):
        member = lax.rem(me + hop, chunks)
        picked = (row == source + member * share) & (lane < 2 * share)
        pieces.append(dot_nn(state, picked.astype(BF16)).astype(BF16))
    return pieces


def first_kernel(heads, chunks, *refs):
    incoming, refs = refs[:chunks], refs[chunks:]
    rows_ref, refs = refs[0], refs[1:]
    residuals, refs = refs[:9], refs[9:]
    main_ref, outs = refs[0], refs[1:]
    dnormed = gathered_product(chunks, lax.axis_index("tensor"), incoming, rows_ref)
    main, state = mixer_back(heads, dnormed, residuals)
    main_ref[...] = main
    for out, piece in zip(outs, picked_members(chunks, state)):
        out[...] = piece


def next_kernel(heads, chunks, count, active, *refs):
    incoming, refs = refs[:count], refs[count:]
    residuals, refs = refs[:9], refs[9:]
    channels = residuals[0].shape[2]
    dnormed = incoming[0][:, :channels].astype(F32)
    for message in incoming[1:]:
        dnormed = dnormed + message[:, :channels].astype(F32)
    states = residuals[4].shape[2] * 2
    joined = incoming[0].shape[1] > channels
    if joined:
        place = slice(channels, channels + states)
        state = incoming[0][:, place].astype(F32)
        for hop in range(1, chunks):
            state = state + incoming[hop][:, place].astype(F32)
        share = states // chunks
        pieces = picked_members(chunks, state.astype(BF16))
        place = slice(channels + states, channels + states + channels // 2)
        for hop in range(chunks):
            piece = pieces[hop][:, :share]
            halves = [incoming[hop][start : start + share, place] for start in (0, share)]
            dnormed = dnormed + jnp.concatenate([dot_nn(piece, half) for half in halves], axis=1)
    main, state = mixer_back(heads, dnormed, residuals)
    if count > 1:
        done = lax.axis_index("pipe") > active
        main = jnp.where(done, refs[0][...], main)
        state = jnp.where(done, refs[1][...], state)
        refs = refs[2:]
    refs[0][...] = main
    refs[1][...] = state
    if count > 1:
        for ref, piece in zip(refs[2:], picked_members(chunks, state)):
            ref[...] = piece


def sum_pieces(pieces, width):
    total = pieces[0][...].astype(F32)
    for piece in pieces[1:]:
        total = total + piece[...].astype(F32)
    return total.astype(BF16)[:, :width]


def project_kernel(chunks, final, *refs):
    main_ref, refs = refs[0], refs[1:]
    pieces, refs = refs[:chunks], refs[chunks:]
    count = chunks if final else 0
    newest, refs = refs[:count], refs[count:]
    state_ref, refs = refs[0], refs[1:]
    if final:
        own_ref, other_ref, refs = refs[0], refs[1], refs[2:]
    step_rows_ref, cols_ref, refs = refs[0], refs[1], refs[2:]
    outs, refs = refs[:chunks], refs[chunks:]
    cols, sems = refs
    wide = cols.shape[2]
    heads = step_rows_ref.shape[0]
    me = lax.axis_index("tensor")
    width = cols.shape[1]
    places = []
    copies = []
    for hop in range(chunks):
        place = pl.ds(pl.multiple_of(lax.rem(me + hop, chunks) * width, width), width)
        copy = pltpu.make_async_copy(cols_ref.at[place, :], cols.at[hop], sems.at[hop])
        copy.start()
        places.append(place)
        copies.append(copy)
    main = main_ref[...]
    state = [sum_pieces(pieces, pieces[0].shape[1])]
    if final:
        nothing = jnp.zeros_like(state[0])
        first = lax.axis_index("pipe") == 0
        state = [
            jnp.where(first, piece[...], other)
            for piece, other in zip(newest, state + [nothing] * (chunks - 1))
        ]
    share = state_ref.shape[0]
    if final:
        others = jnp.concatenate([piece[:, :share] for piece in state[1:]], axis=1)
    core = lax.axis_index("dp")
    half = chunks // 2
    for hop in range(chunks):
        product = dot_nn(state[0][:, :share], state_ref[:, places[hop]])
        if final:
            chunk = lax.rem(me + hop, chunks)
            mine = chunk // half == core
            place = pl.ds(pl.multiple_of(lax.rem(chunk, half) * width, width), width)
            held = jnp.where(mine, own_ref[:, place], other_ref[:, place])
            product = product + jnp.where(first, dot_nn(others, held), 0.0)
        product = product + dot_nn(main[:, wide : wide + heads], step_rows_ref[:, places[hop]])
        copies[hop].wait()
        outs[hop][...] = (product + dot_nt(main[:, :wide], cols[hop])).astype(BF16)


def compose_kernel(half, *refs):
    rows, refs = refs[:half], refs[half:]
    cols_ref, step_rows_ref, state_ref, joint_ref, main_sum, maps_sum = refs
    wide = cols_ref.shape[1]
    heads = step_rows_ref.shape[0]
    step = pl.program_id(0)
    size = rows[0].shape[0]
    map_width = main_sum.shape[1]
    section = lax.axis_index("pipe")

    @pl.when((section > 0) & (section < lax.axis_size("pipe") - 1))
    def _():
        stacked = jnp.concatenate([row[...] for row in rows], axis=0)
        main = dot_nn(stacked, cols_ref[...])
        steps = dot_nt(stacked, step_rows_ref[...])
        maps = dot_nt(state_ref[...], stacked)

        @pl.when(step == 0)
        def _():
            main_sum[:, :wide] = main
            main_sum[:, wide:] = jnp.zeros_like(main_sum[:, wide:])
            main_sum[:, wide : wide + heads] = steps
            maps_sum[...] = maps

        @pl.when(step > 0)
        def _():
            main_sum[:, :wide] += main
            main_sum[:, wide : wide + heads] += steps
            maps_sum[...] += maps

        @pl.when(step == pl.num_programs(0) - 1)
        def _():
            for hop in range(half):
                joint_ref[:size, hop * map_width : (hop + 1) * map_width] = main_sum[
                    hop * size : (hop + 1) * size, :
                ].astype(BF16)
            joint_ref[size:, : half * size] = maps_sum[...].astype(BF16)


def by_hop(chunks, own, other):
    core = lax.axis_index("dp")
    half = chunks // 2
    return [
        jnp.where((core == 0) == (hop < half), own[hop % half], other[hop % half])
        for hop in range(chunks)
    ]


def send_kernel(chunks, ahead, main_ref, state_ref, *refs):
    others, refs = refs[: chunks - 1], refs[chunks - 1 :]
    sources, refs = refs[:2], refs[2:]
    outs, refs = refs[:chunks], refs[chunks:]
    held, sems = refs[-3:-1], refs[-1]
    half = chunks // 2
    map_width = main_ref.shape[1]
    states = state_ref.shape[1]
    share = states // chunks
    size = held[0].shape[0] - share
    copies = [
        pltpu.make_async_copy(source, place, sems.at[index])
        for index, (source, place) in enumerate(zip(sources, held))
    ]
    for copy in copies:
        copy.start()
    if ahead:
        stack_ref, map_ref = refs[:2]

        @pl.when(lax.axis_index("pipe") == 0)
        def _():
            for index, other in enumerate(others):
                stack_ref[index * share : (index + 1) * share, :] = other[...]

    main = main_ref[...]
    state = state_ref[...]
    if not ahead:
        pieces = picked_members(chunks, state)
    for copy in copies:
        copy.wait()

    def terms(joint):
        return [
            dot_nt(main, joint[:size, hop * map_width : (hop + 1) * map_width])
            for hop in range(half)
        ]

    def maps(joint):
        return [joint[size:, hop * size : (hop + 1) * size] for hop in range(half)]

    total = by_hop(chunks, terms(held[0]), terms(held[1]))
    kept = by_hop(chunks, maps(held[0]), maps(held[1]))
    if not ahead:
        for hop in range(chunks):
            total[hop] = total[hop] + dot_nn(pieces[0][:, :share], kept[hop])
        for away, other in enumerate(others, 1):
            term = dot_nn(pieces[away][:, :share], other[...])
            for hop in range(chunks):
                start = (hop + away) % chunks * size
                total[hop] = total[hop] + term[:, start : start + size]
    for hop in range(chunks):
        outs[hop][:, :size] = total[hop].astype(BF16)
        if ahead:
            map_ref[:, hop * size : (hop + 1) * size] = kept[hop]
            outs[hop][:, size : size + states] = state
            for part in range(2):
                outs[hop][part * share : (part + 1) * share, size + states :] = kept[hop][
                    :, part * (size // 2) : (part + 1) * (size // 2)
                ]


def carry_kernel(chunks, *refs):
    refs[-1][...] = sum_pieces(refs[:chunks], refs[0].shape[1])


def dnormed_kernel(chunks, *refs):
    incoming, refs = refs[:chunks], refs[chunks:]
    *sources, out_ref, rows, sem = refs
    core = lax.axis_index("dp")
    last = lax.axis_index("pipe") == lax.axis_size("pipe") - 1
    for lane, source in enumerate(sources):

        @pl.when(last & (core == lane))
        def _():
            copy = pltpu.make_async_copy(source, rows, sem)
            copy.start()
            copy.wait()

    @pl.when(last)
    def _():
        product = gathered_product(chunks, lax.axis_index("tensor"), incoming, rows)
        out_ref[...] = product.astype(BF16)


def gathered_product(chunks, me, incoming, rows):
    width = incoming[0].shape[1]
    total = None
    for hop in range(chunks):
        chunk = lax.rem(me + chunks - hop, chunks)
        term = dot_nt(
            incoming[hop][...], rows[:, pl.ds(pl.multiple_of(chunk * width, width), width)]
        )
        total = term if total is None else total + term
    return total


def after(value, dependency):
    return lax.optimization_barrier((value, dependency))[0]


def kernel_params():
    return pltpu.CompilerParams(vmem_limit_bytes=VMEM_BYTES)


def whole(count):
    return [pl.BlockSpec(memory_space=SPACE)] * count


def section_pairs(sections, chunks, source, target, hop):
    return [
        (source * chunks + index, target * chunks + (index + hop) % chunks)
        for index in range(chunks)
    ]


def relay_body(
    weight_main,
    weight_state,
    weight_step,
    weight_out,
    conv_main,
    conv_state,
    step_bias,
    decay_log,
    skip_gain,
    norm_gain,
    saved_main,
    saved_state,
    saved_step,
    output_grad,
):
    sections = lax.axis_size("pipe")
    chunks = lax.axis_size("tensor")
    section = lax.axis_index("pipe")
    me = lax.axis_index("tensor")
    core = lax.axis_index("dp")
    length, width = output_grad.shape
    model_width = weight_out.shape[2]
    heads = step_bias.shape[1]
    channels = weight_out.shape[1]
    place = ("pipe", "tensor")

    def within(active, hop):
        return section_pairs(sections, chunks, active, active, hop)

    half = chunks // 2

    def rows_up(hop):
        pairs = []
        for source in range(sections - 1):
            for index in range(chunks):
                for lane in range(2):
                    move = hop + lane * half
                    if source == sections - 2:
                        if lane != hop:
                            continue
                        move = 0
                    start = (source * chunks + index) * 2 + lane
                    target = (source + 1) * chunks + (index + move) % chunks
                    pairs.append((start, target * 2 + lane))
        return pairs

    everywhere = ("pipe", "tensor", "dp")

    def swap(value, sections_in):
        pairs = []
        for source in sections_in:
            for start in range(source * chunks * 2, (source + 1) * chunks * 2):
                pairs.append((start, start ^ 1))
        return lax.ppermute(value, everywhere, pairs)

    far_first = sorted(range(1, chunks), key=lambda hop: -min(hop, chunks - hop))

    def exchange(values, sections_in):
        moved = [values[0]] * chunks
        for hop in far_first:
            pairs = []
            for source in sections_in:
                pairs += within(source, hop)
            moved[hop] = lax.ppermute(values[hop], place, pairs)
        return moved

    incoming = exchange([output_grad] * chunks, [sections - 1])

    rows = [lax.ppermute(weight_out[0], everywhere, rows_up(hop)) for hop in range(half)]
    lanes = ((0, 0), (0, 128 - heads))
    by_head = jnp.pad(
        jnp.stack([step_bias[0], decay_log[0], skip_gain[0]]), ((0, 5), (0, 128 - heads))
    )
    steps = jnp.pad(saved_step[0].astype(F32).T, lanes)
    taps_main = conv_main[0]
    taps_state = conv_state[0].reshape(conv_state.shape[1], -1)
    state_width = taps_state.shape[1]
    residual_shapes = (
        jax.ShapeDtypeStruct((9, length, channels), F32),
        jax.ShapeDtypeStruct((2, length, heads * length), F32),
        jax.ShapeDtypeStruct((length, heads * length), BF16),
        jax.ShapeDtypeStruct((heads * length, channels), BF16),
        jax.ShapeDtypeStruct((2, length, state_width // 2), BF16),
        jax.ShapeDtypeStruct((length, 128), F32),
    )
    residuals = pl.pallas_call(
        lambda *refs: forward_kernel(heads, *refs),
        out_shape=residual_shapes,
        in_specs=whole(8),
        out_specs=whole(6),
        compiler_params=kernel_params(),
        name="forward_residuals",
    )(
        saved_main[0, :, 0],
        saved_main[0, :, 1],
        saved_state[0].reshape(length, -1),
        steps,
        taps_main,
        taps_state,
        by_head,
        norm_gain,
    )
    residuals = tuple(residuals) + (taps_main, taps_state, by_head)
    slice_out = jax.ShapeDtypeStruct((length, channels), BF16)
    message = jax.ShapeDtypeStruct((length, width), BF16)
    map_width = 2 * channels + 128
    main_shape = jax.ShapeDtypeStruct((length, map_width), BF16)
    piece_shape = jax.ShapeDtypeStruct((length, 128), BF16)
    hbm = pl.BlockSpec(memory_space=pl.ANY)
    main_cols = weight_main[0].reshape(model_width, -1)
    step_rows = weight_step[0]
    residuals = residuals[:-1] + (after(by_head, main_cols),)

    main, *pieces = pl.pallas_call(
        lambda *refs: first_kernel(heads, chunks, *refs),
        out_shape=(main_shape,) + (piece_shape,) * chunks,
        in_specs=whole(chunks + 10),
        out_specs=whole(1 + chunks),
        compiler_params=kernel_params(),
        name="section_first",
    )(*incoming, weight_out[0], *residuals)

    def project_call(main, pieces, newest=(), others=()):
        return pl.pallas_call(
            lambda *refs: project_kernel(chunks, bool(others), *refs),
            out_shape=(message,) * chunks,
            in_specs=whole(3 + chunks + len(newest) + len(others)) + [hbm],
            out_specs=whole(chunks),
            scratch_shapes=[
                pltpu.VMEM((chunks, width, 2 * channels), BF16),
                pltpu.SemaphoreType.DMA((chunks,)),
            ],
            compiler_params=kernel_params(),
            name="project",
        )(main, *pieces, *newest, state_cols, *others, step_rows, main_cols)

    pieces = exchange(pieces, [sections - 1])
    state_cols = after(weight_state[0], main).reshape(model_width, -1).T
    state_share = state_cols.shape[0]
    parts = project_call(main, pieces)
    exchanged = exchange(parts, [sections - 1])

    grid_steps = 2
    depth = model_width // grid_steps
    rows_spec = pl.BlockSpec((channels, depth), lambda step: (0, step))
    def pass_back(messages, active):
        moved = []
        for hop in range(chunks):
            pairs = section_pairs(sections, chunks, active, active - 1, chunks - hop)
            moved.append(lax.ppermute(messages[hop], place, pairs))
        return moved

    result = pl.pallas_call(
        lambda *refs: carry_kernel(chunks, *refs),
        out_shape=message,
        in_specs=whole(chunks),
        out_specs=pl.BlockSpec(memory_space=SPACE),
        compiler_params=kernel_params(),
        name="carry_next",
    )(*exchanged)
    exchanged = exchange([result] * chunks, [sections - 1])
    dnormed = pl.pallas_call(
        lambda *refs: dnormed_kernel(chunks, *refs),
        out_shape=slice_out,
        in_specs=whole(chunks) + [hbm] * 2,
        out_specs=pl.BlockSpec(memory_space=SPACE),
        scratch_shapes=[
            pltpu.VMEM((channels, model_width), BF16),
            pltpu.SemaphoreType.DMA,
        ],
        compiler_params=kernel_params(),
        name="dnormed_back",
    )(*exchanged, *rows)
    pairs = section_pairs(sections, chunks, sections - 1, sections - 2, 0)
    incoming = [lax.ppermute(dnormed, place, pairs)]
    joint_shape = jax.ShapeDtypeStruct((channels + state_share, half * map_width), BF16)
    joint = pl.pallas_call(
        lambda *refs: compose_kernel(half, *refs),
        grid=(grid_steps,),
        out_shape=joint_shape,
        in_specs=[rows_spec] * half
        + [pl.BlockSpec((depth, 2 * channels), lambda step: (step, 0))]
        + [pl.BlockSpec((count, depth), lambda step: (0, step)) for count in (heads, state_share)],
        out_specs=pl.BlockSpec(joint_shape.shape, lambda step: (0, 0)),
        scratch_shapes=[
            pltpu.VMEM((half * channels, map_width), F32),
            pltpu.VMEM((state_share, half * channels), F32),
        ],
        compiler_params=kernel_params(),
        name="compose_weights",
    )(*rows[:-1], after(rows[-1], dnormed), main_cols, step_rows, state_cols)

    half_cols = lax.dynamic_slice_in_dim(
        after(state_cols, parts[0]), core * (model_width // 2), model_width // 2, 1
    )
    residuals = residuals[:-1] + (after(by_head, (joint, half_cols)),)

    state_shape = jax.ShapeDtypeStruct((length, state_width), BF16)
    joined = jax.ShapeDtypeStruct((length, channels + state_width + channels // 2), BF16)
    assert 2 * state_share == length

    def next_call(incoming, kept, active):
        count = chunks if len(incoming) > 1 else 0
        main, state, *pieces = pl.pallas_call(
            lambda *refs: next_kernel(heads, chunks, len(incoming), active, *refs),
            out_shape=(main_shape, state_shape) + (piece_shape,) * count,
            in_specs=whole(len(incoming) + 9 + len(kept)),
            out_specs=whole(2 + count),
            compiler_params=kernel_params(),
            name="section_next",
        )(*incoming, *residuals, *kept)
        return (main, state), pieces

    joint_other = None
    kept = ()
    summed = None
    for active in range(sections - 2, -1, -1):
        kept, pieces = next_call(incoming, kept, active)
        if active == 0:
            break
        if joint_other is None:
            joint_other = swap(after(joint, kept[0]), range(1, sections - 1))
        ahead = active == sections - 2
        if ahead:
            late = after(half_cols, kept[0])
            others = [
                lax.ppermute(late, place, within(0, chunks - away)) for away in range(1, chunks)
            ]
            stack = jax.ShapeDtypeStruct(((chunks - 1) * state_share, model_width // 2), BF16)
            state_map = jax.ShapeDtypeStruct((state_share, chunks * channels), BF16)
            outs = (joined,) * chunks + (stack, state_map)
        else:
            outs = (slice_out,) * chunks
        messages = pl.pallas_call(
            lambda *refs: send_kernel(chunks, ahead, *refs),
            out_shape=outs,
            in_specs=whole(2 + len(others)) + [hbm] * 2,
            out_specs=whole(len(outs)),
            scratch_shapes=[pltpu.VMEM(joint_shape.shape, BF16)] * 2
            + [pltpu.SemaphoreType.DMA((2,))],
            compiler_params=kernel_params(),
            name="send_ahead" if ahead else "send_back",
        )(*kept, *others, joint, joint_other)
        incoming = pass_back(messages, active)
        if ahead:
            stack, late = messages[chunks], after(messages[chunks + 1], incoming[0])
            others = [
                lax.ppermute(late, place, within(1, chunks - away)) for away in range(1, chunks)
            ]
        else:
            shared = (stack, swap(after(stack, messages[0]), [0]))
            summed = exchange(after(pieces, incoming[0]), range(1, sections - 1))

    parts = project_call(kept[0], summed, pieces, shared)
    exchanged = exchange(parts, range(sections - 1))
    total = exchanged[0].astype(F32)
    for part in exchanged[1:]:
        total = total + part.astype(F32)
    return jnp.where(section == sections - 1, result, total.astype(BF16))[None]


def solution(mesh):
    narrow = mesh.shape["tensor"] == GROUP_SPAN
    return jax.shard_map(
        relay_body if narrow else wide_body,
        mesh=mesh,
        in_specs=(
            P("pipe", None, None, "tensor"),
            P("pipe", None, None, "tensor"),
            P("pipe", "tensor", None),
            P("pipe", "tensor", None),
            P("pipe", None, "tensor"),
            P("pipe", None, None, None),
            P("pipe", "tensor"),
            P("pipe", "tensor"),
            P("pipe", "tensor"),
            P("pipe", "tensor"),
            P("pipe", "dp", None, "tensor"),
            P("pipe", "dp", None, None),
            P("pipe", "tensor", "dp"),
            P("dp", "tensor"),
        ),
        out_specs=P("pipe", "dp", "tensor"),
        check_vma=False,
    )
```

```python
import jax
import jax.numpy as jnp
from jax import lax
from jax.experimental import pallas as pl
from jax.experimental.pallas import tpu as pltpu
from jax.sharding import PartitionSpec as P

NSTATE = 128
GROUP_SPAN = 4
STRETCH = 128


EPSILON = 1e-05
HIGHEST = lax.Precision.HIGHEST


def from_partner(value, axis, bit):
    mask = 2**bit
    pairs = [(source, source ^ mask) for source in range(lax.axis_size(axis))]
    return lax.ppermute(value, axis, pairs)


def passed_along(value, axis, steps):
    count = lax.axis_size(axis)
    leading, last = (max(0, -steps), min(count, count - steps))
    return lax.ppermute(value, axis, [(source, source + steps) for source in range(leading, last)])


def causal_conv(signal, kernel):
    taps = kernel.shape[0]
    length = signal.shape[0]
    padded = jnp.pad(signal, ((taps - 1, 0), (0, 0)))
    summed = kernel[0] * padded[0:length]
    for offset in range(1, taps):
        summed = summed + kernel[offset] * padded[offset : offset + length]
    return summed


def state_space(values, step_sizes, decay_rates, inputs, readout):
    length, head_count, head_size = values.shape
    blocks = length // STRETCH
    state_width = inputs.shape[1]
    decays = (step_sizes * decay_rates[:, None]).reshape(head_count, blocks, STRETCH)
    running = jnp.cumsum(decays, axis=2)
    scaled = (values * step_sizes.T[:, :, None]).reshape(blocks, STRETCH, head_count, head_size)
    inputs_blocked = inputs.reshape(blocks, STRETCH, state_width)
    readout_blocked = readout.reshape(blocks, STRETCH, state_width)
    scores = jnp.einsum("cin,cjn->cij", readout_blocked, inputs_blocked, precision=HIGHEST)
    position = jnp.arange(STRETCH)
    causal = position[:, None] >= position[None, :]
    differ = running[:, :, :, None] - running[:, :, None, :]
    weights = jnp.where(causal, jnp.exp(jnp.where(causal, differ, 0.0)), 0.0) * scores[None]
    within = jnp.einsum("hcij,cjhp->cihp", weights, scaled, precision=HIGHEST)
    tail_decay = jnp.exp(running[:, :, -1:] - running)
    weighted = scaled * jnp.transpose(tail_decay, (1, 2, 0))[:, :, :, None]
    block_sums = jnp.einsum("cjhp,cjn->chpn", weighted, inputs_blocked, precision=HIGHEST)
    shrinks = jnp.exp(running[:, :, -1]).T

    def advance(carried, item):
        newest, shrink = item
        return (carried * shrink[:, None, None] + newest, carried)

    anchor = jnp.zeros((head_count, head_size, state_width), jnp.float32)
    _, entering = lax.scan(advance, anchor, (block_sums, shrinks))
    across = jnp.einsum("cin,chpn->cihp", readout_blocked, entering, precision=HIGHEST)
    across = across * jnp.transpose(jnp.exp(running), (1, 2, 0))[:, :, :, None]
    return (within + across).reshape(length, head_count, head_size)


def mamba_mixer(
    main_proj,
    state_proj,
    step_proj,
    conv_main,
    conv_state,
    step_bias,
    decay_log,
    skip_gain,
    norm_gain,
):
    length = main_proj.shape[0]
    head_count = step_proj.shape[0]
    gating = main_proj[:, 0]
    mixed_in = jax.nn.silu(causal_conv(main_proj[:, 1], conv_main))
    flat_state = state_proj.reshape(length, -1)
    state_conv = jax.nn.silu(
        causal_conv(flat_state, conv_state.reshape(conv_state.shape[0], -1))
    ).reshape(length, 2, -1)
    step_sizes = jax.nn.softplus(step_proj + step_bias[:, None])
    decay_rates = -jnp.exp(decay_log)
    values = mixed_in.reshape(length, head_count, -1)
    scanned = state_space(values, step_sizes, decay_rates, state_conv[:, 0], state_conv[:, 1])
    scanned = scanned + skip_gain[None, :, None] * values
    gated = scanned.reshape(length, -1) * jax.nn.silu(gating)
    inverse = lax.rsqrt(jnp.mean(gated * gated, axis=1, keepdims=True) + EPSILON)
    return gated * inverse * norm_gain


def wide_body(
    weight_main,
    weight_state,
    weight_step,
    weight_out,
    conv_main,
    conv_state,
    step_bias,
    decay_log,
    skip_gain,
    norm_gain,
    saved_main,
    saved_state,
    saved_step,
    output_grad,
):
    sections = lax.axis_size("pipe")
    section = lax.axis_index("pipe")
    tensor_index = lax.axis_index("tensor")
    member = tensor_index % GROUP_SPAN
    group = tensor_index // GROUP_SPAN
    span_bits = GROUP_SPAN.bit_length() - 1
    length = saved_main.shape[1]
    col_count = output_grad.shape[1]
    model_width = weight_out.shape[2]
    main_cols = weight_main[0].reshape(model_width, -1)
    state_cols = weight_state[0].reshape(model_width, -1)
    step_rows = weight_step[0]
    out_rows = weight_out[0]
    state_group = lax.dynamic_slice_in_dim(saved_state[0], group * NSTATE, NSTATE, 2)
    conv_group = lax.dynamic_slice_in_dim(conv_state[0], group * NSTATE, NSTATE, 2)

    def local_mixer(first_in, second_in, third_in):
        return mamba_mixer(
            first_in,
            second_in,
            third_in,
            conv_main[0],
            conv_group,
            step_bias[0],
            decay_log[0],
            skip_gain[0],
            norm_gain[0],
        )

    _, pullback = jax.vjp(
        local_mixer,
        saved_main[0].astype(jnp.float32),
        state_group.astype(jnp.float32),
        saved_step[0].astype(jnp.float32),
    )
    result = jnp.zeros((length, col_count), jnp.bfloat16)
    incoming = output_grad
    for moment in range(sections):
        back_grad_main, back_grad_state, back_grad_step = pullback(
            lax.dot_general(
                lax.all_gather(incoming, "tensor", axis=1, tiled=True),
                out_rows,
                (((1,), (1,)), ((), ())),
                preferred_element_type=jnp.float32,
            )
        )
        kept = back_grad_state
        for bit in range(span_bits - 1, -1, -1):
            half = kept.shape[2] // 2
            lower = kept[:, :, :half]
            upper = kept[:, :, half:]
            high = member // 2**bit % 2 == 1
            own = jnp.where(high, upper, lower)
            other = jnp.where(high, lower, upper)
            kept = own + from_partner(other, "tensor", bit)
        grad_main = back_grad_main.astype(jnp.bfloat16).reshape(length, -1)
        grad_state = kept.astype(jnp.bfloat16).reshape(length, -1)
        grad_step = back_grad_step.astype(jnp.bfloat16)
        summed = lax.dot_general(
            main_cols, grad_main, (((1,), (1,)), ((), ())), preferred_element_type=jnp.float32
        )
        summed = summed + lax.dot_general(
            state_cols, grad_state, (((1,), (1,)), ((), ())), preferred_element_type=jnp.float32
        )
        owned = lax.psum_scatter(
            summed
            + lax.dot_general(
                step_rows, grad_step, (((0,), (0,)), ((), ())), preferred_element_type=jnp.float32
            ),
            "tensor",
            scatter_dimension=0,
            tiled=True,
        ).T.astype(jnp.bfloat16)
        result = jnp.where(section == sections - 1 - moment, owned, result)
        if moment + 1 < sections:
            incoming = passed_along(owned, "pipe", -1)
    return result[None]


BF16 = jnp.bfloat16
F32 = jnp.float32
SPACE = pltpu.VMEM
VMEM_BYTES = 28 * 2**20


def dot_nt(left, right, **options):
    return lax.dot_general(
        left, right, (((1,), (1,)), ((), ())), preferred_element_type=F32, **options
    )


def dot_tn(left, right):
    return lax.dot_general(left, right, (((0,), (0,)), ((), ())), preferred_element_type=F32)


def dot_nn(left, right, **options):
    return jnp.dot(left, right, preferred_element_type=F32, **options)


def iota(shape, dim):
    return lax.broadcasted_iota(jnp.int32, shape, dim)


def head_lanes(shape, head, size):
    lane = iota(shape, 1)
    return (lane >= head * size) & (lane < (head + 1) * size)


def conv_taps(signal, taps):
    count = taps.shape[0]
    row = iota(signal.shape, 0)
    total = taps[count - 1 : count] * signal
    for back in range(1, count):
        moved = jnp.where(row >= back, pltpu.roll(signal, back, 0), 0.0)
        total = total + taps[count - 1 - back : count - back] * moved
    return total


def conv_taps_back(grad, taps):
    count = taps.shape[0]
    length = grad.shape[0]
    row = iota(grad.shape, 0)
    total = taps[count - 1 : count] * grad
    for ahead in range(1, count):
        moved = jnp.where(row < length - ahead, pltpu.roll(grad, length - ahead, 0), 0.0)
        total = total + taps[count - 1 - ahead : count - ahead] * moved
    return total


def silu_and_slope(value):
    gate = jax.nn.sigmoid(value)
    return value * gate, gate * (1.0 + value * (1.0 - gate))


def forward_kernel(
    heads,
    gate_ref,
    mixer_ref,
    state_ref,
    step_ref,
    taps_main_ref,
    taps_state_ref,
    heads_ref,
    gain_ref,
    maps_ref,
    decay_ref,
    decayed_ref,
    values_ref,
    state_out_ref,
    slope_ref,
):
    length, channels = gate_ref.shape
    size = channels // heads
    states = state_ref.shape[1] // 2
    gate, gate_slope = silu_and_slope(gate_ref[...].astype(F32))
    value, value_slope = silu_and_slope(
        conv_taps(mixer_ref[...].astype(F32), taps_main_ref[...])
    )
    state, state_slope = silu_and_slope(
        conv_taps(state_ref[...].astype(F32), taps_state_ref[...])
    )
    inputs = state[:, :states]
    readout = state[:, states:]
    raw_step = step_ref[...] + heads_ref[0:1]
    step = jnp.maximum(raw_step, 0.0) + jnp.log1p(jnp.exp(-jnp.abs(raw_step)))
    slope_ref[...] = jax.nn.sigmoid(raw_step)
    rate = -jnp.exp(heads_ref[1:2])
    square = (length, length)
    later = iota(square, 0) >= iota(square, 1)
    earlier = iota(square, 0) <= iota(square, 1)
    running = dot_nn(later.astype(F32), step * rate, precision=HIGHEST)
    running_row = running.T
    scores = dot_nt(readout, inputs, precision=HIGHEST)
    scores_back = dot_nt(inputs, readout, precision=HIGHEST)
    wide = (length, channels)
    step_wide = jnp.zeros(wide, F32)
    skip_wide = jnp.zeros(wide, F32)
    for head in range(heads):
        lanes = head_lanes(wide, head, size)
        step_wide = jnp.where(lanes, step[:, head : head + 1], step_wide)
        skip_wide = jnp.where(lanes, heads_ref[2:3, head : head + 1], skip_wide)
    scaled = value * step_wide
    output = skip_wide * value
    for head in range(heads):
        lanes = head_lanes(wide, head, size)
        columns = pl.ds(head * length, length)
        column = running[:, head : head + 1]
        row = running_row[head : head + 1, :]
        decay = jnp.where(later, jnp.exp(jnp.where(later, column - row, 0.0)), 0.0)
        back = jnp.where(earlier, jnp.exp(jnp.where(earlier, row - column, 0.0)), 0.0)
        weights = decay * scores
        own = jnp.where(lanes, scaled, 0.0)
        output = output + dot_nn(weights, own, precision=HIGHEST)
        decay_ref[0, :, columns] = decay
        decay_ref[1, :, columns] = weights
        decayed_ref[:, columns] = (back * scores_back).astype(BF16)
        values_ref[columns, :] = own.astype(BF16)
    gated = output * gate
    inverse = lax.rsqrt(jnp.mean(gated * gated, axis=1, keepdims=True) + EPSILON)
    gain = gain_ref[...]
    normal = gated * inverse
    maps_ref[0] = gain * inverse
    maps_ref[1] = normal * inverse
    maps_ref[2] = gain * normal * (1.0 / channels)
    maps_ref[3] = gate
    maps_ref[4] = output * gate_slope
    maps_ref[5] = skip_wide * value_slope
    maps_ref[6] = step_wide * value_slope
    maps_ref[7] = value
    maps_ref[8] = state_slope
    state_out_ref[0] = inputs.astype(BF16)
    state_out_ref[1] = readout.astype(BF16)


def mixer_back(heads, dnormed, residuals):
    (
        maps_ref,
        decay_ref,
        decayed_ref,
        values_ref,
        state_ref,
        slope_ref,
        taps_main_ref,
        taps_state_ref,
        heads_ref,
    ) = residuals
    length, channels = dnormed.shape
    size = channels // heads
    shared = jnp.sum(dnormed * maps_ref[2], axis=1, keepdims=True)
    d_gated = dnormed * maps_ref[0] - maps_ref[1] * shared
    d_output = d_gated * maps_ref[3]
    d_gate = d_gated * maps_ref[4]
    by_head = jnp.concatenate(
        [
            jnp.where(head_lanes(d_output.shape, head, size), d_output, 0.0).astype(BF16)
            for head in range(heads)
        ],
        axis=0,
    )
    d_scaled = dot_nn(decayed_ref[...], by_head)
    d_weights = dot_nt(d_output.astype(BF16), values_ref[...])
    d_decayed = d_weights * decay_ref[0]
    d_scores = d_decayed[:, :length]
    for head in range(1, heads):
        d_scores = d_scores + d_decayed[:, head * length : (head + 1) * length]
    d_exponent = d_weights * decay_ref[1]
    square = (length, length)
    onward = (iota(square, 0) <= iota(square, 1)).astype(BF16)
    spanning = dot_nn(onward, d_exponent.astype(BF16))
    row = iota(spanning.shape, 0)
    source = iota(spanning.shape, 1) % length
    spanning = jnp.where(source < row, spanning, 0.0)
    lane = iota((channels, 128), 1)
    of_channel = (iota((channels, 128), 0) // size == lane).astype(BF16)
    of_source = (
        iota((heads * length, 128), 0) // length == iota((heads * length, 128), 1)
    ).astype(BF16)
    rate = -jnp.exp(heads_ref[1:2])
    d_step = dot_nn((d_scaled * maps_ref[7]).astype(BF16), of_channel)
    d_step = d_step + rate * dot_nn(spanning.astype(BF16), of_source)
    d_step = d_step * slope_ref[...]
    rounded = d_scores.astype(BF16)
    d_readout = dot_nn(rounded, state_ref[0])
    d_inputs = dot_tn(rounded, state_ref[1])
    d_state = jnp.concatenate([d_inputs, d_readout], axis=1) * maps_ref[8]
    d_mixer = d_output * maps_ref[5] + d_scaled * maps_ref[6]
    main = jnp.concatenate(
        [
            d_gate.astype(BF16),
            conv_taps_back(d_mixer, taps_main_ref[...]).astype(BF16),
            d_step.astype(BF16),
        ],
        axis=1,
    )
    return main, conv_taps_back(d_state, taps_state_ref[...]).astype(BF16)


def picked_members(chunks, state):
    me = lax.axis_index("tensor")
    states = state.shape[1] // 2
    share = states // chunks
    shape = (state.shape[1], 128)
    row = iota(shape, 0)
    lane = iota(shape, 1)
    source = jnp.where(lane < share, lane, lane + states - share)
    pieces = []
    for hop in range(chunks):
        member = lax.rem(me + hop, chunks)
        picked = (row == source + member * share) & (lane < 2 * share)
        pieces.append(dot_nn(state, picked.astype(BF16)).astype(BF16))
    return pieces


def first_kernel(heads, chunks, *refs):
    incoming, refs = refs[:chunks], refs[chunks:]
    rows_ref, refs = refs[0], refs[1:]
    residuals, refs = refs[:9], refs[9:]
    main_ref, outs = refs[0], refs[1:]
    dnormed = gathered_product(chunks, lax.axis_index("tensor"), incoming, rows_ref)
    main, state = mixer_back(heads, dnormed, residuals)
    main_ref[...] = main
    for out, piece in zip(outs, picked_members(chunks, state)):
        out[...] = piece


def next_kernel(heads, chunks, count, active, *refs):
    incoming, refs = refs[:count], refs[count:]
    residuals, refs = refs[:9], refs[9:]
    channels = residuals[0].shape[2]
    dnormed = incoming[0][:, :channels].astype(F32)
    for message in incoming[1:]:
        dnormed = dnormed + message[:, :channels].astype(F32)
    states = residuals[4].shape[2] * 2
    joined = incoming[0].shape[1] > channels
    if joined:
        place = slice(channels, channels + states)
        state = incoming[0][:, place].astype(F32)
        for hop in range(1, chunks):
            state = state + incoming[hop][:, place].astype(F32)
        share = states // chunks
        pieces = picked_members(chunks, state.astype(BF16))
        place = slice(channels + states, channels + states + channels // 2)
        for hop in range(chunks):
            piece = pieces[hop][:, :share]
            halves = [incoming[hop][start : start + share, place] for start in (0, share)]
            dnormed = dnormed + jnp.concatenate([dot_nn(piece, half) for half in halves], axis=1)
    main, state = mixer_back(heads, dnormed, residuals)
    if count > 1:
        done = lax.axis_index("pipe") > active
        main = jnp.where(done, refs[0][...], main)
        state = jnp.where(done, refs[1][...], state)
        refs = refs[2:]
    refs[0][...] = main
    refs[1][...] = state
    if count > 1:
        for ref, piece in zip(refs[2:], picked_members(chunks, state)):
            ref[...] = piece


def sum_pieces(pieces, width):
    total = pieces[0][...].astype(F32)
    for piece in pieces[1:]:
        total = total + piece[...].astype(F32)
    return total.astype(BF16)[:, :width]


def project_kernel(chunks, final, *refs):
    main_ref, refs = refs[0], refs[1:]
    pieces, refs = refs[:chunks], refs[chunks:]
    count = chunks if final else 0
    newest, refs = refs[:count], refs[count:]
    state_ref, refs = refs[0], refs[1:]
    if final:
        own_ref, other_ref, refs = refs[0], refs[1], refs[2:]
    step_rows_ref, cols_ref, refs = refs[0], refs[1], refs[2:]
    outs, refs = refs[:chunks], refs[chunks:]
    cols, sems = refs
    wide = cols.shape[2]
    heads = step_rows_ref.shape[0]
    me = lax.axis_index("tensor")
    width = cols.shape[1]
    places = []
    copies = []
    for hop in range(chunks):
        place = pl.ds(pl.multiple_of(lax.rem(me + hop, chunks) * width, width), width)
        copy = pltpu.make_async_copy(cols_ref.at[place, :], cols.at[hop], sems.at[hop])
        copy.start()
        places.append(place)
        copies.append(copy)
    main = main_ref[...]
    state = [sum_pieces(pieces, pieces[0].shape[1])]
    if final:
        nothing = jnp.zeros_like(state[0])
        first = lax.axis_index("pipe") == 0
        state = [
            jnp.where(first, piece[...], other)
            for piece, other in zip(newest, state + [nothing] * (chunks - 1))
        ]
    share = state_ref.shape[0]
    if final:
        others = jnp.concatenate([piece[:, :share] for piece in state[1:]], axis=1)
    core = lax.axis_index("dp")
    half = chunks // 2
    for hop in range(chunks):
        product = dot_nn(state[0][:, :share], state_ref[:, places[hop]])
        if final:
            chunk = lax.rem(me + hop, chunks)
            mine = chunk // half == core
            place = pl.ds(pl.multiple_of(lax.rem(chunk, half) * width, width), width)
            held = jnp.where(mine, own_ref[:, place], other_ref[:, place])
            product = product + jnp.where(first, dot_nn(others, held), 0.0)
        product = product + dot_nn(main[:, wide : wide + heads], step_rows_ref[:, places[hop]])
        copies[hop].wait()
        outs[hop][...] = (product + dot_nt(main[:, :wide], cols[hop])).astype(BF16)


def compose_kernel(half, *refs):
    rows, refs = refs[:half], refs[half:]
    cols_ref, step_rows_ref, state_ref, joint_ref, main_sum, maps_sum = refs
    wide = cols_ref.shape[1]
    heads = step_rows_ref.shape[0]
    step = pl.program_id(0)
    size = rows[0].shape[0]
    map_width = main_sum.shape[1]
    section = lax.axis_index("pipe")

    @pl.when((section > 0) & (section < lax.axis_size("pipe") - 1))
    def _():
        stacked = jnp.concatenate([row[...] for row in rows], axis=0)
        main = dot_nn(stacked, cols_ref[...])
        small = jnp.concatenate([state_ref[...], step_rows_ref[...]], axis=0)
        product = dot_nt(stacked, small)
        maps = product[:, : state_ref.shape[0]]
        steps = product[:, state_ref.shape[0] :]

        @pl.when(step == 0)
        def _():
            main_sum[:, :wide] = main
            main_sum[:, wide:] = jnp.zeros_like(main_sum[:, wide:])
            main_sum[:, wide : wide + heads] = steps
            maps_sum[...] = maps

        @pl.when(step > 0)
        def _():
            main_sum[:, :wide] += main
            main_sum[:, wide : wide + heads] += steps
            maps_sum[...] += maps

        @pl.when(step == pl.num_programs(0) - 1)
        def _():
            for hop in range(half):
                joint_ref[:size, hop * map_width : (hop + 1) * map_width] = main_sum[
                    hop * size : (hop + 1) * size, :
                ].astype(BF16)
            joint_ref[size:, : half * size] = maps_sum[...].T.astype(BF16)


def by_hop(chunks, own, other):
    core = lax.axis_index("dp")
    half = chunks // 2
    return [
        jnp.where((core == 0) == (hop < half), own[hop % half], other[hop % half])
        for hop in range(chunks)
    ]


def send_kernel(chunks, ahead, main_ref, state_ref, *refs):
    others, refs = refs[: chunks - 1], refs[chunks - 1 :]
    sources, refs = refs[:2], refs[2:]
    outs, refs = refs[:chunks], refs[chunks:]
    held, sems = refs[-3:-1], refs[-1]
    half = chunks // 2
    map_width = main_ref.shape[1]
    states = state_ref.shape[1]
    share = states // chunks
    size = held[0].shape[0] - share
    copies = [
        pltpu.make_async_copy(source, place, sems.at[index])
        for index, (source, place) in enumerate(zip(sources, held))
    ]
    for copy in copies:
        copy.start()
    if ahead:
        stack_ref, map_ref = refs[:2]

        @pl.when(lax.axis_index("pipe") == 0)
        def _():
            for index, other in enumerate(others):
                stack_ref[index * share : (index + 1) * share, :] = other[...]

    main = main_ref[...]
    state = state_ref[...]
    if not ahead:
        pieces = picked_members(chunks, state)
    for copy in copies:
        copy.wait()

    def terms(joint):
        return [
            dot_nt(main, joint[:size, hop * map_width : (hop + 1) * map_width])
            for hop in range(half)
        ]

    def maps(joint):
        return [joint[size:, hop * size : (hop + 1) * size] for hop in range(half)]

    total = by_hop(chunks, terms(held[0]), terms(held[1]))
    kept = by_hop(chunks, maps(held[0]), maps(held[1]))
    if not ahead:
        for hop in range(chunks):
            total[hop] = total[hop] + dot_nn(pieces[0][:, :share], kept[hop])
        for away, other in enumerate(others, 1):
            term = dot_nn(pieces[away][:, :share], other[...])
            for hop in range(chunks):
                start = (hop + away) % chunks * size
                total[hop] = total[hop] + term[:, start : start + size]
    for hop in range(chunks):
        outs[hop][:, :size] = total[hop].astype(BF16)
        if ahead:
            map_ref[:, hop * size : (hop + 1) * size] = kept[hop]
            outs[hop][:, size : size + states] = state
            for part in range(2):
                outs[hop][part * share : (part + 1) * share, size + states :] = kept[hop][
                    :, part * (size // 2) : (part + 1) * (size // 2)
                ]


def carry_kernel(chunks, *refs):
    refs[-1][...] = sum_pieces(refs[:chunks], refs[0].shape[1])


def dnormed_kernel(chunks, *refs):
    incoming, refs = refs[:chunks], refs[chunks:]
    *sources, out_ref, rows, sem = refs
    core = lax.axis_index("dp")
    last = lax.axis_index("pipe") == lax.axis_size("pipe") - 1
    for lane, source in enumerate(sources):

        @pl.when(last & (core == lane))
        def _():
            copy = pltpu.make_async_copy(source, rows, sem)
            copy.start()
            copy.wait()

    @pl.when(last)
    def _():
        product = gathered_product(chunks, lax.axis_index("tensor"), incoming, rows)
        out_ref[...] = product.astype(BF16)


def gathered_product(chunks, me, incoming, rows):
    width = incoming[0].shape[1]
    total = None
    for hop in range(chunks):
        chunk = lax.rem(me + chunks - hop, chunks)
        term = dot_nt(
            incoming[hop][...], rows[:, pl.ds(pl.multiple_of(chunk * width, width), width)]
        )
        total = term if total is None else total + term
    return total


def after(value, dependency):
    return lax.optimization_barrier((value, dependency))[0]


def kernel_params():
    return pltpu.CompilerParams(vmem_limit_bytes=VMEM_BYTES)


def whole(count):
    return [pl.BlockSpec(memory_space=SPACE)] * count


def section_pairs(sections, chunks, source, target, hop):
    return [
        (source * chunks + index, target * chunks + (index + hop) % chunks)
        for index in range(chunks)
    ]


def relay_body(
    weight_main,
    weight_state,
    weight_step,
    weight_out,
    conv_main,
    conv_state,
    step_bias,
    decay_log,
    skip_gain,
    norm_gain,
    saved_main,
    saved_state,
    saved_step,
    output_grad,
):
    sections = lax.axis_size("pipe")
    chunks = lax.axis_size("tensor")
    section = lax.axis_index("pipe")
    me = lax.axis_index("tensor")
    core = lax.axis_index("dp")
    length, width = output_grad.shape
    model_width = weight_out.shape[2]
    heads = step_bias.shape[1]
    channels = weight_out.shape[1]
    place = ("pipe", "tensor")

    def within(active, hop):
        return section_pairs(sections, chunks, active, active, hop)

    half = chunks // 2

    def rows_up(hop):
        pairs = []
        for source in range(sections - 1):
            for index in range(chunks):
                for lane in range(2):
                    move = hop + lane * half
                    if source == sections - 2:
                        if lane != hop:
                            continue
                        move = 0
                    start = (source * chunks + index) * 2 + lane
                    target = (source + 1) * chunks + (index + move) % chunks
                    pairs.append((start, target * 2 + lane))
        return pairs

    everywhere = ("pipe", "tensor", "dp")

    def swap(value, sections_in):
        pairs = []
        for source in sections_in:
            for start in range(source * chunks * 2, (source + 1) * chunks * 2):
                pairs.append((start, start ^ 1))
        return lax.ppermute(value, everywhere, pairs)

    far_first = sorted(range(1, chunks), key=lambda hop: -min(hop, chunks - hop))

    def exchange(values, sections_in):
        moved = [values[0]] * chunks
        for hop in far_first:
            pairs = []
            for source in sections_in:
                pairs += within(source, hop)
            moved[hop] = lax.ppermute(values[hop], place, pairs)
        return moved

    incoming = exchange([output_grad] * chunks, [sections - 1])

    rows = [lax.ppermute(weight_out[0], everywhere, rows_up(hop)) for hop in range(half)]
    lanes = ((0, 0), (0, 128 - heads))
    by_head = jnp.pad(
        jnp.stack([step_bias[0], decay_log[0], skip_gain[0]]), ((0, 5), (0, 128 - heads))
    )
    steps = jnp.pad(saved_step[0].astype(F32).T, lanes)
    taps_main = conv_main[0]
    taps_state = conv_state[0].reshape(conv_state.shape[1], -1)
    state_width = taps_state.shape[1]
    residual_shapes = (
        jax.ShapeDtypeStruct((9, length, channels), F32),
        jax.ShapeDtypeStruct((2, length, heads * length), F32),
        jax.ShapeDtypeStruct((length, heads * length), BF16),
        jax.ShapeDtypeStruct((heads * length, channels), BF16),
        jax.ShapeDtypeStruct((2, length, state_width // 2), BF16),
        jax.ShapeDtypeStruct((length, 128), F32),
    )
    residuals = pl.pallas_call(
        lambda *refs: forward_kernel(heads, *refs),
        out_shape=residual_shapes,
        in_specs=whole(8),
        out_specs=whole(6),
        compiler_params=kernel_params(),
        name="forward_residuals",
    )(
        saved_main[0, :, 0],
        saved_main[0, :, 1],
        saved_state[0].reshape(length, -1),
        steps,
        taps_main,
        taps_state,
        by_head,
        norm_gain,
    )
    residuals = tuple(residuals) + (taps_main, taps_state, by_head)
    slice_out = jax.ShapeDtypeStruct((length, channels), BF16)
    message = jax.ShapeDtypeStruct((length, width), BF16)
    map_width = 2 * channels + 128
    main_shape = jax.ShapeDtypeStruct((length, map_width), BF16)
    piece_shape = jax.ShapeDtypeStruct((length, 128), BF16)
    hbm = pl.BlockSpec(memory_space=pl.ANY)
    main_cols = weight_main[0].reshape(model_width, -1)
    step_rows = weight_step[0]
    residuals = residuals[:-1] + (after(by_head, main_cols),)

    main, *pieces = pl.pallas_call(
        lambda *refs: first_kernel(heads, chunks, *refs),
        out_shape=(main_shape,) + (piece_shape,) * chunks,
        in_specs=whole(chunks + 10),
        out_specs=whole(1 + chunks),
        compiler_params=kernel_params(),
        name="section_first",
    )(*incoming, weight_out[0], *residuals)

    def project_call(main, pieces, newest=(), others=()):
        return pl.pallas_call(
            lambda *refs: project_kernel(chunks, bool(others), *refs),
            out_shape=(message,) * chunks,
            in_specs=whole(3 + chunks + len(newest) + len(others)) + [hbm],
            out_specs=whole(chunks),
            scratch_shapes=[
                pltpu.VMEM((chunks, width, 2 * channels), BF16),
                pltpu.SemaphoreType.DMA((chunks,)),
            ],
            compiler_params=kernel_params(),
            name="project",
        )(main, *pieces, *newest, state_cols, *others, step_rows, main_cols)

    pieces = exchange(pieces, [sections - 1])
    state_cols = after(weight_state[0], main).reshape(model_width, -1).T
    state_share = state_cols.shape[0]
    parts = project_call(main, pieces)
    exchanged = exchange(parts, [sections - 1])

    grid_steps = 2
    depth = model_width // grid_steps
    rows_spec = pl.BlockSpec((channels, depth), lambda step: (0, step))
    def pass_back(messages, active):
        moved = []
        for hop in range(chunks):
            pairs = section_pairs(sections, chunks, active, active - 1, chunks - hop)
            moved.append(lax.ppermute(messages[hop], place, pairs))
        return moved

    result = pl.pallas_call(
        lambda *refs: carry_kernel(chunks, *refs),
        out_shape=message,
        in_specs=whole(chunks),
        out_specs=pl.BlockSpec(memory_space=SPACE),
        compiler_params=kernel_params(),
        name="carry_next",
    )(*exchanged)
    exchanged = exchange([result] * chunks, [sections - 1])
    dnormed = pl.pallas_call(
        lambda *refs: dnormed_kernel(chunks, *refs),
        out_shape=slice_out,
        in_specs=whole(chunks) + [hbm] * 2,
        out_specs=pl.BlockSpec(memory_space=SPACE),
        scratch_shapes=[
            pltpu.VMEM((channels, model_width), BF16),
            pltpu.SemaphoreType.DMA,
        ],
        compiler_params=kernel_params(),
        name="dnormed_back",
    )(*exchanged, *rows)
    pairs = section_pairs(sections, chunks, sections - 1, sections - 2, 0)
    incoming = [lax.ppermute(dnormed, place, pairs)]
    joint_shape = jax.ShapeDtypeStruct((channels + state_share, half * map_width), BF16)
    joint = pl.pallas_call(
        lambda *refs: compose_kernel(half, *refs),
        grid=(grid_steps,),
        out_shape=joint_shape,
        in_specs=[rows_spec] * half
        + [pl.BlockSpec((depth, 2 * channels), lambda step: (step, 0))]
        + [pl.BlockSpec((count, depth), lambda step: (0, step)) for count in (heads, state_share)],
        out_specs=pl.BlockSpec(joint_shape.shape, lambda step: (0, 0)),
        scratch_shapes=[
            pltpu.VMEM((half * channels, map_width), F32),
            pltpu.VMEM((half * channels, state_share), F32),
        ],
        compiler_params=kernel_params(),
        name="compose_weights",
    )(*rows[:-1], after(rows[-1], dnormed), main_cols, step_rows, state_cols)

    half_cols = lax.dynamic_slice_in_dim(
        after(state_cols, parts[0]), core * (model_width // 2), model_width // 2, 1
    )
    residuals = residuals[:-1] + (after(by_head, (joint, half_cols)),)

    state_shape = jax.ShapeDtypeStruct((length, state_width), BF16)
    joined = jax.ShapeDtypeStruct((length, channels + state_width + channels // 2), BF16)
    assert 2 * state_share == length

    def next_call(incoming, kept, active):
        count = chunks if len(incoming) > 1 else 0
        main, state, *pieces = pl.pallas_call(
            lambda *refs: next_kernel(heads, chunks, len(incoming), active, *refs),
            out_shape=(main_shape, state_shape) + (piece_shape,) * count,
            in_specs=whole(len(incoming) + 9 + len(kept)),
            out_specs=whole(2 + count),
            compiler_params=kernel_params(),
            name="section_next",
        )(*incoming, *residuals, *kept)
        return (main, state), pieces

    joint_other = None
    kept = ()
    summed = None
    for active in range(sections - 2, -1, -1):
        kept, pieces = next_call(incoming, kept, active)
        if active == 0:
            break
        if joint_other is None:
            joint_other = swap(after(joint, kept[0]), range(1, sections - 1))
        ahead = active == sections - 2
        if ahead:
            late = after(half_cols, kept[0])
            others = [
                lax.ppermute(late, place, within(0, chunks - away)) for away in range(1, chunks)
            ]
            stack = jax.ShapeDtypeStruct(((chunks - 1) * state_share, model_width // 2), BF16)
            state_map = jax.ShapeDtypeStruct((state_share, chunks * channels), BF16)
            outs = (joined,) * chunks + (stack, state_map)
        else:
            outs = (slice_out,) * chunks
        messages = pl.pallas_call(
            lambda *refs: send_kernel(chunks, ahead, *refs),
            out_shape=outs,
            in_specs=whole(2 + len(others)) + [hbm] * 2,
            out_specs=whole(len(outs)),
            scratch_shapes=[pltpu.VMEM(joint_shape.shape, BF16)] * 2
            + [pltpu.SemaphoreType.DMA((2,))],
            compiler_params=kernel_params(),
            name="send_ahead" if ahead else "send_back",
        )(*kept, *others, joint, joint_other)
        incoming = pass_back(messages, active)
        if ahead:
            stack, late = messages[chunks], after(messages[chunks + 1], incoming[0])
            others = exchange([late] * chunks, [1])[:0:-1]
        else:
            shared = (stack, swap(after(stack, messages[0]), [0]))
            summed = exchange(after(pieces, incoming[0]), range(1, sections - 1))

    parts = project_call(kept[0], summed, pieces, shared)
    exchanged = exchange(parts, range(sections - 1))
    total = exchanged[0].astype(F32)
    for part in exchanged[1:]:
        total = total + part.astype(F32)
    return jnp.where(section == sections - 1, result, total.astype(BF16))[None]


def solution(mesh):
    narrow = mesh.shape["tensor"] == GROUP_SPAN
    return jax.shard_map(
        relay_body if narrow else wide_body,
        mesh=mesh,
        in_specs=(
            P("pipe", None, None, "tensor"),
            P("pipe", None, None, "tensor"),
            P("pipe", "tensor", None),
            P("pipe", "tensor", None),
            P("pipe", None, "tensor"),
            P("pipe", None, None, None),
            P("pipe", "tensor"),
            P("pipe", "tensor"),
            P("pipe", "tensor"),
            P("pipe", "tensor"),
            P("pipe", "dp", None, "tensor"),
            P("pipe", "dp", None, None),
            P("pipe", "tensor", "dp"),
            P("dp", "tensor"),
        ),
        out_specs=P("pipe", "dp", "tensor"),
        check_vma=False,
    )
```
